32 devices in a mesh: section: 2 (over x), ctx: 8 (over z, y), fsdp: 2 (over core).
Axes of the slice: x: 2, y: 2, z: 4, core: 2. Of those that a mesh axis runs over, the one named last changes fastest.
Arguments:
- inputs: bfloat16 [2, 2, 1024, 640], P(None, 'fsdp', 'ctx'), may hold values from -6 to 6
- out_cotangent: bfloat16 [2, 2, 1024, 640], P(None, 'fsdp', 'ctx'), may hold values from -6 to 6
- block_order: int32 [16], replicated, may hold values from 0 to 15, as said below
- w_query: bfloat16 [2, 640, 1024], P('section', 'fsdp'), may hold values from -0.25 to 0.25
- w_key: bfloat16 [2, 640, 256], P('section', 'fsdp'), may hold values from -0.25 to 0.25
- w_value: bfloat16 [2, 640, 256], P('section', 'fsdp'), may hold values from -0.25 to 0.25
- w_output: bfloat16 [2, 1024, 640], P('section', 'fsdp'), may hold values from -0.1875 to 0.1875
- w_gate: bfloat16 [2, 640, 2048], P('section', 'fsdp'), may hold values from -0.25 to 0.25
- w_up: bfloat16 [2, 640, 2048], P('section', 'fsdp'), may hold values from -0.25 to 0.25
- w_down: bfloat16 [2, 2048, 640], P('section', 'fsdp'), may hold values from -0.125 to 0.125
- g_input: bfloat16 [2, 640], P('section', 'fsdp'), may hold values from 0.5 to 1.5
- g_query: bfloat16 [2, 256], P('section', 'fsdp'), may hold values from 0.5 to 1.5
- g_key: bfloat16 [2, 256], P('section', 'fsdp'), may hold values from 0.5 to 1.5
- g_post_attn: bfloat16 [2, 640], P('section', 'fsdp'), may hold values from 0.5 to 1.5
- g_pre_ffw: bfloat16 [2, 640], P('section', 'fsdp'), may hold values from 0.5 to 1.5
- g_post_ffw: bfloat16 [2, 640], P('section', 'fsdp'), may hold values from 0.5 to 1.5
Outputs:
- acts: bfloat16 [2, 2, 2, 1024, 640], P('section', None, 'fsdp', 'ctx')
- input_grads: bfloat16 [2, 2, 2, 1024, 640], P('section', None, 'fsdp', 'ctx')
- grad_w_query: float32 [2, 640, 1024], P('section', 'fsdp')
- grad_w_key: float32 [2, 640, 256], P('section', 'fsdp')
- grad_w_value: float32 [2, 640, 256], P('section', 'fsdp')
- grad_w_output: float32 [2, 1024, 640], P('section', 'fsdp')
- grad_w_gate: float32 [2, 640, 2048], P('section', 'fsdp')
- grad_w_up: float32 [2, 640, 2048], P('section', 'fsdp')
- grad_w_down: float32 [2, 2048, 640], P('section', 'fsdp')
- grad_g_input: float32 [2, 640], P('section', 'fsdp')
- grad_g_query: float32 [2, 256], P('section', 'fsdp')
- grad_g_key: float32 [2, 256], P('section', 'fsdp')
- grad_g_post_attn: float32 [2, 640], P('section', 'fsdp')
- grad_g_pre_ffw: float32 [2, 640], P('section', 'fsdp')
- grad_g_post_ffw: float32 [2, 640], P('section', 'fsdp')
The draws below stay inside these ranges and needn't reach their ends.
Inputs may be any that keep to these rules, and one draw needn't show every extreme that they name: block_order is a permutation of 0 to 15 whose entries 2i and 2i + 1 add up to 15.
All inputs are finite; a program needn't handle non-finite values.
Results may differ from the reference program's by a relative error of at most 0.038.
Values may be sent and summed in bfloat16 or wider, within the bound.
No kernel may reach another device: no remote copies, remote signals or barrier semaphores. Data moves between devices by JAX's collectives and lax.ppermute only.
A program may use at most 192 MiB of HBM per device.

```python
import math
import jax
import jax.numpy as jnp
from jax import lax

D = 640
HEADS = 4
HEAD_DIM = 256
FF = 2048
MICRO = 2
BLOCK = 64
BLOCKS = 16
SEQ_LEN = 1024
SEQS = 2


def draw_block_order(key, part):
    key = jax.random.fold_in(key, 7)
    order_key, swap_key = jax.random.split(key)
    pair_count = BLOCKS // 2
    lower_half = jax.random.permutation(order_key, pair_count).astype(jnp.int32)
    upper_half = BLOCKS - 1 - lower_half
    flipped = jax.random.randint(swap_key, (pair_count,), 0, 2, dtype=jnp.int32)
    earlier = jnp.where(flipped == 1, upper_half, lower_half)
    later_slot = jnp.where(flipped == 1, lower_half, upper_half)
    return jnp.stack([earlier, later_slot], axis=1).reshape(BLOCKS).astype(jnp.int32)


def shard_levels(own_key, extent, pieces, smallest, high):
    factor_of = 1.0
    for axis_at, shards_of in pieces:
        steps = jax.random.uniform(jax.random.fold_in(jax.random.fold_in(own_key, 6), axis_at), (shards_of,), jnp.float32, smallest / len(pieces), high / len(pieces))
        factor_of = factor_of * jnp.repeat(jnp.exp(steps), extent[axis_at] // shards_of).reshape((-1,) + (1,) * (len(extent) - 1 - axis_at))
    return factor_of


def normal_values(key, shape, width, limit, cuts=(), held_as=jnp.bfloat16):
    array = jax.random.normal(key, shape, jnp.float32) * width
    if len(cuts) > 0:
        array = shard_levels(key, shape, cuts, -0.22, 0.18) * array
    return jnp.clip(array, min=-limit, max=limit).astype(held_as)


def setup_inputs(seed: int = 0) -> dict:
    splits = jax.random.split(jax.random.key(seed), 17)
    inputs = normal_values(splits[0], (MICRO, SEQS, SEQ_LEN, D), 1.0, 6.0, ((1, 2), (2, 8)))
    out_cotangent = normal_values(splits[1], (MICRO, SEQS, SEQ_LEN, D), 1.0, 6.0, ((1, 2), (2, 8)))
    block_order = draw_block_order(jax.random.fold_in(splits[16], 71), 0)
    w_query = normal_values(splits[3], (2, D, HEADS * HEAD_DIM), D ** -0.5, 0.25, ((0, 2), (1, 2)))
    w_key = normal_values(splits[4], (2, D, HEAD_DIM), D ** -0.5, 0.25, ((0, 2), (1, 2)))
    w_value = normal_values(splits[5], (2, D, HEAD_DIM), D ** -0.5, 0.25, ((0, 2), (1, 2)))
    w_output = normal_values(splits[6], (2, HEADS * HEAD_DIM, D), (HEADS * HEAD_DIM) ** -0.5, 0.1875, ((0, 2), (1, 2)))
    w_gate = normal_values(splits[7], (2, D, FF), D ** -0.5, 0.25, ((0, 2), (1, 2)))
    w_up = normal_values(splits[8], (2, D, FF), D ** -0.5, 0.25, ((0, 2), (1, 2)))
    w_down = normal_values(splits[9], (2, FF, D), FF ** -0.5, 0.125, ((0, 2), (1, 2)))
    g_input = jnp.clip(1.0 + 0.1 * jax.random.normal(splits[10], (2, D), jnp.float32), 0.5, 1.5).astype(jnp.bfloat16)
    g_query = jnp.clip(1.0 + 0.1 * jax.random.normal(splits[11], (2, HEAD_DIM), jnp.float32), 0.5, 1.5).astype(jnp.bfloat16)
    g_key = jnp.clip(1.0 + 0.1 * jax.random.normal(splits[12], (2, HEAD_DIM), jnp.float32), 0.5, 1.5).astype(jnp.bfloat16)
    g_post_attn = jnp.clip(1.0 + 0.1 * jax.random.normal(splits[13], (2, D), jnp.float32), 0.5, 1.5).astype(jnp.bfloat16)
    g_pre_ffw = jnp.clip(1.0 + 0.1 * jax.random.normal(splits[14], (2, D), jnp.float32), 0.5, 1.5).astype(jnp.bfloat16)
    g_post_ffw = jnp.clip(1.0 + 0.1 * jax.random.normal(splits[15], (2, D), jnp.float32), 0.5, 1.5).astype(jnp.bfloat16)
    return dict(inputs=inputs, out_cotangent=out_cotangent, block_order=block_order, w_query=w_query, w_key=w_key, w_value=w_value, w_output=w_output, w_gate=w_gate, w_up=w_up, w_down=w_down, g_input=g_input, g_query=g_query, g_key=g_key, g_post_attn=g_post_attn, g_pre_ffw=g_pre_ffw, g_post_ffw=g_post_ffw)


epsilon = 1e-06
rope_base = 1000000.0
masked = -1e+30
score_scale = 0.0625

@jax.custom_vjp
def low(v):
    return lax.optimization_barrier(v.astype(jnp.bfloat16)).astype(jnp.float32)

@jax.custom_vjp
def low_back(v):
    return v

def low_keep(v):
    return (low(v), None)

def low_pass(kept, grad):
    return (grad,)

def back_keep(v):
    return (v, None)

def back_low(kept, grad):
    return (low(grad),)
low.defvjp(low_keep, low_pass)
low_back.defvjp(back_keep, back_low)

def product(left, right):
    return jnp.dot(left, right, precision=lax.Precision.HIGHEST, preferred_element_type=jnp.float32)

def norm_apply(values_in, gain_vec):
    factor = lax.rsqrt(lax.optimization_barrier(jnp.mean(values_in * values_in, axis=-1, keepdims=True)) + epsilon)
    return values_in * factor * gain_vec

def rotate(values_in, cos_table, sin_table):
    half_width = values_in.shape[-1] // 2
    former = values_in[..., :half_width]
    latter = values_in[..., half_width:]
    return jnp.concatenate([former * cos_table - latter * sin_table, latter * cos_table + former * sin_table], axis=-1)

def attend(query_block, query_pos, keys_all, values_all, key_pos):
    scores = low_back(jnp.einsum('hqd,kd->hqk', query_block, keys_all, precision=lax.Precision.HIGHEST) * score_scale)
    allowed = key_pos[None, None, :] <= query_pos[None, :, None]
    attn_probs = low(jax.nn.softmax(jnp.where(allowed, scores, masked), axis=-1))
    return jnp.einsum('hqk,kd->hqd', attn_probs, values_all, precision=lax.Precision.HIGHEST)

def layer_apply(params, positions, cos_table, sin_table, hidden):
    w_query, w_key, w_value, w_output, w_gate, w_up, w_down, g_input, g_query, g_key, g_post_attn, g_pre_ffw, g_post_ffw = params
    seq_len = hidden.shape[0]
    normed = low(norm_apply(hidden, g_input))
    queries = low_back(product(normed, w_query)).reshape(seq_len, HEADS, HEAD_DIM)
    keys_lin = low_back(product(normed, w_key))
    values_all = low(low_back(product(normed, w_value)))
    queries = low(rotate(norm_apply(queries, g_query), cos_table[:, None, :], sin_table[:, None, :]))
    keys_all = low(rotate(norm_apply(keys_lin, g_key), cos_table, sin_table))
    block_len = math.gcd(seq_len, 1024)
    query_blocks = jnp.transpose(queries.reshape(seq_len // block_len, block_len, HEADS, HEAD_DIM), (0, 2, 1, 3))
    pos_blocks = positions.reshape(seq_len // block_len, block_len)
    attend_block = jax.checkpoint(lambda pair_in: attend(pair_in[0], pair_in[1], keys_all, values_all, positions))
    attended = lax.map(attend_block, (query_blocks, pos_blocks))
    attn_out = low(low_back(jnp.transpose(attended, (0, 2, 1, 3)).reshape(seq_len, HEADS * HEAD_DIM)))
    branch = low_back(product(attn_out, w_output))
    middle = hidden + norm_apply(branch, g_post_attn)
    pre_ffw = low(norm_apply(middle, g_pre_ffw))
    gate_lin = low_back(product(pre_ffw, w_gate))
    up_lin = low_back(product(pre_ffw, w_up))
    hidden_ffw = low(jax.nn.gelu(gate_lin, approximate=True) * up_lin)
    down_out = low_back(product(hidden_ffw, w_down))
    return middle + norm_apply(down_out, g_post_ffw)

def section_apply(params, positions, cos_table, sin_table, hidden):
    layer_one = jax.checkpoint(lambda seq_in: layer_apply(params, positions, cos_table, sin_table, seq_in))
    return lax.map(layer_one, hidden)

def reference(inputs, out_cotangent, block_order, w_query, w_key, w_value, w_output, w_gate, w_up, w_down, g_input, g_query, g_key, g_post_attn, g_pre_ffw, g_post_ffw):
    seq_index = jnp.arange(SEQ_LEN, dtype=jnp.int32)
    positions = (jnp.take(block_order, seq_index // BLOCK) * BLOCK + seq_index % BLOCK).astype(jnp.int32)
    half_width = HEAD_DIM // 2
    frequency = rope_base ** (-jnp.arange(half_width, dtype=jnp.float32) / half_width)
    angles = positions.astype(jnp.float32)[:, None] * frequency[None, :]
    cos_table = jnp.cos(angles)
    sin_table = jnp.sin(angles)
    weights = tuple((weight_arg.astype(jnp.float32) for weight_arg in (w_query, w_key, w_value, w_output, w_gate, w_up, w_down, g_input, g_query, g_key, g_post_attn, g_pre_ffw, g_post_ffw)))
    first_params = tuple((weight_arg[0] for weight_arg in weights))
    second_params = tuple((weight_arg[1] for weight_arg in weights))
    seq_count = MICRO * SEQS
    hidden = inputs.astype(jnp.float32).reshape(seq_count, SEQ_LEN, D)

    def run_section(params, seq_in):
        return section_apply(params, positions, cos_table, sin_table, seq_in)
    first_out, first_back = jax.vjp(run_section, first_params, hidden)
    sent_acts = low(first_out)
    second_out, second_back = jax.vjp(run_section, second_params, sent_acts)
    second_grads, sent_grad = second_back(out_cotangent.astype(jnp.float32).reshape(seq_count, SEQ_LEN, D))
    returned = low(sent_grad)
    first_grads, input_grad = first_back(returned)
    out_shape = (2, MICRO, SEQS, SEQ_LEN, D)
    acts = jnp.stack([sent_acts, second_out]).astype(jnp.bfloat16).reshape(out_shape)
    input_grads = jnp.stack([input_grad, returned]).astype(jnp.bfloat16).reshape(out_shape)
    grads = [jnp.stack([first_grads[member], second_grads[member]]) for member in range(13)]
    return (acts, input_grads, grads[0], grads[1], grads[2], grads[3], grads[4], grads[5], grads[6], grads[7], grads[8], grads[9], grads[10], grads[11], grads[12])
```

```python
import jax
import jax.numpy as jnp
from jax import lax
from jax.sharding import PartitionSpec as P

epsilon = 1e-06
rope_base = 1000000.0
masked = -1e30
score_scale = 0.0625
f32 = jnp.float32
bf16 = jnp.bfloat16


def dot_f32(left, right):
    return jnp.dot(left, right, preferred_element_type=f32)


def dot_nt(left, right):
    return lax.dot_general(left, right, (((1,), (1,)), ((), ())), preferred_element_type=f32)


def dot_tn(left, right):
    return lax.dot_general(left, right, (((0,), (0,)), ((), ())), preferred_element_type=f32)


def norm_factor(values_in):
    return lax.rsqrt(jnp.mean(values_in * values_in, axis=-1, keepdims=True) + epsilon)


def norm_apply(values_in, gain_vec):
    return values_in * norm_factor(values_in) * gain_vec


def norm_back(values_in, gain_vec, grad_out):
    factor = norm_factor(values_in)
    scaled = grad_out * gain_vec
    grad_in = factor * (
        scaled - values_in * factor * factor * jnp.mean(scaled * values_in, axis=-1, keepdims=True)
    )
    grad_gain = jnp.sum((grad_out * values_in * factor).reshape(-1, values_in.shape[-1]), axis=0)
    return (grad_in, grad_gain)


def rotate(values_in, cos_table, sin_table):
    half_width = values_in.shape[-1] // 2
    former = values_in[..., :half_width]
    latter = values_in[..., half_width:]
    return jnp.concatenate(
        [former * cos_table - latter * sin_table, latter * cos_table + former * sin_table], axis=-1
    )


def unrotate(grad_in, cos_table, sin_table):
    return rotate(grad_in, cos_table, -sin_table)


def gelu_fn(values_in):
    return jax.nn.gelu(values_in, approximate=True)


def rotation_tables(positions, half_width):
    frequency = rope_base ** (-jnp.arange(half_width, dtype=f32) / half_width)
    angles = positions.astype(f32)[:, None] * frequency[None, :]
    return (jnp.cos(angles), jnp.sin(angles))


def xor_permute(shard, axis, mask):
    count = lax.axis_size(axis)
    return lax.ppermute(shard, axis, [(i, i ^ mask) for i in range(count)])


def small_ctx():
    return lax.axis_size("ctx") == 8


def ctx_order():
    count = lax.axis_size("ctx")
    slots = jnp.arange(count, dtype=jnp.int32)
    if small_ctx():
        return lax.axis_index("ctx") ^ slots
    return slots


def gather_ctx(shard):
    if not small_ctx():
        return lax.all_gather(shard, "ctx", axis=0)
    blocks = [None] * 8
    blocks[0] = shard
    for mask in (6, 4, 2):
        blocks[mask] = xor_permute(shard, "ctx", mask)
    for mask in (0, 2, 4, 6):
        blocks[mask + 1] = xor_permute(blocks[mask], "ctx", 1)
    return jnp.stack(blocks)


def scatter_ctx(parts):
    if not small_ctx():
        return lax.psum_scatter(parts.astype(f32), "ctx", scatter_dimension=0, tiled=False)
    sums = {}
    for mask in (6, 4, 2, 0):
        came = xor_permute(parts[mask + 1], "ctx", 1)
        sums[mask] = parts[mask].astype(f32) + came.astype(f32)
    total = sums[0]
    for mask in (6, 4, 2):
        low = lax.optimization_barrier(sums[mask].astype(bf16))
        total = total + xor_permute(low, "ctx", mask).astype(f32)
    return total


def sum_ctx(shard):
    if not small_ctx():
        return lax.psum(shard.astype(f32), "ctx")
    ctx_index = lax.axis_index("ctx")
    y_index = ctx_index & 1
    z_index = ctx_index >> 1
    half = shard.shape[0] // 2
    keep = lax.dynamic_slice_in_dim(shard, y_index * half, half, 0)
    send = lax.dynamic_slice_in_dim(shard, (1 - y_index) * half, half, 0)
    came = xor_permute(send, "ctx", 1)
    inward = [(z * 2 + y, t * 2 + y) for z, t in ((0, 1), (3, 2)) for y in (0, 1)]
    middle = [(z * 2 + y, t * 2 + y) for z, t in ((1, 2), (2, 1)) for y in (0, 1)]
    outward = [(z * 2 + y, t * 2 + y) for z, t in ((1, 0), (2, 3)) for y in (0, 1)]

    def add(left, right):
        return lax.optimization_barrier((left.astype(f32) + right.astype(f32)).astype(bf16))

    part = add(keep, came)
    part = add(part, lax.ppermute(part, "ctx", inward))
    part = add(part, lax.ppermute(part, "ctx", middle))
    back = lax.ppermute(part, "ctx", outward)
    total = jnp.where((z_index == 1) | (z_index == 2), part, back)
    other = xor_permute(total, "ctx", 1)
    first = jnp.where(y_index == 0, total, other)
    second = jnp.where(y_index == 0, other, total)
    return jnp.concatenate([first, second], axis=0).astype(f32)


def gather_fsdp(shard):
    other = xor_permute(shard, "fsdp", 1)
    is_first = lax.axis_index("fsdp") == 0
    return jnp.concatenate(
        [jnp.where(is_first, shard, other), jnp.where(is_first, other, shard)], axis=0
    )


def scatter_fsdp(terms):
    half = terms.shape[0] // 2
    fsdp_index = lax.axis_index("fsdp")
    keep = lax.dynamic_slice_in_dim(terms, fsdp_index * half, half, 0)
    send = lax.dynamic_slice_in_dim(terms, (1 - fsdp_index) * half, half, 0)
    came = xor_permute(send.astype(bf16), "fsdp", 1)
    return (keep.astype(f32) + came.astype(f32)).astype(bf16)


def on_device(
    inputs,
    out_cotangent,
    block_order,
    w_query,
    w_key,
    w_value,
    w_output,
    w_gate,
    w_up,
    w_down,
    g_input,
    g_query,
    g_key,
    g_post_attn,
    g_pre_ffw,
    g_post_ffw,
):
    section_index = lax.axis_index("section")
    ctx_index = lax.axis_index("ctx")
    micro_count, seq_local, tokens, model_width = inputs.shape
    groups = micro_count * seq_local
    rows = groups * tokens
    block_len = tokens // 2
    gains_own = jnp.concatenate(
        [g_input[0], g_post_attn[0], g_pre_ffw[0], g_post_ffw[0], g_query[0], g_key[0]]
    )
    w_kv_own = jnp.concatenate([w_key[0], w_value[0]], axis=1)
    gains_other = xor_permute(gains_own.reshape(1, -1), "fsdp", 1)
    gains_pair = jnp.stack([gains_own, gains_other[0]])
    gains_pair = jnp.where(lax.axis_index("fsdp") == 0, gains_pair, gains_pair[::-1])
    w_kv = gather_fsdp(w_kv_own)
    w_q = gather_fsdp(w_query[0])
    w_out = gather_fsdp(w_output[0])
    w_ffw_in = gather_fsdp(jnp.concatenate([w_gate[0], w_up[0]], axis=1))
    w_dn = gather_fsdp(w_down[0])
    half_model = model_width // 2
    gains = gains_pair.astype(f32)
    gain_input = gains[:, :half_model].reshape(-1)
    gain_attn = gains[:, half_model : 2 * half_model].reshape(-1)
    gain_pre = gains[:, 2 * half_model : 3 * half_model].reshape(-1)
    gain_post = gains[:, 3 * half_model : 4 * half_model].reshape(-1)
    half_head = g_query.shape[1]
    gain_query = gains[:, 4 * half_model : 4 * half_model + half_head].reshape(-1)
    gain_key = gains[:, 4 * half_model + half_head :].reshape(-1)
    head_dim = 2 * half_head
    query_cols = w_out.shape[0]
    head_count = query_cols // head_dim
    ff_width = w_dn.shape[0]
    ctx_size = lax.axis_size("ctx")
    order = ctx_order()
    slot_pairs = block_order.reshape(ctx_size, 2)
    offsets = jnp.arange(block_len, dtype=jnp.int32)

    def spread(slot_ids):
        return (slot_ids.reshape(-1)[:, None] * block_len + offsets[None, :]).reshape(-1)

    local_pos = spread(slot_pairs[ctx_index])
    key_pos = spread(slot_pairs[order])
    cos_table, sin_table = rotation_tables(local_pos, head_dim // 2)
    query_pos = jnp.tile(local_pos, head_count)
    allowed = key_pos[None, None, :] <= query_pos[None, :, None]

    def to_heads(flat):
        split = flat.reshape(groups, tokens, head_count, head_dim)
        return jnp.transpose(split, (0, 2, 1, 3)).reshape(groups, head_count * tokens, head_dim)

    def from_heads(stacked):
        split = stacked.reshape(groups, head_count, tokens, head_dim)
        return jnp.transpose(split, (0, 2, 1, 3)).reshape(rows, query_cols)

    def forward(hidden):
        normed = norm_apply(hidden, gain_input).astype(bf16)
        kv_lin = dot_f32(normed, w_kv)
        key_lin = kv_lin[:, :head_dim]
        key_rot = rotate(
            norm_apply(key_lin, gain_key).reshape(groups, tokens, head_dim), cos_table, sin_table
        ).reshape(rows, head_dim)
        kv_low = jnp.concatenate([key_rot, kv_lin[:, head_dim:]], axis=1).astype(bf16)
        kv_all = gather_ctx(kv_low.reshape(groups, tokens, 2 * head_dim))
        kv_all = jnp.transpose(kv_all, (1, 0, 2, 3)).reshape(
            groups, ctx_size * tokens, 2 * head_dim
        )
        query_lin = dot_f32(normed, w_q).reshape(groups, tokens, head_count, head_dim)
        query_rot = rotate(
            norm_apply(query_lin, gain_query), cos_table[:, None, :], sin_table[:, None, :]
        ).astype(bf16)
        query_rows = to_heads(query_rot)
        keys = kv_all[:, :, :head_dim]
        values = kv_all[:, :, head_dim:]
        scores = (
            jnp.einsum("sqd,skd->sqk", query_rows, keys, preferred_element_type=f32) * score_scale
        )
        scores = jnp.where(allowed, scores, masked)
        row_max = jnp.max(scores, axis=-1, keepdims=True)
        weights = jnp.exp(scores - row_max)
        row_total = jnp.sum(weights, axis=-1, keepdims=True)
        attn_rows = (
            jnp.einsum("sqk,skd->sqd", weights.astype(bf16), values, preferred_element_type=f32)
            / row_total
        )
        log_total = row_max + jnp.log(row_total)
        attn_low = from_heads(attn_rows).astype(bf16)
        branch = dot_f32(attn_low, w_out)
        middle = hidden + norm_apply(branch, gain_attn)
        pre_ffw = norm_apply(middle, gain_pre).astype(bf16)
        gate_up = dot_f32(pre_ffw, w_ffw_in)
        hidden_ffw = (gelu_fn(gate_up[:, :ff_width]) * gate_up[:, ff_width:]).astype(bf16)
        down_out = dot_f32(hidden_ffw, w_dn)
        result = (middle + norm_apply(down_out, gain_post)).astype(bf16)
        saved = (
            hidden,
            normed,
            query_lin,
            key_lin,
            query_rows,
            kv_all,
            attn_rows,
            log_total,
            attn_low,
            branch,
            middle,
            pre_ffw,
            gate_up,
            hidden_ffw,
            down_out,
        )
        return (result, saved)

    def backward(grad_flat, saved):
        (
            hidden,
            normed,
            query_lin,
            key_lin,
            query_rows,
            kv_all,
            attn_rows,
            log_total,
            attn_low,
            branch,
            middle,
            pre_ffw,
            gate_up,
            hidden_ffw,
            down_out,
        ) = saved
        down_part, grad_gain_post = norm_back(down_out, gain_post, grad_flat)
        down_grad = down_part.astype(bf16)
        ffw_grad = dot_nt(down_grad, w_dn)
        activated, gelu_back = jax.vjp(gelu_fn, gate_up[:, :ff_width])
        gate_grad = gelu_back(ffw_grad * gate_up[:, ff_width:])[0]
        gate_up_grad = jnp.concatenate([gate_grad, ffw_grad * activated], axis=1).astype(bf16)
        pre_grad = dot_nt(gate_up_grad, w_ffw_in)
        middle_part, grad_gain_pre = norm_back(middle, gain_pre, pre_grad)
        middle_grad = grad_flat + middle_part
        branch_part, grad_gain_attn = norm_back(branch, gain_attn, middle_grad)
        branch_grad = branch_part.astype(bf16)
        attn_grad = dot_nt(branch_grad, w_out).astype(bf16)
        grad_rows = to_heads(attn_grad)
        row_delta = jnp.sum(grad_rows.astype(f32) * attn_rows, axis=-1, keepdims=True)
        key_rows = kv_all.shape[1]
        span = tokens * min(8, ctx_size)

        def span_grads(start, query_grad):
            kv_part = lax.dynamic_slice_in_dim(kv_all, start, span, 1)
            keys = kv_part[:, :, :head_dim]
            values = kv_part[:, :, head_dim:]
            seen = lax.dynamic_slice_in_dim(key_pos, start, span, 0)[None, None, :]
            scores = (
                jnp.einsum("sqd,skd->sqk", query_rows, keys, preferred_element_type=f32)
                * score_scale
            )
            probs = jnp.exp(
                jnp.where(seen <= query_pos[None, :, None], scores - log_total, masked)
            )
            prob_grad = jnp.einsum(
                "sqd,skd->sqk", grad_rows, values, preferred_element_type=f32
            )
            score_grad = (probs * (prob_grad - row_delta)).astype(bf16)
            query_part = (
                jnp.einsum("sqk,skd->sqd", score_grad, keys, preferred_element_type=f32)
                * score_scale
            )
            key_part = (
                jnp.einsum("sqk,sqd->skd", score_grad, query_rows, preferred_element_type=f32)
                * score_scale
            )
            value_part = jnp.einsum(
                "sqk,sqd->skd", probs.astype(bf16), grad_rows, preferred_element_type=f32
            )
            both = jnp.concatenate([key_part, value_part], axis=2).astype(bf16)
            return (query_grad + query_part, both)

        query_zero = jnp.zeros(query_rows.shape, f32)
        if key_rows == span:
            query_grad, kv_parts = span_grads(0, query_zero)
        else:

            def one_span(index, state):
                query_sum, all_parts = state
                query_sum, both = span_grads(index * span, query_sum)
                return (
                    query_sum,
                    lax.dynamic_update_slice_in_dim(all_parts, both, index * span, 1),
                )

            query_grad, kv_parts = lax.fori_loop(
                0, key_rows // span, one_span, (query_zero, jnp.zeros(kv_all.shape, bf16))
            )
        kv_parts = jnp.transpose(
            kv_parts.reshape(groups, ctx_size, tokens, 2 * head_dim), (1, 0, 2, 3)
        )
        kv_grad = scatter_ctx(kv_parts).reshape(rows, 2 * head_dim)
        query_tok_grad = from_heads(query_grad).reshape(groups, tokens, head_count, head_dim)
        query_lin_grad, grad_gain_query = norm_back(
            query_lin,
            gain_query,
            unrotate(query_tok_grad, cos_table[:, None, :], sin_table[:, None, :]),
        )
        key_lin_grad, grad_gain_key = norm_back(
            key_lin,
            gain_key,
            unrotate(
                kv_grad[:, :head_dim].reshape(groups, tokens, head_dim), cos_table, sin_table
            ).reshape(rows, head_dim),
        )
        query_low = query_lin_grad.reshape(rows, query_cols).astype(bf16)
        kv_grad_low = jnp.concatenate([key_lin_grad, kv_grad[:, head_dim:]], axis=1).astype(bf16)
        normed_grad = dot_nt(query_low, w_q) + dot_nt(kv_grad_low, w_kv)
        input_part, grad_gain_input = norm_back(hidden, gain_input, normed_grad)
        input_grad = (middle_grad + input_part).astype(bf16)

        def weight_grads():
            return (
                dot_tn(hidden_ffw, down_grad),
                dot_tn(pre_ffw, gate_up_grad),
                dot_tn(attn_low, branch_grad),
                dot_tn(normed, jnp.concatenate([query_low, kv_grad_low], axis=1)),
                (
                    grad_gain_input,
                    grad_gain_attn,
                    grad_gain_pre,
                    grad_gain_post,
                    grad_gain_query,
                    grad_gain_key,
                ),
            )

        return (input_grad, weight_grads)

    own_input = inputs.reshape(rows, model_width)
    first_result, _ = forward(own_input.astype(f32))
    received = lax.ppermute(first_result, "section", [(0, 1)])
    hidden = jnp.where(section_index == 0, own_input, received)
    result, saved = forward(hidden.astype(f32))
    own_grad = out_cotangent.reshape(rows, model_width)
    first_grad, _ = backward(own_grad.astype(f32), saved)
    grad_received = lax.ppermute(first_grad, "section", [(1, 0)])
    grad_in = jnp.where(section_index == 1, own_grad, grad_received)
    input_grad, weight_grads = backward(grad_in.astype(f32), saved)
    grad_down, grad_ffw, grad_out, grad_qkv, grad_gains = weight_grads()
    sum_down = sum_ctx(scatter_fsdp(grad_down))
    sum_gate = sum_ctx(scatter_fsdp(grad_ffw[:, :ff_width]))
    sum_up = sum_ctx(scatter_fsdp(grad_ffw[:, ff_width:]))
    sum_out = sum_ctx(scatter_fsdp(grad_out))
    gain_rows = jnp.concatenate([member.reshape(2, -1) for member in grad_gains], axis=1)
    width = gain_rows.shape[1]
    pad = jnp.zeros((2, 31, width), f32)
    gain_rows = jnp.concatenate([gain_rows[:, None, :], pad], axis=1)
    tail = jnp.concatenate(
        [grad_qkv[:half_model], gain_rows[0], grad_qkv[half_model:], gain_rows[1]], axis=0
    )
    sum_tail = sum_ctx(scatter_fsdp(tail))
    sum_query = sum_tail[:half_model, :query_cols]
    sum_key = sum_tail[:half_model, query_cols : query_cols + head_dim]
    sum_value = sum_tail[:half_model, query_cols + head_dim :]
    sum_gains = sum_tail[half_model]
    cuts = [0]
    for member in grad_gains:
        cuts.append(cuts[-1] + member.shape[0] // 2)
    gain_parts = [sum_gains[cuts[i] : cuts[i + 1]] for i in range(6)]
    shape = (micro_count, seq_local, tokens, model_width)
    members = (
        sum_query,
        sum_key,
        sum_value,
        sum_out,
        sum_gate,
        sum_up,
        sum_down,
        gain_parts[0],
        gain_parts[4],
        gain_parts[5],
        gain_parts[1],
        gain_parts[2],
        gain_parts[3],
    )
    return (result.reshape(shape)[None], input_grad.reshape(shape)[None]) + tuple(
        member[None] for member in members
    )


def solution(mesh):
    weight = P("section", "fsdp", None)
    gain = P("section", "fsdp")
    in_specs = (
        (P(None, "fsdp", "ctx", None),) * 2 + (P(),) + (weight,) * 7 + (gain,) * 6
    )
    out_specs = (
        (P("section", None, "fsdp", "ctx", None),) * 2 + (weight,) * 7 + (gain,) * 6
    )
    return jax.shard_map(
        on_device, mesh=mesh, in_specs=in_specs, out_specs=out_specs, check_vma=False
    )
```

```python
import functools

import jax
import jax.numpy as jnp
from jax import lax
from jax.experimental import pallas as pl
from jax.experimental.pallas import tpu as pltpu
from jax.sharding import PartitionSpec as P

epsilon = 1e-06
rope_base = 1000000.0
masked = -1e30
score_scale = 0.0625
gelu_slope = 0.7978845608028654
gelu_cubic = 0.044715
f32 = jnp.float32
bf16 = jnp.bfloat16
vmem_bytes = 56 * 1024 * 1024


def dot_nn(left, right):
    return jnp.dot(left, right, preferred_element_type=f32)


def dot_nt(left, right):
    return lax.dot_general(left, right, (((1,), (1,)), ((), ())), preferred_element_type=f32)


def dot_tn(left, right):
    return lax.dot_general(left, right, (((0,), (0,)), ((), ())), preferred_element_type=f32)


def norm_factor(values_in):
    return lax.rsqrt(jnp.mean(values_in * values_in, axis=-1, keepdims=True) + epsilon)


def norm_apply(values_in, gain_vec):
    return values_in * norm_factor(values_in) * gain_vec


def norm_back(values_in, gain_vec, grad_out):
    factor = norm_factor(values_in)
    scaled = grad_out * gain_vec
    grad_in = factor * (
        scaled - values_in * factor * factor * jnp.mean(scaled * values_in, axis=-1, keepdims=True)
    )
    grad_gain = jnp.sum(grad_out * values_in * factor, axis=0, keepdims=True)
    return (grad_in, grad_gain)


def rotate(values_in, cos_table, sin_table):
    half_width = values_in.shape[-1] // 2
    former = values_in[..., :half_width]
    latter = values_in[..., half_width:]
    return jnp.concatenate(
        [former * cos_table - latter * sin_table, latter * cos_table + former * sin_table], axis=-1
    )


def rotation_tables(positions, half_width):
    frequency = rope_base ** (-jnp.arange(half_width, dtype=f32) / half_width)
    angles = positions.astype(f32)[:, None] * frequency[None, :]
    return (jnp.cos(angles), jnp.sin(angles))


def call_kernel(body, out_shapes, inputs, far_inputs, scratch):
    whole = pl.BlockSpec(memory_space=pltpu.VMEM)
    far = pl.BlockSpec(memory_space=pl.ANY)
    return pl.pallas_call(
        body,
        out_shape=out_shapes,
        in_specs=[whole] * len(inputs) + [far] * len(far_inputs),
        out_specs=jax.tree.map(lambda _: whole, out_shapes),
        scratch_shapes=scratch,
        compiler_params=pltpu.CompilerParams(vmem_limit_bytes=vmem_bytes),
    )(*inputs, *far_inputs)


def struct(shape, dtype):
    return jax.ShapeDtypeStruct(shape, dtype)


def start_halves(own, other, target, sems, first_sem):
    half = own.shape[0]
    fsdp_index = lax.axis_index("fsdp")
    copies = [
        pltpu.make_async_copy(
            own, target.at[pl.ds(fsdp_index * half, half)], sems.at[first_sem]
        ),
        pltpu.make_async_copy(
            other, target.at[pl.ds((1 - fsdp_index) * half, half)], sems.at[first_sem + 1]
        ),
    ]
    for copy in copies:
        copy.start()
    return copies


def wait_all(copies):
    for copy in copies:
        copy.wait()


def whole_gain(own_ref, other_ref, start, width):
    own = own_ref[:, start : start + width].astype(f32)
    other = other_ref[:, start : start + width].astype(f32)
    is_first = lax.axis_index("fsdp") == 0
    return jnp.concatenate(
        [jnp.where(is_first, own, other), jnp.where(is_first, other, own)], axis=1
    )


class Sizes:
    def __init__(self, groups, tokens, model, heads, head_dim, ff, blocks):
        self.groups, self.tokens, self.model = groups, tokens, model
        self.heads, self.head_dim, self.ff, self.blocks = heads, head_dim, ff, blocks
        self.rows = groups * tokens
        self.query_cols = heads * head_dim
        self.head_rows = heads * tokens
        self.keys = blocks * tokens
        self.span = tokens * min(8, blocks)
        self.chunk = min(256, self.head_rows)
        half = model // 2
        self.gain_at = {
            "input": (0, half),
            "attn": (half, half),
            "pre": (2 * half, half),
            "post": (3 * half, half),
            "query": (4 * half, head_dim // 2),
            "key": (4 * half + head_dim // 2, head_dim // 2),
        }


def kv_kernel(
    sz, hidden, gain_own, gain_other, cos_ref, sin_ref, k_own, k_other, v_own, v_other,
    normed, key_lin, kv_low, wk, wv, sems,
):
    k_copies = start_halves(k_own, k_other, wk, sems, 0)
    v_copies = start_halves(v_own, v_other, wv, sems, 2)
    gain_input = whole_gain(gain_own, gain_other, *sz.gain_at["input"])
    gain_key = whole_gain(gain_own, gain_other, *sz.gain_at["key"])
    low = norm_apply(hidden[...].astype(f32), gain_input).astype(bf16)
    normed[...] = low
    wait_all(k_copies)
    lin = dot_nn(low, wk[...])
    key_lin[...] = lin
    cos = jnp.concatenate([cos_ref[...]] * sz.groups, axis=0)
    sin = jnp.concatenate([sin_ref[...]] * sz.groups, axis=0)
    kv_low[:, : sz.head_dim] = rotate(norm_apply(lin, gain_key), cos, sin).astype(bf16)
    wait_all(v_copies)
    kv_low[:, sz.head_dim :] = dot_nn(low, wv[...]).astype(bf16)


def project_kv(sz, hidden, gains, tables, w_key, w_value):
    half = (sz.model, sz.head_dim)
    return call_kernel(
        functools.partial(kv_kernel, sz),
        [
            struct((sz.rows, sz.model), bf16),
            struct((sz.rows, sz.head_dim), f32),
            struct((sz.rows, 2 * sz.head_dim), bf16),
        ],
        [hidden, *gains, *tables],
        [*w_key, *w_value],
        [pltpu.VMEM(half, bf16), pltpu.VMEM(half, bf16), pltpu.SemaphoreType.DMA((4,))],
    )


def query_kernel(
    sz, normed, gain_own, gain_other, cos_ref, sin_ref, q_own, q_other,
    query_lin, query_low, wq, sems,
):
    copies = start_halves(q_own, q_other, wq, sems, 0)
    gain_query = whole_gain(gain_own, gain_other, *sz.gain_at["query"])
    cos = jnp.concatenate([cos_ref[...]] * sz.groups, axis=0)
    sin = jnp.concatenate([sin_ref[...]] * sz.groups, axis=0)
    low = normed[...]
    wait_all(copies)
    for head in range(sz.heads):
        cols = slice(head * sz.head_dim, (head + 1) * sz.head_dim)
        lin = dot_nn(low, wq[:, cols])
        query_lin[:, cols] = lin
        turned = rotate(norm_apply(lin, gain_query), cos, sin)
        turned = (turned.astype(bf16).astype(f32) * score_scale).astype(bf16)
        for group in range(sz.groups):
            query_low[group, head * sz.tokens : (head + 1) * sz.tokens, :] = turned[
                group * sz.tokens : (group + 1) * sz.tokens
            ]


def project_query(sz, normed, gains, tables, w_query):
    return call_kernel(
        functools.partial(query_kernel, sz),
        [
            struct((sz.rows, sz.query_cols), f32),
            struct((sz.groups, sz.head_rows, sz.head_dim), bf16),
        ],
        [normed, *gains, *tables],
        [*w_query],
        [pltpu.VMEM((sz.model, sz.query_cols), bf16), pltpu.SemaphoreType.DMA((2,))],
    )


def start_blocks(sz, blocks, target, sems, first_sem):
    copies = []
    for index, block in enumerate(blocks):
        copies.append(
            pltpu.make_async_copy(
                block,
                target.at[:, pl.ds(index * sz.tokens, sz.tokens)],
                sems.at[first_sem + index],
            )
        )
    for copy in copies:
        copy.start()
    return copies


def load_group(sz, stacked, group, target, sems, first_sem):
    def one(index):
        return pltpu.make_async_copy(
            stacked.at[index, group],
            target.at[0, pl.ds(index * sz.tokens, sz.tokens)],
            sems.at[first_sem + index],
        )

    def start(index, carry):
        one(index).start()
        return carry

    def wait(index, carry):
        one(index).wait()
        return carry

    lax.fori_loop(0, sz.blocks, start, 0)
    lax.fori_loop(0, sz.blocks, wait, 0)


def forward_kernel(sz, block_count, save, *refs):
    query_low, hidden, gain_own, gain_other, key_row, query_col = refs[:6]
    refs = refs[6:]
    blocks, refs = refs[:block_count], refs[block_count:]
    out_pair, gate_pair, up_pair, down_pair = (refs[2 * i : 2 * i + 2] for i in range(4))
    refs = refs[8:]
    result, refs = refs[0], refs[1:]
    if save:
        log_total, attn_low, branch_ref, middle_ref, pre_ref, gate_ref, up_ref, act_ref, down_ref = (
            refs[:9]
        )
        refs = refs[9:]
    else:
        attn_low, act_ref = refs[:2]
        refs = refs[2:]
    kv, w_out, w_gate, w_up, w_down, sems = refs
    if block_count > 1:
        kv_copies = start_blocks(sz, blocks, kv, sems, 8)
    out_copies = start_halves(*out_pair, w_out, sems, 0)
    gate_copies = start_halves(*gate_pair, w_gate, sems, 2)
    up_copies = start_halves(*up_pair, w_up, sems, 4)
    down_copies = start_halves(*down_pair, w_down, sems, 6)
    gain_attn = whole_gain(gain_own, gain_other, *sz.gain_at["attn"])
    gain_pre = whole_gain(gain_own, gain_other, *sz.gain_at["pre"])
    gain_post = whole_gain(gain_own, gain_other, *sz.gain_at["post"])
    if block_count > 1:
        wait_all(kv_copies)
    spans = sz.keys // sz.span
    for group in range(sz.groups):
        slot = group if block_count > 1 else 0
        if block_count == 1:
            load_group(sz, blocks[0], group, kv, sems, 8)
        for first in range(0, sz.head_rows, sz.chunk):
            query = query_low[group, first : first + sz.chunk, :]
            query_pos = query_col[first : first + sz.chunk, :]

            def one_span(index, state):
                row_max, row_total, row_sum = state
                at = pl.ds(index * sz.span, sz.span)
                scores = dot_nt(query, kv[slot, at, : sz.head_dim])
                scores = jnp.where(key_row[:, at] <= query_pos, scores, masked)
                new_max = jnp.maximum(row_max, jnp.max(scores, axis=1, keepdims=True))
                probs = jnp.exp(scores - new_max)
                part = dot_nn(probs.astype(bf16), kv[slot, at, sz.head_dim :])
                shrink = jnp.exp(row_max - new_max)
                return (
                    new_max,
                    row_total * shrink + jnp.sum(probs, axis=1, keepdims=True),
                    row_sum * shrink + part,
                )

            state = (
                jnp.full((sz.chunk, 1), masked, f32),
                jnp.zeros((sz.chunk, 1), f32),
                jnp.zeros((sz.chunk, sz.head_dim), f32),
            )
            if spans == 1:
                state = one_span(0, state)
            else:
                state = lax.fori_loop(0, spans, one_span, state)
            row_max, row_total, row_sum = state
            attended = (row_sum / row_total).astype(bf16)
            if save:
                log_total[group, first : first + sz.chunk, :] = row_max + jnp.log(row_total)
            for part in range(sz.chunk // sz.tokens):
                head = first // sz.tokens + part
                attn_low[
                    group * sz.tokens : (group + 1) * sz.tokens,
                    head * sz.head_dim : (head + 1) * sz.head_dim,
                ] = attended[part * sz.tokens : (part + 1) * sz.tokens]
    wait_all(out_copies)
    branch = dot_nn(attn_low[...], w_out[...])
    middle = hidden[...].astype(f32) + norm_apply(branch, gain_attn)
    pre_ffw = norm_apply(middle, gain_pre).astype(bf16)
    if save:
        branch_ref[...] = branch
        middle_ref[...] = middle
        pre_ref[...] = pre_ffw
    wait_all(gate_copies)
    wait_all(up_copies)
    step = min(512, sz.ff)
    for first in range(0, sz.ff, step):
        cols = slice(first, first + step)
        gate = dot_nn(pre_ffw, w_gate[:, cols])
        up = dot_nn(pre_ffw, w_up[:, cols])
        if save:
            gate_ref[:, cols] = gate
            up_ref[:, cols] = up
        bend = jnp.tanh(gelu_slope * (gate + gelu_cubic * gate * gate * gate))
        act_ref[:, cols] = (0.5 * gate * (1.0 + bend) * up).astype(bf16)
    wait_all(down_copies)
    down_out = dot_nn(act_ref[...], w_down[...])
    if save:
        down_ref[...] = down_out
    result[...] = (middle + norm_apply(down_out, gain_post)).astype(bf16)


def forward_layer(sz, query_low, hidden, gains, places, blocks, weights, save):
    rows, model = sz.rows, sz.model
    outs = [struct((rows, model), bf16)]
    attn = (rows, sz.query_cols)
    act = (rows, sz.ff)
    scratch = []
    if save:
        outs += [
            struct((sz.groups, sz.head_rows, 1), f32),
            struct(attn, bf16),
            struct((rows, model), f32),
            struct((rows, model), f32),
            struct((rows, model), bf16),
            struct(act, f32),
            struct(act, f32),
            struct(act, bf16),
            struct((rows, model), f32),
        ]
    else:
        scratch += [pltpu.VMEM(attn, bf16), pltpu.VMEM(act, bf16)]
    scratch += [
        pltpu.VMEM((sz.groups if len(blocks) > 1 else 1, sz.keys, 2 * sz.head_dim), bf16),
        pltpu.VMEM((sz.query_cols, model), bf16),
        pltpu.VMEM((model, sz.ff), bf16),
        pltpu.VMEM((model, sz.ff), bf16),
        pltpu.VMEM((sz.ff, model), bf16),
        pltpu.SemaphoreType.DMA((8 + sz.blocks,)),
    ]
    far = [*blocks, *weights["out"], *weights["gate"], *weights["up"], *weights["down"]]
    return call_kernel(
        functools.partial(forward_kernel, sz, len(blocks), save),
        outs,
        [query_low, hidden, *gains, places["key_row"], places["query_col"]],
        far,
        scratch,
    )


def backward_kernel(sz, block_count, *refs):
    (
        grad_ref, gain_own, gain_other, down_out, gate_ref, up_ref, middle, branch,
        query_low, log_row, key_col, query_row,
    ) = refs[:12]
    refs = refs[12:]
    blocks, refs = refs[:block_count], refs[block_count:]
    out_pair, gate_pair, up_pair, down_pair = (refs[2 * i : 2 * i + 2] for i in range(4))
    refs = refs[8:]
    (
        middle_grad, down_grad, gate_grad, up_grad, branch_grad, gain_post_grad, gain_pre_grad,
        gain_attn_grad, query_grad,
    ) = refs[:9]
    refs = refs[9:]
    parts, refs = refs[:block_count], refs[block_count:]
    kv, w_out, w_gate, w_up, w_down, key_sum, value_sum, sems = refs
    down_copies = start_halves(*down_pair, w_down, sems, 0)
    gate_copies = start_halves(*gate_pair, w_gate, sems, 2)
    up_copies = start_halves(*up_pair, w_up, sems, 4)
    out_copies = start_halves(*out_pair, w_out, sems, 6)
    if block_count > 1:
        kv_copies = start_blocks(sz, blocks, kv, sems, 8)
    gain_attn = whole_gain(gain_own, gain_other, *sz.gain_at["attn"])
    gain_pre = whole_gain(gain_own, gain_other, *sz.gain_at["pre"])
    gain_post = whole_gain(gain_own, gain_other, *sz.gain_at["post"])
    grad = grad_ref[...].astype(f32)
    down_part, gain_post_grad[...] = norm_back(down_out[...], gain_post, grad)
    down_low = down_part.astype(bf16)
    down_grad[...] = down_low
    wait_all(down_copies)
    wait_all(gate_copies)
    wait_all(up_copies)
    step = min(512, sz.ff)
    pre_grad = jnp.zeros((sz.rows, sz.model), f32)
    for first in range(0, sz.ff, step):
        cols = slice(first, first + step)
        ffw_grad = dot_nt(down_low, w_down[cols, :])
        gate = gate_ref[:, cols]
        up = up_ref[:, cols]
        square = gate * gate
        bend = jnp.tanh(gelu_slope * (gate + gelu_cubic * square * gate))
        half_open = 0.5 * (1.0 + bend)
        slope = half_open + 0.5 * gate * (1.0 - bend * bend) * gelu_slope * (
            1.0 + 3.0 * gelu_cubic * square
        )
        gate_low = (ffw_grad * up * slope).astype(bf16)
        up_low = (ffw_grad * gate * half_open).astype(bf16)
        gate_grad[:, cols] = gate_low
        up_grad[:, cols] = up_low
        pre_grad = pre_grad + dot_nt(gate_low, w_gate[:, cols]) + dot_nt(up_low, w_up[:, cols])
    middle_part, gain_pre_grad[...] = norm_back(middle[...], gain_pre, pre_grad)
    total = grad + middle_part
    middle_grad[...] = total
    branch_part, gain_attn_grad[...] = norm_back(branch[...], gain_attn, total)
    branch_low = branch_part.astype(bf16)
    branch_grad[...] = branch_low
    wait_all(out_copies)
    attn_grad = dot_nt(branch_low, w_out[...]).astype(bf16)
    if block_count > 1:
        wait_all(kv_copies)
    spans = sz.keys // sz.span
    heads_in = sz.chunk // sz.tokens
    chunks = range(0, sz.head_rows, sz.chunk)

    def probs_of(slot, group, first, at):
        query = query_low[group, first : first + sz.chunk, :]
        query_pos = query_row[:, first : first + sz.chunk]
        log_here = log_row[group, :, first : first + sz.chunk]
        scores = dot_nt(kv[slot, at, : sz.head_dim], query)
        probs = jnp.exp(jnp.where(key_col[at, :] <= query_pos, scores - log_here, masked))
        grad_rows = jnp.concatenate(
            [
                attn_grad[
                    group * sz.tokens : (group + 1) * sz.tokens,
                    (first // sz.tokens + part) * sz.head_dim : (first // sz.tokens + part + 1)
                    * sz.head_dim,
                ]
                for part in range(heads_in)
            ],
            axis=0,
        )
        return probs, dot_nt(kv[slot, at, sz.head_dim :], grad_rows), query, grad_rows

    def finish(slot, first, at, got, delta):
        probs, prob_grad, query, grad_rows = got
        score_grad = (probs * (prob_grad - delta)).astype(bf16)
        key_part = dot_nn(score_grad, query)
        value_part = dot_nn(probs.astype(bf16), grad_rows)
        if first == 0:
            key_sum[...] = key_part
            value_sum[...] = value_part
        else:
            key_sum[...] += key_part
            value_sum[...] += value_part
        return dot_tn(score_grad, kv[slot, at, : sz.head_dim])

    for group in range(sz.groups):
        if block_count > 1:
            for first in chunks:
                at = slice(0, sz.span)
                got = probs_of(group, group, first, at)
                delta = jnp.sum(got[0] * got[1], axis=0, keepdims=True)
                query_grad[group, first : first + sz.chunk, :] = finish(
                    group, first, at, got, delta
                )
            for index in range(block_count):
                at = slice(index * sz.tokens, (index + 1) * sz.tokens)
                parts[index][group, :, : sz.head_dim] = key_sum[at, :].astype(bf16)
                parts[index][group, :, sz.head_dim :] = value_sum[at, :].astype(bf16)
            continue
        load_group(sz, blocks[0], group, kv, sems, 8)
        deltas = []
        for first in chunks:

            def add_delta(index, delta, first=first):
                got = probs_of(0, group, first, pl.ds(index * sz.span, sz.span))
                return delta + jnp.sum(got[0] * got[1], axis=0, keepdims=True)

            deltas.append(lax.fori_loop(0, spans, add_delta, jnp.zeros((1, sz.chunk), f32)))
            query_grad[group, first : first + sz.chunk, :] = jnp.zeros(
                (sz.chunk, sz.head_dim), f32
            )

        def add_span(index, carry):
            at = pl.ds(index * sz.span, sz.span)
            for first, delta in zip(chunks, deltas):
                query_grad[group, first : first + sz.chunk, :] += finish(
                    0, first, at, probs_of(0, group, first, at), delta
                )
            per_span = sz.span // sz.tokens
            for step in range(per_span):
                rows = slice(step * sz.tokens, (step + 1) * sz.tokens)
                target = parts[0].at[index * per_span + step, group]
                target[:, : sz.head_dim] = key_sum[rows, :].astype(bf16)
                target[:, sz.head_dim :] = value_sum[rows, :].astype(bf16)
            return carry

        lax.fori_loop(0, spans, add_span, 0)


def backward_layer(sz, grad, gains, saved, places, blocks, weights):
    rows, model = sz.rows, sz.model
    gain = struct((1, model), f32)
    outs = [
        struct((rows, model), f32),
        struct((rows, model), bf16),
        struct((rows, sz.ff), bf16),
        struct((rows, sz.ff), bf16),
        struct((rows, model), bf16),
        gain,
        gain,
        gain,
        struct((sz.groups, sz.head_rows, sz.head_dim), f32),
    ]
    outs += [struct(block.shape, bf16) for block in blocks]
    scratch = [
        pltpu.VMEM((sz.groups if len(blocks) > 1 else 1, sz.keys, 2 * sz.head_dim), bf16),
        pltpu.VMEM((sz.query_cols, model), bf16),
        pltpu.VMEM((model, sz.ff), bf16),
        pltpu.VMEM((model, sz.ff), bf16),
        pltpu.VMEM((sz.ff, model), bf16),
        pltpu.VMEM((sz.span, sz.head_dim), f32),
        pltpu.VMEM((sz.span, sz.head_dim), f32),
        pltpu.SemaphoreType.DMA((8 + sz.blocks,)),
    ]
    inputs = [
        grad, *gains, saved["down_out"], saved["gate"], saved["up"], saved["middle"],
        saved["branch"], saved["query_low"], saved["log_row"], places["key_col"],
        places["query_row"],
    ]
    far = [*blocks, *weights["out"], *weights["gate"], *weights["up"], *weights["down"]]
    got = call_kernel(
        functools.partial(backward_kernel, sz, len(blocks)), outs, inputs, far, scratch
    )
    return got[:9], got[9:]


def query_back_kernel(
    sz, query_grad, query_lin, gain_own, gain_other, cos_ref, sin_ref, q_own, q_other,
    lin_grad, normed_grad, gain_grad, wq, sems,
):
    copies = start_halves(q_own, q_other, wq, sems, 0)
    gain_query = whole_gain(gain_own, gain_other, *sz.gain_at["query"])
    cos = jnp.concatenate([cos_ref[...]] * sz.groups, axis=0)
    sin = jnp.concatenate([sin_ref[...]] * sz.groups, axis=0)
    gain_sum = jnp.zeros((1, sz.head_dim), f32)
    for head in range(sz.heads):
        cols = slice(head * sz.head_dim, (head + 1) * sz.head_dim)
        rows = slice(head * sz.tokens, (head + 1) * sz.tokens)
        grad = jnp.concatenate([query_grad[g, rows, :] for g in range(sz.groups)], axis=0)
        turned = rotate(grad * score_scale, cos, -sin)
        part, gain_part = norm_back(query_lin[:, cols], gain_query, turned)
        lin_grad[:, cols] = part.astype(bf16)
        gain_sum = gain_sum + gain_part
    gain_grad[...] = gain_sum
    wait_all(copies)
    normed_grad[...] = dot_nt(lin_grad[...], wq[...])


def query_back(sz, query_grad, query_lin, gains, tables, w_query):
    return call_kernel(
        functools.partial(query_back_kernel, sz),
        [
            struct((sz.rows, sz.query_cols), bf16),
            struct((sz.rows, sz.model), f32),
            struct((1, sz.head_dim), f32),
        ],
        [query_grad, query_lin, *gains, *tables],
        [*w_query],
        [pltpu.VMEM((sz.model, sz.query_cols), bf16), pltpu.SemaphoreType.DMA((2,))],
    )


def input_back_kernel(sz, term_count, *refs):
    terms, refs = refs[:term_count], refs[term_count:]
    (
        key_lin, hidden, query_part, middle_grad, gain_own, gain_other, cos_ref, sin_ref,
        k_own, k_other, v_own, v_other, input_grad, kv_grad, gain_input_grad, gain_key_grad,
        wk, wv, sems,
    ) = refs
    k_copies = start_halves(k_own, k_other, wk, sems, 0)
    v_copies = start_halves(v_own, v_other, wv, sems, 2)
    gain_input = whole_gain(gain_own, gain_other, *sz.gain_at["input"])
    gain_key = whole_gain(gain_own, gain_other, *sz.gain_at["key"])
    cos = jnp.concatenate([cos_ref[...]] * sz.groups, axis=0)
    sin = jnp.concatenate([sin_ref[...]] * sz.groups, axis=0)
    total = terms[0][...].astype(f32)
    for term in terms[1:]:
        total = total + term[...].astype(f32)
    turned = rotate(total[:, : sz.head_dim], cos, -sin)
    key_part, gain_key_grad[...] = norm_back(key_lin[...], gain_key, turned)
    key_low = key_part.astype(bf16)
    value_low = total[:, sz.head_dim :].astype(bf16)
    kv_grad[:, : sz.head_dim] = key_low
    kv_grad[:, sz.head_dim :] = value_low
    wait_all(k_copies)
    wait_all(v_copies)
    normed_grad = query_part[...] + dot_nt(key_low, wk[...]) + dot_nt(value_low, wv[...])
    part, gain_input_grad[...] = norm_back(hidden[...].astype(f32), gain_input, normed_grad)
    input_grad[...] = (middle_grad[...] + part).astype(bf16)


def input_back(sz, terms, key_lin, hidden, query_part, middle_grad, gains, tables, w_key, w_value):
    half = (sz.model, sz.head_dim)
    flat = [term.reshape(sz.rows, 2 * sz.head_dim) for term in terms]
    return call_kernel(
        functools.partial(input_back_kernel, sz, len(flat)),
        [
            struct((sz.rows, sz.model), bf16),
            struct((sz.rows, 2 * sz.head_dim), bf16),
            struct((1, sz.model), f32),
            struct((1, sz.head_dim), f32),
        ],
        [*flat, key_lin, hidden, query_part, middle_grad, *gains, *tables],
        [*w_key, *w_value],
        [pltpu.VMEM(half, bf16), pltpu.VMEM(half, bf16), pltpu.SemaphoreType.DMA((4,))],
    )


def xor_permute(shard, axis, mask):
    count = lax.axis_size(axis)
    return lax.ppermute(shard, axis, [(i, i ^ mask) for i in range(count)])


def small_ctx():
    return lax.axis_size("ctx") == 8


def ctx_order():
    count = lax.axis_size("ctx")
    slots = jnp.arange(count, dtype=jnp.int32)
    if small_ctx():
        return lax.axis_index("ctx") ^ slots
    return slots


def gather_ctx(shard):
    if not small_ctx():
        return [lax.all_gather(shard, "ctx", axis=0)]
    blocks = [None] * 8
    blocks[0] = shard
    for mask in (6, 4, 2):
        blocks[mask] = xor_permute(shard, "ctx", mask)
    for mask in (0, 2, 4, 6):
        blocks[mask + 1] = xor_permute(blocks[mask], "ctx", 1)
    return blocks


def scatter_ctx(parts):
    if len(parts) == 1:
        return [lax.psum_scatter(parts[0].astype(f32), "ctx", scatter_dimension=0, tiled=False)]
    terms = []
    for mask in (6, 4, 2):
        came = xor_permute(parts[mask + 1], "ctx", 1)
        both = (parts[mask].astype(f32) + came.astype(f32)).astype(bf16)
        terms.append(xor_permute(both, "ctx", mask))
    return terms + [parts[0], xor_permute(parts[1], "ctx", 1)]


def sum_ctx(shard):
    if not small_ctx():
        return lax.psum(shard.astype(f32), "ctx")
    ctx_index = lax.axis_index("ctx")
    y_index = ctx_index & 1
    z_index = ctx_index >> 1
    half = shard.shape[0] // 2
    keep = lax.dynamic_slice_in_dim(shard, y_index * half, half, 0)
    send = lax.dynamic_slice_in_dim(shard, (1 - y_index) * half, half, 0)
    came = xor_permute(send, "ctx", 1)
    inward = [(z * 2 + y, t * 2 + y) for z, t in ((0, 1), (3, 2)) for y in (0, 1)]
    middle = [(z * 2 + y, t * 2 + y) for z, t in ((1, 2), (2, 1)) for y in (0, 1)]
    outward = [(z * 2 + y, t * 2 + y) for z, t in ((1, 0), (2, 3)) for y in (0, 1)]

    def add(left, right):
        return lax.optimization_barrier((left.astype(f32) + right.astype(f32)).astype(bf16))

    part = add(keep, came)
    part = add(part, lax.ppermute(part, "ctx", inward))
    part = add(part, lax.ppermute(part, "ctx", middle))
    back = lax.ppermute(part, "ctx", outward)
    total = jnp.where((z_index == 1) | (z_index == 2), part, back)
    other = xor_permute(total, "ctx", 1)
    first = jnp.where(y_index == 0, total, other)
    second = jnp.where(y_index == 0, other, total)
    return jnp.concatenate([first, second], axis=0).astype(f32)


def weight_term(left, right):
    half = left.shape[1] // 2
    fsdp_index = lax.axis_index("fsdp")
    keep = lax.dynamic_slice_in_dim(left, fsdp_index * half, half, 1)
    send = lax.dynamic_slice_in_dim(left, (1 - fsdp_index) * half, half, 1)
    came = xor_permute(dot_tn(send, right).astype(bf16), "fsdp", 1)
    return (dot_tn(keep, right) + came.astype(f32)).astype(bf16)


def on_device(
    inputs,
    out_cotangent,
    block_order,
    w_query,
    w_key,
    w_value,
    w_output,
    w_gate,
    w_up,
    w_down,
    g_input,
    g_query,
    g_key,
    g_post_attn,
    g_pre_ffw,
    g_post_ffw,
):
    section_index = lax.axis_index("section")
    fsdp_index = lax.axis_index("fsdp")
    ctx_index = lax.axis_index("ctx")
    ctx_size = lax.axis_size("ctx")
    micro_count, seq_local, tokens, model_width = inputs.shape
    head_dim = 2 * g_query.shape[1]
    sz = Sizes(
        micro_count * seq_local,
        tokens,
        model_width,
        w_query.shape[2] // head_dim,
        head_dim,
        w_gate.shape[2],
        ctx_size,
    )
    block_len = tokens // 2
    gains_own = jnp.concatenate([g_input, g_post_attn, g_pre_ffw, g_post_ffw, g_query, g_key], 1)
    gains = (gains_own, xor_permute(gains_own, "fsdp", 1))
    weights = {}
    for name, own in (
        ("key", w_key),
        ("value", w_value),
        ("query", w_query),
        ("out", w_output),
        ("gate", w_gate),
        ("up", w_up),
        ("down", w_down),
    ):
        weights[name] = (own[0], xor_permute(own[0], "fsdp", 1))
    slot_pairs = block_order.reshape(ctx_size, 2)
    offsets = jnp.arange(block_len, dtype=jnp.int32)

    def spread(slot_ids):
        return (slot_ids.reshape(-1)[:, None] * block_len + offsets[None, :]).reshape(-1)

    local_pos = spread(slot_pairs[ctx_index])
    key_pos = spread(slot_pairs[ctx_order()])
    tables = rotation_tables(local_pos, head_dim // 2)
    query_pos = jnp.tile(local_pos, sz.heads)
    places = {
        "key_row": key_pos.reshape(1, -1),
        "key_col": key_pos.reshape(-1, 1),
        "query_row": query_pos.reshape(1, -1),
        "query_col": query_pos.reshape(-1, 1),
    }
    block_shape = (sz.groups, tokens, 2 * head_dim)

    def forward(hidden, save):
        normed, key_lin, kv_low = project_kv(
            sz, hidden, gains, tables, weights["key"], weights["value"]
        )
        blocks = gather_ctx(kv_low.reshape(block_shape))
        query_lin, query_low = project_query(sz, normed, gains, tables, weights["query"])
        got = forward_layer(sz, query_low, hidden, gains, places, blocks, weights, save)
        if not save:
            return got[0], None
        names = (
            "log_total", "attn_low", "branch", "middle", "pre_ffw", "gate", "up", "act", "down_out"
        )
        saved = dict(zip(names, got[1:]))
        saved["log_row"] = saved["log_total"].reshape(sz.groups, 1, sz.head_rows)
        saved.update(
            hidden=hidden, normed=normed, key_lin=key_lin, query_lin=query_lin,
            query_low=query_low, blocks=blocks,
        )
        return got[0], saved

    def backward(grad, saved):
        got, parts = backward_layer(sz, grad, gains, saved, places, saved["blocks"], weights)
        middle_grad = got[0]
        query_low_grad, query_part, gain_query = query_back(
            sz, got[8], saved["query_lin"], gains, tables, weights["query"]
        )
        terms = scatter_ctx(parts)
        input_grad, kv_grad, gain_input, gain_key = input_back(
            sz, terms, saved["key_lin"], saved["hidden"], query_part, middle_grad, gains, tables,
            weights["key"], weights["value"],
        )
        return input_grad, dict(
            down=got[1], gate=got[2], up=got[3], branch=got[4], post=got[5], pre=got[6],
            attn=got[7], query_lin=query_low_grad, query=gain_query, kv=kv_grad,
            input=gain_input, key=gain_key,
        )

    own_input = inputs.reshape(sz.rows, model_width)
    first_result, _ = forward(own_input, False)
    received = lax.ppermute(first_result, "section", [(0, 1)])
    hidden = jnp.where(section_index == 0, own_input, received)
    result, saved = forward(hidden, True)
    own_grad = out_cotangent.reshape(sz.rows, model_width)
    first_grad, _ = backward(own_grad, saved)
    grad_received = lax.ppermute(first_grad, "section", [(1, 0)])
    grad_in = jnp.where(section_index == 1, own_grad, grad_received)
    input_grad, grads = backward(grad_in, saved)

    sum_down = sum_ctx(weight_term(saved["act"], grads["down"]))
    sum_gate = sum_ctx(weight_term(saved["pre_ffw"], grads["gate"]))
    sum_up = sum_ctx(weight_term(saved["pre_ffw"], grads["up"]))
    sum_out = sum_ctx(weight_term(saved["attn_low"], grads["branch"]))
    sum_query = sum_ctx(weight_term(saved["normed"], grads["query_lin"]))
    names = ("input", "attn", "pre", "post", "query", "key")
    gain_rows = jnp.concatenate([grads[name].reshape(2, -1) for name in names], axis=1)
    kv_width = 2 * head_dim
    gain_rows = gain_rows.reshape(2, -1, kv_width)
    gain_count = gain_rows.shape[1]
    gain_rows = jnp.pad(gain_rows, ((0, 0), (0, 32 - gain_count), (0, 0)))
    gain_keep = lax.dynamic_index_in_dim(gain_rows, fsdp_index, 0, keepdims=False)
    gain_send = lax.dynamic_index_in_dim(gain_rows, 1 - fsdp_index, 0, keepdims=False)
    gain_came = xor_permute(gain_send.astype(bf16), "fsdp", 1)
    gain_term = (gain_keep + gain_came.astype(f32)).astype(bf16)
    kv_term = weight_term(saved["normed"], grads["kv"])
    sum_tail = sum_ctx(jnp.concatenate([kv_term, gain_term], axis=0))
    half_model = model_width // 2
    sum_key = sum_tail[:half_model, :head_dim]
    sum_value = sum_tail[:half_model, head_dim:]
    sum_gains = sum_tail[half_model : half_model + gain_count].reshape(-1)
    gain_sums = {}
    for name in names:
        start, width = sz.gain_at[name]
        gain_sums[name] = sum_gains[start : start + width]
    shape = (micro_count, seq_local, tokens, model_width)
    members = (
        sum_query,
        sum_key,
        sum_value,
        sum_out,
        sum_gate,
        sum_up,
        sum_down,
        gain_sums["input"],
        gain_sums["query"],
        gain_sums["key"],
        gain_sums["attn"],
        gain_sums["pre"],
        gain_sums["post"],
    )
    return (result.reshape(shape)[None], input_grad.reshape(shape)[None]) + tuple(
        member[None] for member in members
    )


def solution(mesh):
    weight = P("section", "fsdp", None)
    gain = P("section", "fsdp")
    in_specs = (P(None, "fsdp", "ctx", None),) * 2 + (P(),) + (weight,) * 7 + (gain,) * 6
    out_specs = (
        (P("section", None, "fsdp", "ctx", None),) * 2 + (weight,) * 7 + (gain,) * 6
    )
    return jax.shard_map(
        on_device, mesh=mesh, in_specs=in_specs, out_specs=out_specs, check_vma=False
    )
```

```python
import functools

import jax
import jax.numpy as jnp
from jax import lax
from jax.experimental import pallas as pl
from jax.experimental.pallas import tpu as pltpu
from jax.sharding import PartitionSpec as P

epsilon = 1e-06
rope_base = 1000000.0
masked = -1e30
score_scale = 0.0625
gelu_slope = 0.7978845608028654
gelu_cubic = 0.044715
f32 = jnp.float32
bf16 = jnp.bfloat16
vmem_bytes = 56 * 1024 * 1024


def dot_nn(left, right):
    return jnp.dot(left, right, preferred_element_type=f32)


def dot_nt(left, right):
    return lax.dot_general(left, right, (((1,), (1,)), ((), ())), preferred_element_type=f32)


def dot_tn(left, right):
    return lax.dot_general(left, right, (((0,), (0,)), ((), ())), preferred_element_type=f32)


def norm_factor(values_in):
    return lax.rsqrt(jnp.mean(values_in * values_in, axis=-1, keepdims=True) + epsilon)


def norm_apply(values_in, gain_vec):
    return values_in * norm_factor(values_in) * gain_vec


def norm_back(values_in, gain_vec, grad_out):
    factor = norm_factor(values_in)
    scaled = grad_out * gain_vec
    grad_in = factor * (
        scaled - values_in * factor * factor * jnp.mean(scaled * values_in, axis=-1, keepdims=True)
    )
    grad_gain = jnp.sum(grad_out * values_in * factor, axis=0, keepdims=True)
    return (grad_in, grad_gain)


def rotate(values_in, cos_table, sin_table):
    half_width = values_in.shape[-1] // 2
    former = values_in[..., :half_width]
    latter = values_in[..., half_width:]
    return jnp.concatenate(
        [former * cos_table - latter * sin_table, latter * cos_table + former * sin_table], axis=-1
    )


def rotation_tables(positions, half_width):
    frequency = rope_base ** (-jnp.arange(half_width, dtype=f32) / half_width)
    angles = positions.astype(f32)[:, None] * frequency[None, :]
    return (jnp.cos(angles), jnp.sin(angles))


def call_kernel(body, out_shapes, inputs, far_inputs, scratch):
    whole = pl.BlockSpec(memory_space=pltpu.VMEM)
    far = pl.BlockSpec(memory_space=pl.ANY)
    return pl.pallas_call(
        body,
        out_shape=out_shapes,
        in_specs=[whole] * len(inputs) + [far] * len(far_inputs),
        out_specs=jax.tree.map(lambda _: whole, out_shapes),
        scratch_shapes=scratch,
        compiler_params=pltpu.CompilerParams(vmem_limit_bytes=vmem_bytes),
    )(*inputs, *far_inputs)


def struct(shape, dtype):
    return jax.ShapeDtypeStruct(shape, dtype)


def start_halves(own, other, target, sems, first_sem):
    half = own.shape[0]
    fsdp_index = lax.axis_index("fsdp")
    copies = [
        pltpu.make_async_copy(
            own, target.at[pl.ds(fsdp_index * half, half)], sems.at[first_sem]
        ),
        pltpu.make_async_copy(
            other, target.at[pl.ds((1 - fsdp_index) * half, half)], sems.at[first_sem + 1]
        ),
    ]
    for copy in copies:
        copy.start()
    return copies


def wait_all(copies):
    for copy in copies:
        copy.wait()


def whole_gain(own_ref, other_ref, start, width):
    own = own_ref[:, start : start + width].astype(f32)
    other = other_ref[:, start : start + width].astype(f32)
    is_first = lax.axis_index("fsdp") == 0
    return jnp.concatenate(
        [jnp.where(is_first, own, other), jnp.where(is_first, other, own)], axis=1
    )


class Sizes:
    def __init__(self, groups, tokens, model, heads, head_dim, ff, blocks):
        self.groups, self.tokens, self.model = groups, tokens, model
        self.heads, self.head_dim, self.ff, self.blocks = heads, head_dim, ff, blocks
        self.rows = groups * tokens
        self.query_cols = heads * head_dim
        self.head_rows = heads * tokens
        self.keys = blocks * tokens
        self.span = tokens * min(8, blocks)
        self.chunk = min(256, self.head_rows)
        half = model // 2
        self.gain_at = {
            "input": (0, half),
            "attn": (half, half),
            "pre": (2 * half, half),
            "post": (3 * half, half),
            "query": (4 * half, head_dim // 2),
            "key": (4 * half + head_dim // 2, head_dim // 2),
        }


def kv_kernel(
    sz, hidden, gain_own, gain_other, cos_ref, sin_ref, k_own, k_other, v_own, v_other,
    normed, key_lin, kv_low, wk, wv, sems,
):
    k_copies = start_halves(k_own, k_other, wk, sems, 0)
    v_copies = start_halves(v_own, v_other, wv, sems, 2)
    gain_input = whole_gain(gain_own, gain_other, *sz.gain_at["input"])
    gain_key = whole_gain(gain_own, gain_other, *sz.gain_at["key"])
    low = norm_apply(hidden[...].astype(f32), gain_input).astype(bf16)
    normed[...] = low
    wait_all(k_copies)
    lin = dot_nn(low, wk[...])
    key_lin[...] = lin
    cos = jnp.concatenate([cos_ref[...]] * sz.groups, axis=0)
    sin = jnp.concatenate([sin_ref[...]] * sz.groups, axis=0)
    kv_low[:, : sz.head_dim] = rotate(norm_apply(lin, gain_key), cos, sin).astype(bf16)
    wait_all(v_copies)
    kv_low[:, sz.head_dim :] = dot_nn(low, wv[...]).astype(bf16)


def project_kv(sz, hidden, gains, tables, w_key, w_value):
    half = (sz.model, sz.head_dim)
    return call_kernel(
        functools.partial(kv_kernel, sz),
        [
            struct((sz.rows, sz.model), bf16),
            struct((sz.rows, sz.head_dim), f32),
            struct((sz.rows, 2 * sz.head_dim), bf16),
        ],
        [hidden, *gains, *tables],
        [*w_key, *w_value],
        [pltpu.VMEM(half, bf16), pltpu.VMEM(half, bf16), pltpu.SemaphoreType.DMA((4,))],
    )


def query_kernel(
    sz, normed, gain_own, gain_other, cos_ref, sin_ref, q_own, q_other,
    query_lin, query_low, wq, sems,
):
    copies = start_halves(q_own, q_other, wq, sems, 0)
    gain_query = whole_gain(gain_own, gain_other, *sz.gain_at["query"])
    cos = jnp.concatenate([cos_ref[...]] * sz.groups, axis=0)
    sin = jnp.concatenate([sin_ref[...]] * sz.groups, axis=0)
    low = normed[...]
    wait_all(copies)
    for head in range(sz.heads):
        cols = slice(head * sz.head_dim, (head + 1) * sz.head_dim)
        lin = dot_nn(low, wq[:, cols])
        query_lin[:, cols] = lin
        turned = rotate(norm_apply(lin, gain_query), cos, sin)
        turned = (turned.astype(bf16).astype(f32) * score_scale).astype(bf16)
        for group in range(sz.groups):
            query_low[group, head * sz.tokens : (head + 1) * sz.tokens, :] = turned[
                group * sz.tokens : (group + 1) * sz.tokens
            ]


def project_query(sz, normed, gains, tables, w_query):
    return call_kernel(
        functools.partial(query_kernel, sz),
        [
            struct((sz.rows, sz.query_cols), f32),
            struct((sz.groups, sz.head_rows, sz.head_dim), bf16),
        ],
        [normed, *gains, *tables],
        [*w_query],
        [pltpu.VMEM((sz.model, sz.query_cols), bf16), pltpu.SemaphoreType.DMA((2,))],
    )


def start_blocks(sz, blocks, target, sems, first_sem):
    copies = []
    for index, block in enumerate(blocks):
        copies.append(
            pltpu.make_async_copy(
                block,
                target.at[:, pl.ds(index * sz.tokens, sz.tokens)],
                sems.at[first_sem + index],
            )
        )
    for copy in copies:
        copy.start()
    return copies


def load_group(sz, stacked, group, target, sems, first_sem):
    def one(index):
        return pltpu.make_async_copy(
            stacked.at[index, group],
            target.at[0, pl.ds(index * sz.tokens, sz.tokens)],
            sems.at[first_sem + index],
        )

    def start(index, carry):
        one(index).start()
        return carry

    def wait(index, carry):
        one(index).wait()
        return carry

    lax.fori_loop(0, sz.blocks, start, 0)
    lax.fori_loop(0, sz.blocks, wait, 0)


def forward_kernel(sz, block_count, save, *refs):
    query_low, hidden, gain_own, gain_other, key_row, query_col = refs[:6]
    refs = refs[6:]
    blocks, refs = refs[:block_count], refs[block_count:]
    out_pair, gate_pair, up_pair, down_pair = (refs[2 * i : 2 * i + 2] for i in range(4))
    refs = refs[8:]
    result, refs = refs[0], refs[1:]
    if save:
        log_total, attn_low, branch_ref, middle_ref, pre_ref, gate_ref, up_ref, act_ref, down_ref = (
            refs[:9]
        )
        refs = refs[9:]
    else:
        attn_low, act_ref = refs[:2]
        refs = refs[2:]
    kv, w_out, w_gate, w_up, w_down, sems = refs
    if block_count > 1:
        kv_copies = start_blocks(sz, blocks, kv, sems, 8)
    out_copies = start_halves(*out_pair, w_out, sems, 0)
    gate_copies = start_halves(*gate_pair, w_gate, sems, 2)
    up_copies = start_halves(*up_pair, w_up, sems, 4)
    down_copies = start_halves(*down_pair, w_down, sems, 6)
    gain_attn = whole_gain(gain_own, gain_other, *sz.gain_at["attn"])
    gain_pre = whole_gain(gain_own, gain_other, *sz.gain_at["pre"])
    gain_post = whole_gain(gain_own, gain_other, *sz.gain_at["post"])
    if block_count > 1:
        wait_all(kv_copies)
    spans = sz.keys // sz.span
    for group in range(sz.groups):
        slot = group if block_count > 1 else 0
        if block_count == 1:
            load_group(sz, blocks[0], group, kv, sems, 8)
        for first in range(0, sz.head_rows, sz.chunk):
            query = query_low[group, first : first + sz.chunk, :]
            query_pos = query_col[first : first + sz.chunk, :]

            def one_span(index, state):
                row_max, row_total, row_sum = state
                at = pl.ds(index * sz.span, sz.span)
                scores = dot_nt(query, kv[slot, at, : sz.head_dim])
                scores = jnp.where(key_row[:, at] <= query_pos, scores, masked)
                new_max = jnp.maximum(row_max, jnp.max(scores, axis=1, keepdims=True))
                probs = jnp.exp(scores - new_max)
                part = dot_nn(probs.astype(bf16), kv[slot, at, sz.head_dim :])
                shrink = jnp.exp(row_max - new_max)
                return (
                    new_max,
                    row_total * shrink + jnp.sum(probs, axis=1, keepdims=True),
                    row_sum * shrink + part,
                )

            state = (
                jnp.full((sz.chunk, 1), masked, f32),
                jnp.zeros((sz.chunk, 1), f32),
                jnp.zeros((sz.chunk, sz.head_dim), f32),
            )
            if spans == 1:
                state = one_span(0, state)
            else:
                state = lax.fori_loop(0, spans, one_span, state)
            row_max, row_total, row_sum = state
            attended = (row_sum / row_total).astype(bf16)
            if save:
                log_total[group, first : first + sz.chunk, :] = row_max + jnp.log(row_total)
            for part in range(sz.chunk // sz.tokens):
                head = first // sz.tokens + part
                attn_low[
                    group * sz.tokens : (group + 1) * sz.tokens,
                    head * sz.head_dim : (head + 1) * sz.head_dim,
                ] = attended[part * sz.tokens : (part + 1) * sz.tokens]
    wait_all(out_copies)
    branch = dot_nn(attn_low[...], w_out[...])
    middle = hidden[...].astype(f32) + norm_apply(branch, gain_attn)
    pre_ffw = norm_apply(middle, gain_pre).astype(bf16)
    if save:
        branch_ref[...] = branch
        middle_ref[...] = middle
        pre_ref[...] = pre_ffw
    wait_all(gate_copies)
    wait_all(up_copies)
    step = min(512, sz.ff)
    for first in range(0, sz.ff, step):
        cols = slice(first, first + step)
        gate = dot_nn(pre_ffw, w_gate[:, cols])
        up = dot_nn(pre_ffw, w_up[:, cols])
        if save:
            gate_ref[:, cols] = gate
            up_ref[:, cols] = up
        bend = jnp.tanh(gelu_slope * (gate + gelu_cubic * gate * gate * gate))
        act_ref[:, cols] = (0.5 * gate * (1.0 + bend) * up).astype(bf16)
    wait_all(down_copies)
    down_out = dot_nn(act_ref[...], w_down[...])
    if save:
        down_ref[...] = down_out
    result[...] = (middle + norm_apply(down_out, gain_post)).astype(bf16)


def forward_layer(sz, query_low, hidden, gains, places, blocks, weights, save):
    rows, model = sz.rows, sz.model
    outs = [struct((rows, model), bf16)]
    attn = (rows, sz.query_cols)
    act = (rows, sz.ff)
    scratch = []
    if save:
        outs += [
            struct((sz.groups, sz.head_rows, 1), f32),
            struct(attn, bf16),
            struct((rows, model), f32),
            struct((rows, model), f32),
            struct((rows, model), bf16),
            struct(act, f32),
            struct(act, f32),
            struct(act, bf16),
            struct((rows, model), f32),
        ]
    else:
        scratch += [pltpu.VMEM(attn, bf16), pltpu.VMEM(act, bf16)]
    scratch += [
        pltpu.VMEM((sz.groups if len(blocks) > 1 else 1, sz.keys, 2 * sz.head_dim), bf16),
        pltpu.VMEM((sz.query_cols, model), bf16),
        pltpu.VMEM((model, sz.ff), bf16),
        pltpu.VMEM((model, sz.ff), bf16),
        pltpu.VMEM((sz.ff, model), bf16),
        pltpu.SemaphoreType.DMA((8 + sz.blocks,)),
    ]
    far = [*blocks, *weights["out"], *weights["gate"], *weights["up"], *weights["down"]]
    return call_kernel(
        functools.partial(forward_kernel, sz, len(blocks), save),
        outs,
        [query_low, hidden, *gains, places["key_row"], places["query_col"]],
        far,
        scratch,
    )


def ffw_back_kernel(sz, *refs):
    grad_ref, gain_own, gain_other, down_out, gate_ref, up_ref, middle, branch = refs[:8]
    refs = refs[8:]
    out_pair, gate_pair, up_pair, down_pair = (refs[2 * i : 2 * i + 2] for i in range(4))
    refs = refs[8:]
    (
        middle_grad, down_grad, gate_grad, up_grad, branch_grad, gain_post_grad, gain_pre_grad,
        gain_attn_grad, attn_grad,
    ) = refs[:9]
    w_out, w_gate, w_up, w_down, sems = refs[9:]
    down_copies = start_halves(*down_pair, w_down, sems, 0)
    gate_copies = start_halves(*gate_pair, w_gate, sems, 2)
    up_copies = start_halves(*up_pair, w_up, sems, 4)
    out_copies = start_halves(*out_pair, w_out, sems, 6)
    gain_attn = whole_gain(gain_own, gain_other, *sz.gain_at["attn"])
    gain_pre = whole_gain(gain_own, gain_other, *sz.gain_at["pre"])
    gain_post = whole_gain(gain_own, gain_other, *sz.gain_at["post"])
    grad = grad_ref[...].astype(f32)
    down_part, gain_post_grad[...] = norm_back(down_out[...], gain_post, grad)
    down_low = down_part.astype(bf16)
    down_grad[...] = down_low
    wait_all(down_copies)
    wait_all(gate_copies)
    wait_all(up_copies)
    step = min(512, sz.ff)
    pre_grad = jnp.zeros((sz.rows, sz.model), f32)
    for first in range(0, sz.ff, step):
        cols = slice(first, first + step)
        ffw_grad = dot_nt(down_low, w_down[cols, :])
        gate = gate_ref[:, cols]
        up = up_ref[:, cols]
        square = gate * gate
        bend = jnp.tanh(gelu_slope * (gate + gelu_cubic * square * gate))
        half_open = 0.5 * (1.0 + bend)
        slope = half_open + 0.5 * gate * (1.0 - bend * bend) * gelu_slope * (
            1.0 + 3.0 * gelu_cubic * square
        )
        gate_low = (ffw_grad * up * slope).astype(bf16)
        up_low = (ffw_grad * gate * half_open).astype(bf16)
        gate_grad[:, cols] = gate_low
        up_grad[:, cols] = up_low
        pre_grad = pre_grad + dot_nt(gate_low, w_gate[:, cols]) + dot_nt(up_low, w_up[:, cols])
    middle_part, gain_pre_grad[...] = norm_back(middle[...], gain_pre, pre_grad)
    total = grad + middle_part
    middle_grad[...] = total
    branch_part, gain_attn_grad[...] = norm_back(branch[...], gain_attn, total)
    branch_low = branch_part.astype(bf16)
    branch_grad[...] = branch_low
    wait_all(out_copies)
    attn_grad[...] = dot_nt(branch_low, w_out[...]).astype(bf16)


def attn_back_kernel(sz, block_count, *refs):
    attn_grad, query_low, log_row, key_col, query_row = refs[:5]
    refs = refs[5:]
    blocks, refs = refs[:block_count], refs[block_count:]
    query_grad, refs = refs[0], refs[1:]
    parts, refs = refs[:block_count], refs[block_count:]
    kv, key_sum, value_sum, sems = refs
    if block_count > 1:
        wait_all(start_blocks(sz, blocks, kv, sems, 0))
    spans = sz.keys // sz.span
    heads_in = sz.chunk // sz.tokens
    chunks = range(0, sz.head_rows, sz.chunk)

    def probs_of(slot, group, first, at):
        query = query_low[group, first : first + sz.chunk, :]
        query_pos = query_row[:, first : first + sz.chunk]
        log_here = log_row[group, :, first : first + sz.chunk]
        scores = dot_nt(kv[slot, at, : sz.head_dim], query)
        probs = jnp.exp(jnp.where(key_col[at, :] <= query_pos, scores - log_here, masked))
        grad_rows = jnp.concatenate(
            [
                attn_grad[
                    group * sz.tokens : (group + 1) * sz.tokens,
                    (first // sz.tokens + part) * sz.head_dim : (first // sz.tokens + part + 1)
                    * sz.head_dim,
                ]
                for part in range(heads_in)
            ],
            axis=0,
        )
        return probs, dot_nt(kv[slot, at, sz.head_dim :], grad_rows), query, grad_rows

    def finish(slot, first, at, got, delta):
        probs, prob_grad, query, grad_rows = got
        score_grad = (probs * (prob_grad - delta)).astype(bf16)
        key_part = dot_nn(score_grad, query)
        value_part = dot_nn(probs.astype(bf16), grad_rows)
        if first == 0:
            key_sum[...] = key_part
            value_sum[...] = value_part
        else:
            key_sum[...] += key_part
            value_sum[...] += value_part
        return dot_tn(score_grad, kv[slot, at, : sz.head_dim])

    for group in range(sz.groups):
        if block_count > 1:
            for first in chunks:
                at = slice(0, sz.span)
                got = probs_of(group, group, first, at)
                delta = jnp.sum(got[0] * got[1], axis=0, keepdims=True)
                query_grad[group, first : first + sz.chunk, :] = finish(
                    group, first, at, got, delta
                )
            for index in range(block_count):
                at = slice(index * sz.tokens, (index + 1) * sz.tokens)
                parts[index][group, :, : sz.head_dim] = key_sum[at, :].astype(bf16)
                parts[index][group, :, sz.head_dim :] = value_sum[at, :].astype(bf16)
            continue
        load_group(sz, blocks[0], group, kv, sems, 0)
        deltas = []
        for first in chunks:

            def add_delta(index, delta, first=first):
                got = probs_of(0, group, first, pl.ds(index * sz.span, sz.span))
                return delta + jnp.sum(got[0] * got[1], axis=0, keepdims=True)

            deltas.append(lax.fori_loop(0, spans, add_delta, jnp.zeros((1, sz.chunk), f32)))
            query_grad[group, first : first + sz.chunk, :] = jnp.zeros(
                (sz.chunk, sz.head_dim), f32
            )

        def add_span(index, carry):
            at = pl.ds(index * sz.span, sz.span)
            for first, delta in zip(chunks, deltas):
                query_grad[group, first : first + sz.chunk, :] += finish(
                    0, first, at, probs_of(0, group, first, at), delta
                )
            per_span = sz.span // sz.tokens
            for step in range(per_span):
                rows = slice(step * sz.tokens, (step + 1) * sz.tokens)
                target = parts[0].at[index * per_span + step, group]
                target[:, : sz.head_dim] = key_sum[rows, :].astype(bf16)
                target[:, sz.head_dim :] = value_sum[rows, :].astype(bf16)
            return carry

        lax.fori_loop(0, spans, add_span, 0)


def ffw_back(sz, grad, gains, saved, weights):
    rows, model = sz.rows, sz.model
    gain = struct((1, model), f32)
    outs = [
        struct((rows, model), f32),
        struct((rows, model), bf16),
        struct((rows, sz.ff), bf16),
        struct((rows, sz.ff), bf16),
        struct((rows, model), bf16),
        gain,
        gain,
        gain,
        struct((rows, sz.query_cols), bf16),
    ]
    scratch = [
        pltpu.VMEM((sz.query_cols, model), bf16),
        pltpu.VMEM((model, sz.ff), bf16),
        pltpu.VMEM((model, sz.ff), bf16),
        pltpu.VMEM((sz.ff, model), bf16),
        pltpu.SemaphoreType.DMA((8,)),
    ]
    inputs = [
        grad, *gains, saved["down_out"], saved["gate"], saved["up"], saved["middle"],
        saved["branch"],
    ]
    far = [*weights["out"], *weights["gate"], *weights["up"], *weights["down"]]
    return call_kernel(functools.partial(ffw_back_kernel, sz), outs, inputs, far, scratch)


def attn_back(sz, attn_grad, saved, places):
    blocks = saved["blocks"]
    outs = [struct((sz.groups, sz.head_rows, sz.head_dim), f32)]
    outs += [struct(block.shape, bf16) for block in blocks]
    scratch = [
        pltpu.VMEM((sz.groups if len(blocks) > 1 else 1, sz.keys, 2 * sz.head_dim), bf16),
        pltpu.VMEM((sz.span, sz.head_dim), f32),
        pltpu.VMEM((sz.span, sz.head_dim), f32),
        pltpu.SemaphoreType.DMA((sz.blocks,)),
    ]
    inputs = [
        attn_grad, saved["query_low"], saved["log_row"], places["key_col"], places["query_row"]
    ]
    got = call_kernel(
        functools.partial(attn_back_kernel, sz, len(blocks)), outs, inputs, blocks, scratch
    )
    return got[0], got[1:]


def weight_kernel(sz, cuts, left, right, *refs):
    outs, turned = refs[:-1], refs[-1]
    turned[...] = left[...].T
    half = left.shape[1] // 2
    fsdp_index = lax.axis_index("fsdp")
    y_index = lax.axis_index("ctx") & 1
    for side, owner in ((0, 1 - fsdp_index), (1, fsdp_index)):
        for part, y_half in ((0, y_index), (1, 1 - y_index)):
            first = pl.multiple_of(owner * half + y_half * (half // 2), 16)
            rows = turned[pl.ds(first, half // 2), :]
            for index, (start, stop) in enumerate(cuts):
                outs[2 * index + side][part * (half // 2) : (part + 1) * (half // 2), :] = dot_nn(
                    rows, right[:, start:stop]
                ).astype(bf16)


def weight_terms(sz, left, right, pieces):
    half = left.shape[1] // 2
    width = right.shape[1] // pieces
    cuts = [(index * width, (index + 1) * width) for index in range(pieces)]
    outs = [struct((half, width), bf16)] * (2 * pieces)
    got = call_kernel(
        functools.partial(weight_kernel, sz, cuts),
        outs,
        [left, right],
        [],
        [pltpu.VMEM((left.shape[1], left.shape[0]), bf16)],
    )
    return [(got[2 * index], got[2 * index + 1]) for index in range(pieces)]


def query_back_kernel(
    sz, query_grad, query_lin, gain_own, gain_other, cos_ref, sin_ref, q_own, q_other,
    lin_grad, normed_grad, gain_grad, wq, sems,
):
    copies = start_halves(q_own, q_other, wq, sems, 0)
    gain_query = whole_gain(gain_own, gain_other, *sz.gain_at["query"])
    cos = jnp.concatenate([cos_ref[...]] * sz.groups, axis=0)
    sin = jnp.concatenate([sin_ref[...]] * sz.groups, axis=0)
    gain_sum = jnp.zeros((1, sz.head_dim), f32)
    for head in range(sz.heads):
        cols = slice(head * sz.head_dim, (head + 1) * sz.head_dim)
        rows = slice(head * sz.tokens, (head + 1) * sz.tokens)
        grad = jnp.concatenate([query_grad[g, rows, :] for g in range(sz.groups)], axis=0)
        turned = rotate(grad * score_scale, cos, -sin)
        part, gain_part = norm_back(query_lin[:, cols], gain_query, turned)
        lin_grad[:, cols] = part.astype(bf16)
        gain_sum = gain_sum + gain_part
    gain_grad[...] = gain_sum
    wait_all(copies)
    normed_grad[...] = dot_nt(lin_grad[...], wq[...])


def query_back(sz, query_grad, query_lin, gains, tables, w_query):
    return call_kernel(
        functools.partial(query_back_kernel, sz),
        [
            struct((sz.rows, sz.query_cols), bf16),
            struct((sz.rows, sz.model), f32),
            struct((1, sz.head_dim), f32),
        ],
        [query_grad, query_lin, *gains, *tables],
        [*w_query],
        [pltpu.VMEM((sz.model, sz.query_cols), bf16), pltpu.SemaphoreType.DMA((2,))],
    )


def input_back_kernel(sz, term_count, *refs):
    terms, refs = refs[:term_count], refs[term_count:]
    (
        key_lin, hidden, query_part, middle_grad, gain_own, gain_other, cos_ref, sin_ref,
        k_own, k_other, v_own, v_other, input_grad, kv_grad, gain_input_grad, gain_key_grad,
        wk, wv, sems,
    ) = refs
    k_copies = start_halves(k_own, k_other, wk, sems, 0)
    v_copies = start_halves(v_own, v_other, wv, sems, 2)
    gain_input = whole_gain(gain_own, gain_other, *sz.gain_at["input"])
    gain_key = whole_gain(gain_own, gain_other, *sz.gain_at["key"])
    cos = jnp.concatenate([cos_ref[...]] * sz.groups, axis=0)
    sin = jnp.concatenate([sin_ref[...]] * sz.groups, axis=0)
    total = terms[0][...].astype(f32)
    for term in terms[1:]:
        total = total + term[...].astype(f32)
    turned = rotate(total[:, : sz.head_dim], cos, -sin)
    key_part, gain_key_grad[...] = norm_back(key_lin[...], gain_key, turned)
    key_low = key_part.astype(bf16)
    value_low = total[:, sz.head_dim :].astype(bf16)
    kv_grad[:, : sz.head_dim] = key_low
    kv_grad[:, sz.head_dim :] = value_low
    wait_all(k_copies)
    wait_all(v_copies)
    normed_grad = query_part[...] + dot_nt(key_low, wk[...]) + dot_nt(value_low, wv[...])
    part, gain_input_grad[...] = norm_back(hidden[...].astype(f32), gain_input, normed_grad)
    input_grad[...] = (middle_grad[...] + part).astype(bf16)


def input_back(sz, terms, key_lin, hidden, query_part, middle_grad, gains, tables, w_key, w_value):
    half = (sz.model, sz.head_dim)
    flat = [term.reshape(sz.rows, 2 * sz.head_dim) for term in terms]
    return call_kernel(
        functools.partial(input_back_kernel, sz, len(flat)),
        [
            struct((sz.rows, sz.model), bf16),
            struct((sz.rows, 2 * sz.head_dim), bf16),
            struct((1, sz.model), f32),
            struct((1, sz.head_dim), f32),
        ],
        [*flat, key_lin, hidden, query_part, middle_grad, *gains, *tables],
        [*w_key, *w_value],
        [pltpu.VMEM(half, bf16), pltpu.VMEM(half, bf16), pltpu.SemaphoreType.DMA((4,))],
    )


def xor_permute(shard, axis, mask):
    count = lax.axis_size(axis)
    return lax.ppermute(shard, axis, [(i, i ^ mask) for i in range(count)])


def small_ctx():
    return lax.axis_size("ctx") == 8


def ctx_order():
    count = lax.axis_size("ctx")
    slots = jnp.arange(count, dtype=jnp.int32)
    if small_ctx():
        return lax.axis_index("ctx") ^ slots
    return slots


def after(value, *earlier):
    return lax.optimization_barrier((value, earlier))[0]


def gather_ctx(shard, meanwhile):
    if not small_ctx():
        return [lax.all_gather(shard, "ctx", axis=0)]
    blocks = [None] * 8
    blocks[0] = shard
    for mask in (6, 4, 2):
        blocks[mask] = xor_permute(shard, "ctx", mask)
    blocks[1] = xor_permute(shard, "ctx", 1)
    for mask in (2, 4, 6):
        blocks[mask] = after(blocks[mask], meanwhile)
        blocks[mask + 1] = xor_permute(blocks[mask], "ctx", 1)
    return blocks


def add_low(*terms):
    total = terms[0].astype(f32)
    for term in terms[1:]:
        total = total + term.astype(f32)
    return lax.optimization_barrier(total.astype(bf16))


def xor_pairs(count, mask):
    return [(i, i ^ mask) for i in range(count)]


def scatter_stages(parts):
    y_swap = xor_pairs(8, 1)
    came = yield [(parts[mask + 1], "ctx", y_swap) for mask in (6, 4, 2, 0)]
    sums = [add_low(parts[mask], got) for mask, got in zip((6, 4, 2), came)]
    got = yield [(low, "ctx", xor_pairs(8, mask)) for low, mask in zip(sums, (6, 4, 2))]
    return list(got) + [parts[0], came[3]]


def sum_stages(make):
    send, keep = make()
    ctx_index = lax.axis_index("ctx")
    y_index = ctx_index & 1
    z_index = ctx_index >> 1
    half = send.shape[0] // 2
    y_swap = xor_pairs(8, 1)
    inward = [(z * 2 + y, t * 2 + y) for z, t in ((0, 1), (3, 2)) for y in (0, 1)]
    middle = [(z * 2 + y, t * 2 + y) for z, t in ((1, 2), (2, 1)) for y in (0, 1)]
    outward = [(z * 2 + y, t * 2 + y) for z, t in ((1, 0), (2, 3)) for y in (0, 1)]
    (core,) = yield [(send, "fsdp", [(0, 1), (1, 0)])]
    (came,) = yield [(add_low(keep[half:], core[half:]), "ctx", y_swap)]
    part = add_low(keep[:half], core[:half], came)
    (came,) = yield [(part, "ctx", inward)]
    part = add_low(part, came)
    (came,) = yield [(part, "ctx", middle)]
    part = add_low(part, came)
    (came,) = yield [(part, "ctx", outward)]
    total = jnp.where((z_index == 1) | (z_index == 2), part, came)
    (other,) = yield [(total, "ctx", y_swap)]
    first = jnp.where(y_index == 0, total, other)
    second = jnp.where(y_index == 0, other, total)
    return jnp.concatenate([first, second], axis=0).astype(f32)


def sum_plain(send, keep):
    half = send.shape[0] // 2
    y_index = lax.axis_index("ctx") & 1
    came = xor_permute(send, "fsdp", 1)
    both = add_low(keep, came)
    first = jnp.where(y_index == 0, both[:half], both[half:])
    second = jnp.where(y_index == 0, both[half:], both[:half])
    return lax.psum(jnp.concatenate([first, second], axis=0).astype(f32), "ctx")


def run_staggered(sets):
    results = {}
    states = [dict(entries=list(one), active=[], turn=0, landed=None) for one in sets]
    turn = 0
    while any(st["active"] or st["turn"] < len(st["entries"]) for st in states):
        state = states[turn % len(states)]
        turn += 1
        going = []
        for (name, stage, _), landed in zip(state["active"], state["landed"] or []):
            try:
                going.append((name, stage, stage.send(landed)))
            except StopIteration as end:
                results[name] = end.value
        if state["turn"] < len(state["entries"]):
            for name, make_stage in state["entries"][state["turn"]]:
                stage = make_stage(results)
                going.append((name, stage, next(stage)))
        state["turn"] += 1
        state["active"] = going
        state["landed"] = None
        if not going:
            continue
        operands = [[move[0] for move in moves] for _, _, moves in going]
        for other in states:
            if other is not state and other["landed"] is not None:
                other["landed"] = after(other["landed"], operands)
        state["landed"] = [
            [lax.ppermute(value, axis, pairs) for value, axis, pairs in moves]
            for _, _, moves in going
        ]
    return results


def run_alone(stage):
    moves = next(stage)
    while True:
        try:
            moves = stage.send([lax.ppermute(value, axis, pairs) for value, axis, pairs in moves])
        except StopIteration as end:
            return end.value


def on_device(
    inputs,
    out_cotangent,
    block_order,
    w_query,
    w_key,
    w_value,
    w_output,
    w_gate,
    w_up,
    w_down,
    g_input,
    g_query,
    g_key,
    g_post_attn,
    g_pre_ffw,
    g_post_ffw,
):
    section_index = lax.axis_index("section")
    fsdp_index = lax.axis_index("fsdp")
    ctx_index = lax.axis_index("ctx")
    ctx_size = lax.axis_size("ctx")
    micro_count, seq_local, tokens, model_width = inputs.shape
    head_dim = 2 * g_query.shape[1]
    sz = Sizes(
        micro_count * seq_local,
        tokens,
        model_width,
        w_query.shape[2] // head_dim,
        head_dim,
        w_gate.shape[2],
        ctx_size,
    )
    block_len = tokens // 2
    gains_own = jnp.concatenate([g_input, g_post_attn, g_pre_ffw, g_post_ffw, g_query, g_key], 1)
    gains = (gains_own, xor_permute(gains_own, "fsdp", 1))
    weights = {}
    for name, own in (
        ("key", w_key),
        ("value", w_value),
        ("query", w_query),
        ("out", w_output),
        ("gate", w_gate),
        ("up", w_up),
        ("down", w_down),
    ):
        weights[name] = (own[0], xor_permute(own[0], "fsdp", 1))
    slot_pairs = block_order.reshape(ctx_size, 2)
    offsets = jnp.arange(block_len, dtype=jnp.int32)

    def spread(slot_ids):
        return (slot_ids.reshape(-1)[:, None] * block_len + offsets[None, :]).reshape(-1)

    local_pos = spread(slot_pairs[ctx_index])
    key_pos = spread(slot_pairs[ctx_order()])
    tables = rotation_tables(local_pos, head_dim // 2)
    query_pos = jnp.tile(local_pos, sz.heads)
    places = {
        "key_row": key_pos.reshape(1, -1),
        "key_col": key_pos.reshape(-1, 1),
        "query_row": query_pos.reshape(1, -1),
        "query_col": query_pos.reshape(-1, 1),
    }
    block_shape = (sz.groups, tokens, 2 * head_dim)

    def forward(hidden, save):
        normed, key_lin, kv_low = project_kv(
            sz, hidden, gains, tables, weights["key"], weights["value"]
        )
        query_lin, query_low = project_query(sz, normed, gains, tables, weights["query"])
        blocks = gather_ctx(kv_low.reshape(block_shape), query_low)
        got = forward_layer(sz, query_low, hidden, gains, places, blocks, weights, save)
        if not save:
            return got[0], None
        names = (
            "log_total", "attn_low", "branch", "middle", "pre_ffw", "gate", "up", "act", "down_out"
        )
        saved = dict(zip(names, got[1:]))
        saved["log_row"] = saved["log_total"].reshape(sz.groups, 1, sz.head_rows)
        saved.update(
            hidden=hidden, normed=normed, key_lin=key_lin, query_lin=query_lin,
            query_low=query_low, blocks=blocks,
        )
        return got[0], saved

    def input_part(terms, middle_grad, query_part, saved):
        return input_back(
            sz, terms, saved["key_lin"], saved["hidden"], query_part, middle_grad, gains, tables,
            weights["key"], weights["value"],
        )

    def queries_back(query_grad, saved):
        return query_back(
            sz, query_grad, saved["query_lin"], gains, tables, weights["query"]
        )

    def scatter_plain(parts):
        return [lax.psum_scatter(parts[0].astype(f32), "ctx", scatter_dimension=0, tiled=False)]

    own_input = inputs.reshape(sz.rows, model_width)
    first_result, _ = forward(own_input, False)
    received = lax.ppermute(first_result, "section", [(0, 1)])
    hidden = jnp.where(section_index == 0, own_input, received)
    result, saved = forward(hidden, True)

    own_grad = out_cotangent.reshape(sz.rows, model_width)
    got = ffw_back(sz, own_grad, gains, saved, weights)
    query_grad, parts = attn_back(sz, got[8], saved, places)
    _, query_part, _ = queries_back(query_grad, saved)
    terms = run_alone(scatter_stages(parts)) if small_ctx() else scatter_plain(parts)
    first_grad = input_part(terms, got[0], query_part, saved)[0]
    grad_received = lax.ppermute(first_grad, "section", [(1, 0)])
    grad_in = jnp.where(section_index == 1, own_grad, grad_received)

    got = ffw_back(sz, grad_in, gains, saved, weights)
    middle_grad, down_low, gate_low, up_low, branch_low, gain_post, gain_pre, gain_attn = got[:8]
    down_terms = weight_terms(sz, saved["act"], down_low, 1)
    gate_terms = weight_terms(sz, saved["pre_ffw"], gate_low, 2)
    up_terms = weight_terms(sz, saved["pre_ffw"], up_low, 2)
    out_terms = weight_terms(sz, saved["attn_low"], branch_low, 1)
    query_grad, parts = attn_back(sz, got[8], saved, places)
    query_lin_low, query_part, gain_query = queries_back(query_grad, saved)
    query_terms = weight_terms(sz, saved["normed"], query_lin_low, 1)
    half_down = down_terms[0][0].shape[0] // 2
    cut = half_down // 2

    def down_piece(index):
        rows = [slice(first + index * cut, first + (index + 1) * cut) for first in (0, half_down)]
        return tuple(
            jnp.concatenate([term[rows[0]], term[rows[1]]], axis=0) for term in down_terms[0]
        )

    ends = {}
    kv_width = 2 * head_dim
    gain_count = gains_own.shape[1] // kv_width
    half_model = model_width // 2

    def tail_terms(terms):
        input_grad, kv_grad, gain_input, gain_key = input_part(
            terms, middle_grad, query_part, saved
        )
        ends["input_grad"] = input_grad
        send, keep = weight_terms(sz, saved["normed"], kv_grad, 1)[0]
        gain_grads = (gain_input, gain_attn, gain_pre, gain_post, gain_query, gain_key)
        gain_rows = jnp.concatenate([grad.reshape(2, -1) for grad in gain_grads], axis=1)
        gain_rows = gain_rows.reshape(2, gain_count, kv_width).astype(bf16)
        gain_rows = jnp.pad(gain_rows, ((0, 0), (0, 16 - gain_count), (0, 0)))
        zeros = jnp.zeros_like(gain_rows[0])
        is_lower = (ctx_index & 1) == 0
        pairs = []
        for term, owner in ((send, 1 - fsdp_index), (keep, fsdp_index)):
            here = lax.dynamic_index_in_dim(gain_rows, owner, 0, keepdims=False)
            half = term.shape[0] // 2
            pairs.append(
                jnp.concatenate(
                    [
                        term[:half],
                        jnp.where(is_lower, here, zeros),
                        term[half:],
                        jnp.where(is_lower, zeros, here),
                    ],
                    axis=0,
                )
            )
        return tuple(pairs)

    if small_ctx():

        def chunk(make):
            return lambda results: sum_stages(make)

        sets = [
            [
                [("down0", chunk(lambda: down_piece(0)))],
                [("gate0", chunk(lambda: gate_terms[0]))],
                [("up0", chunk(lambda: up_terms[0])), ("kv", lambda results: scatter_stages(parts))],
                [("out", chunk(lambda: out_terms[0]))],
                [],
                [("tail", lambda results: sum_stages(lambda: tail_terms(results["kv"])))],
            ],
            [
                [("down1", chunk(lambda: down_piece(1)))],
                [("gate1", chunk(lambda: gate_terms[1]))],
                [("up1", chunk(lambda: up_terms[1]))],
                [("query", chunk(lambda: query_terms[0]))],
            ],
        ]
        sums = run_staggered(sets)
    else:
        sums = {}
        for index in range(2):
            sums["down%d" % index] = sum_plain(*down_piece(index))
            sums["gate%d" % index] = sum_plain(*gate_terms[index])
            sums["up%d" % index] = sum_plain(*up_terms[index])
        sums["out"] = sum_plain(*out_terms[0])
        sums["query"] = sum_plain(*query_terms[0])
        sums["tail"] = sum_plain(*tail_terms(scatter_plain(parts)))
    input_grad = ends["input_grad"]
    sum_down = jnp.concatenate(
        [
            sums["down0"][:cut], sums["down1"][:cut], sums["down0"][cut:], sums["down1"][cut:],
        ],
        axis=0,
    )
    sum_gate = jnp.concatenate([sums["gate0"], sums["gate1"]], axis=1)
    sum_up = jnp.concatenate([sums["up0"], sums["up1"]], axis=1)
    sum_out = sums["out"]
    sum_query = sums["query"]
    sum_tail = sums["tail"]
    quarter = half_model // 2
    sum_kv = jnp.concatenate(
        [sum_tail[:quarter], sum_tail[quarter + 16 : quarter + 16 + quarter]], axis=0
    )
    sum_key = sum_kv[:, :head_dim]
    sum_value = sum_kv[:, head_dim:]
    sum_gains = sum_tail[quarter : quarter + gain_count].reshape(-1)
    gain_sums = {}
    for name, (start, width) in sz.gain_at.items():
        gain_sums[name] = sum_gains[start : start + width]
    shape = (micro_count, seq_local, tokens, model_width)
    members = (
        sum_query,
        sum_key,
        sum_value,
        sum_out,
        sum_gate,
        sum_up,
        sum_down,
        gain_sums["input"],
        gain_sums["query"],
        gain_sums["key"],
        gain_sums["attn"],
        gain_sums["pre"],
        gain_sums["post"],
    )
    return (result.reshape(shape)[None], input_grad.reshape(shape)[None]) + tuple(
        member[None] for member in members
    )


def solution(mesh):
    weight = P("section", "fsdp", None)
    gain = P("section", "fsdp")
    in_specs = (P(None, "fsdp", "ctx", None),) * 2 + (P(),) + (weight,) * 7 + (gain,) * 6
    out_specs = (
        (P("section", None, "fsdp", "ctx", None),) * 2 + (weight,) * 7 + (gain,) * 6
    )
    return jax.shard_map(
        on_device, mesh=mesh, in_specs=in_specs, out_specs=out_specs, check_vma=False
    )
```

```python
import functools

import jax
import jax.numpy as jnp
from jax import lax
from jax.experimental import pallas as pl
from jax.experimental.pallas import tpu as pltpu
from jax.sharding import PartitionSpec as P

epsilon = 1e-06
rope_base = 1000000.0
masked = -1e30
score_scale = 0.0625
gelu_slope = 0.7978845608028654
gelu_cubic = 0.044715
f32 = jnp.float32
bf16 = jnp.bfloat16
vmem_bytes = 56 * 1024 * 1024


def dot_nn(left, right):
    return jnp.dot(left, right, preferred_element_type=f32)


def dot_nt(left, right):
    return lax.dot_general(left, right, (((1,), (1,)), ((), ())), preferred_element_type=f32)


def dot_tn(left, right):
    return lax.dot_general(left, right, (((0,), (0,)), ((), ())), preferred_element_type=f32)


def norm_factor(values_in):
    return lax.rsqrt(jnp.mean(values_in * values_in, axis=-1, keepdims=True) + epsilon)


def norm_apply(values_in, gain_vec):
    return values_in * norm_factor(values_in) * gain_vec


def norm_back(values_in, gain_vec, grad_out):
    factor = norm_factor(values_in)
    scaled = grad_out * gain_vec
    grad_in = factor * (
        scaled - values_in * factor * factor * jnp.mean(scaled * values_in, axis=-1, keepdims=True)
    )
    grad_gain = jnp.sum(grad_out * values_in * factor, axis=0, keepdims=True)
    return (grad_in, grad_gain)


def rotate(values_in, cos_table, sin_table):
    half_width = values_in.shape[-1] // 2
    former = values_in[..., :half_width]
    latter = values_in[..., half_width:]
    return jnp.concatenate(
        [former * cos_table - latter * sin_table, latter * cos_table + former * sin_table], axis=-1
    )


def rotation_tables(positions, half_width):
    frequency = rope_base ** (-jnp.arange(half_width, dtype=f32) / half_width)
    angles = positions.astype(f32)[:, None] * frequency[None, :]
    return (jnp.cos(angles), jnp.sin(angles))


def call_kernel(body, out_shapes, inputs, far_inputs, scratch, mega_macs=0):
    moved = 0
    for array in [*inputs, *far_inputs, *out_shapes]:
        moved += array.size * jnp.dtype(array.dtype).itemsize
    whole = pl.BlockSpec(memory_space=pltpu.VMEM)
    far = pl.BlockSpec(memory_space=pl.ANY)
    return pl.pallas_call(
        body,
        out_shape=out_shapes,
        in_specs=[whole] * len(inputs) + [far] * len(far_inputs),
        out_specs=jax.tree.map(lambda _: whole, out_shapes),
        scratch_shapes=scratch,
        compiler_params=pltpu.CompilerParams(vmem_limit_bytes=vmem_bytes),
        cost_estimate=pl.CostEstimate(
            flops=2 * mega_macs * 10**6, bytes_accessed=moved * 3, transcendentals=0
        ),
    )(*inputs, *far_inputs)


def struct(shape, dtype):
    return jax.ShapeDtypeStruct(shape, dtype)


def start_halves(own, other, target, sems, first_sem):
    half = own.shape[0]
    fsdp_index = lax.axis_index("fsdp")
    copies = [
        pltpu.make_async_copy(
            own, target.at[pl.ds(fsdp_index * half, half)], sems.at[first_sem]
        ),
        pltpu.make_async_copy(
            other, target.at[pl.ds((1 - fsdp_index) * half, half)], sems.at[first_sem + 1]
        ),
    ]
    for copy in copies:
        copy.start()
    return copies


def wait_all(copies):
    for copy in copies:
        copy.wait()


def whole_gain(own_ref, other_ref, start, width):
    own = own_ref[:, start : start + width].astype(f32)
    other = other_ref[:, start : start + width].astype(f32)
    is_first = lax.axis_index("fsdp") == 0
    return jnp.concatenate(
        [jnp.where(is_first, own, other), jnp.where(is_first, other, own)], axis=1
    )


class Sizes:
    def __init__(self, groups, tokens, model, heads, head_dim, ff, blocks):
        self.groups, self.tokens, self.model = groups, tokens, model
        self.heads, self.head_dim, self.ff, self.blocks = heads, head_dim, ff, blocks
        self.rows = groups * tokens
        self.query_cols = heads * head_dim
        self.head_rows = heads * tokens
        self.keys = blocks * tokens
        self.span = tokens * min(8, blocks)
        self.chunk = min(256, self.head_rows)
        half = model // 2
        self.gain_at = {
            "input": (0, half),
            "attn": (half, half),
            "pre": (2 * half, half),
            "post": (3 * half, half),
            "query": (4 * half, head_dim // 2),
            "key": (4 * half + head_dim // 2, head_dim // 2),
        }


def kv_kernel(
    sz, hidden, gain_own, gain_other, cos_ref, sin_ref, k_own, k_other, v_own, v_other,
    normed, key_lin, kv_low, wk, wv, sems,
):
    k_copies = start_halves(k_own, k_other, wk, sems, 0)
    v_copies = start_halves(v_own, v_other, wv, sems, 2)
    gain_input = whole_gain(gain_own, gain_other, *sz.gain_at["input"])
    gain_key = whole_gain(gain_own, gain_other, *sz.gain_at["key"])
    low = norm_apply(hidden[...].astype(f32), gain_input).astype(bf16)
    normed[...] = low
    wait_all(k_copies)
    lin = dot_nn(low, wk[...])
    key_lin[...] = lin
    cos = jnp.concatenate([cos_ref[...]] * sz.groups, axis=0)
    sin = jnp.concatenate([sin_ref[...]] * sz.groups, axis=0)
    kv_low[:, : sz.head_dim] = rotate(norm_apply(lin, gain_key), cos, sin).astype(bf16)
    wait_all(v_copies)
    kv_low[:, sz.head_dim :] = dot_nn(low, wv[...]).astype(bf16)


def project_kv(sz, hidden, gains, tables, w_key, w_value):
    half = (sz.model, sz.head_dim)
    return call_kernel(
        functools.partial(kv_kernel, sz),
        [
            struct((sz.rows, sz.model), bf16),
            struct((sz.rows, sz.head_dim), f32),
            struct((sz.rows, 2 * sz.head_dim), bf16),
        ],
        [hidden, *gains, *tables],
        [*w_key, *w_value],
        [pltpu.VMEM(half, bf16), pltpu.VMEM(half, bf16), pltpu.SemaphoreType.DMA((4,))],
    )


def query_kernel(
    sz, normed, gain_own, gain_other, cos_ref, sin_ref, q_own, q_other,
    query_lin, query_low, wq, sems,
):
    copies = start_halves(q_own, q_other, wq, sems, 0)
    gain_query = whole_gain(gain_own, gain_other, *sz.gain_at["query"])
    cos = jnp.concatenate([cos_ref[...]] * sz.groups, axis=0)
    sin = jnp.concatenate([sin_ref[...]] * sz.groups, axis=0)
    low = normed[...]
    wait_all(copies)
    for head in range(sz.heads):
        cols = slice(head * sz.head_dim, (head + 1) * sz.head_dim)
        lin = dot_nn(low, wq[:, cols])
        query_lin[:, cols] = lin
        turned = rotate(norm_apply(lin, gain_query), cos, sin)
        turned = (turned.astype(bf16).astype(f32) * score_scale).astype(bf16)
        for group in range(sz.groups):
            query_low[group, head * sz.tokens : (head + 1) * sz.tokens, :] = turned[
                group * sz.tokens : (group + 1) * sz.tokens
            ]


def project_query(sz, normed, gains, tables, w_query):
    return call_kernel(
        functools.partial(query_kernel, sz),
        [
            struct((sz.rows, sz.query_cols), f32),
            struct((sz.groups, sz.head_rows, sz.head_dim), bf16),
        ],
        [normed, *gains, *tables],
        [*w_query],
        [pltpu.VMEM((sz.model, sz.query_cols), bf16), pltpu.SemaphoreType.DMA((2,))],
    )


def start_blocks(sz, blocks, target, sems, first_sem):
    copies = []
    for index, block in enumerate(blocks):
        copies.append(
            pltpu.make_async_copy(
                block,
                target.at[:, pl.ds(index * sz.tokens, sz.tokens)],
                sems.at[first_sem + index],
            )
        )
    for copy in copies:
        copy.start()
    return copies


def load_group(sz, stacked, group, target, sems, first_sem):
    def one(index):
        return pltpu.make_async_copy(
            stacked.at[index, group],
            target.at[0, pl.ds(index * sz.tokens, sz.tokens)],
            sems.at[first_sem + index],
        )

    def start(index, carry):
        one(index).start()
        return carry

    def wait(index, carry):
        one(index).wait()
        return carry

    lax.fori_loop(0, sz.blocks, start, 0)
    lax.fori_loop(0, sz.blocks, wait, 0)


def forward_kernel(sz, block_count, save, *refs):
    query_low, hidden, gain_own, gain_other, key_row, query_col = refs[:6]
    refs = refs[6:]
    blocks, refs = refs[:block_count], refs[block_count:]
    out_pair, gate_pair, up_pair, down_pair = (refs[2 * i : 2 * i + 2] for i in range(4))
    refs = refs[8:]
    result, refs = refs[0], refs[1:]
    if save:
        log_total, attn_low, branch_ref, middle_ref, pre_ref, gate_ref, up_ref, act_ref, down_ref = (
            refs[:9]
        )
        refs = refs[9:]
    else:
        attn_low, act_ref = refs[:2]
        refs = refs[2:]
    kv, w_out, w_gate, w_up, w_down, sems = refs
    if block_count > 1:
        kv_copies = start_blocks(sz, blocks, kv, sems, 8)
    out_copies = start_halves(*out_pair, w_out, sems, 0)
    gate_copies = start_halves(*gate_pair, w_gate, sems, 2)
    up_copies = start_halves(*up_pair, w_up, sems, 4)
    down_copies = start_halves(*down_pair, w_down, sems, 6)
    gain_attn = whole_gain(gain_own, gain_other, *sz.gain_at["attn"])
    gain_pre = whole_gain(gain_own, gain_other, *sz.gain_at["pre"])
    gain_post = whole_gain(gain_own, gain_other, *sz.gain_at["post"])
    if block_count > 1:
        wait_all(kv_copies)
    spans = sz.keys // sz.span
    for group in range(sz.groups):
        slot = group if block_count > 1 else 0
        if block_count == 1:
            load_group(sz, blocks[0], group, kv, sems, 8)
        for first in range(0, sz.head_rows, sz.chunk):
            query = query_low[group, first : first + sz.chunk, :]
            query_pos = query_col[first : first + sz.chunk, :]

            def one_span(index, state):
                row_max, row_total, row_sum = state
                at = pl.ds(index * sz.span, sz.span)
                scores = dot_nt(query, kv[slot, at, : sz.head_dim])
                scores = jnp.where(key_row[:, at] <= query_pos, scores, masked)
                new_max = jnp.maximum(row_max, jnp.max(scores, axis=1, keepdims=True))
                probs = jnp.exp(scores - new_max)
                part = dot_nn(probs.astype(bf16), kv[slot, at, sz.head_dim :])
                shrink = jnp.exp(row_max - new_max)
                return (
                    new_max,
                    row_total * shrink + jnp.sum(probs, axis=1, keepdims=True),
                    row_sum * shrink + part,
                )

            state = (
                jnp.full((sz.chunk, 1), masked, f32),
                jnp.zeros((sz.chunk, 1), f32),
                jnp.zeros((sz.chunk, sz.head_dim), f32),
            )
            if spans == 1:
                state = one_span(0, state)
            else:
                state = lax.fori_loop(0, spans, one_span, state)
            row_max, row_total, row_sum = state
            attended = (row_sum / row_total).astype(bf16)
            if save:
                log_total[group, first : first + sz.chunk, :] = row_max + jnp.log(row_total)
            for part in range(sz.chunk // sz.tokens):
                head = first // sz.tokens + part
                attn_low[
                    group * sz.tokens : (group + 1) * sz.tokens,
                    head * sz.head_dim : (head + 1) * sz.head_dim,
                ] = attended[part * sz.tokens : (part + 1) * sz.tokens]
    wait_all(out_copies)
    branch = dot_nn(attn_low[...], w_out[...])
    middle = hidden[...].astype(f32) + norm_apply(branch, gain_attn)
    pre_ffw = norm_apply(middle, gain_pre).astype(bf16)
    if save:
        branch_ref[...] = branch
        middle_ref[...] = middle
        pre_ref[...] = pre_ffw
    wait_all(gate_copies)
    wait_all(up_copies)
    step = min(512, sz.ff)
    for first in range(0, sz.ff, step):
        cols = slice(first, first + step)
        gate = dot_nn(pre_ffw, w_gate[:, cols])
        up = dot_nn(pre_ffw, w_up[:, cols])
        if save:
            gate_ref[:, cols] = gate
            up_ref[:, cols] = up
        bend = jnp.tanh(gelu_slope * (gate + gelu_cubic * gate * gate * gate))
        act_ref[:, cols] = (0.5 * gate * (1.0 + bend) * up).astype(bf16)
    wait_all(down_copies)
    down_out = dot_nn(act_ref[...], w_down[...])
    if save:
        down_ref[...] = down_out
    result[...] = (middle + norm_apply(down_out, gain_post)).astype(bf16)


def forward_layer(sz, query_low, hidden, gains, places, blocks, weights, save):
    rows, model = sz.rows, sz.model
    outs = [struct((rows, model), bf16)]
    attn = (rows, sz.query_cols)
    act = (rows, sz.ff)
    scratch = []
    if save:
        outs += [
            struct((sz.groups, sz.head_rows, 1), f32),
            struct(attn, bf16),
            struct((rows, model), f32),
            struct((rows, model), f32),
            struct((rows, model), bf16),
            struct(act, f32),
            struct(act, f32),
            struct(act, bf16),
            struct((rows, model), f32),
        ]
    else:
        scratch += [pltpu.VMEM(attn, bf16), pltpu.VMEM(act, bf16)]
    scratch += [
        pltpu.VMEM((sz.groups if len(blocks) > 1 else 1, sz.keys, 2 * sz.head_dim), bf16),
        pltpu.VMEM((sz.query_cols, model), bf16),
        pltpu.VMEM((model, sz.ff), bf16),
        pltpu.VMEM((model, sz.ff), bf16),
        pltpu.VMEM((sz.ff, model), bf16),
        pltpu.SemaphoreType.DMA((8 + sz.blocks,)),
    ]
    far = [*blocks, *weights["out"], *weights["gate"], *weights["up"], *weights["down"]]
    return call_kernel(
        functools.partial(forward_kernel, sz, len(blocks), save),
        outs,
        [query_low, hidden, *gains, places["key_row"], places["query_col"]],
        far,
        scratch,
    )


def ffw_back_kernel(sz, *refs):
    grad_ref, gain_own, gain_other, down_out, gate_ref, up_ref, middle, branch = refs[:8]
    refs = refs[8:]
    out_pair, gate_pair, up_pair, down_pair = (refs[2 * i : 2 * i + 2] for i in range(4))
    refs = refs[8:]
    (
        middle_grad, down_grad, gate_grad, up_grad, branch_grad, gain_post_grad, gain_pre_grad,
        gain_attn_grad, attn_grad,
    ) = refs[:9]
    w_out, w_gate, w_up, w_down, sems = refs[9:]
    down_copies = start_halves(*down_pair, w_down, sems, 0)
    gate_copies = start_halves(*gate_pair, w_gate, sems, 2)
    up_copies = start_halves(*up_pair, w_up, sems, 4)
    out_copies = start_halves(*out_pair, w_out, sems, 6)
    gain_attn = whole_gain(gain_own, gain_other, *sz.gain_at["attn"])
    gain_pre = whole_gain(gain_own, gain_other, *sz.gain_at["pre"])
    gain_post = whole_gain(gain_own, gain_other, *sz.gain_at["post"])
    grad = grad_ref[...].astype(f32)
    down_part, gain_post_grad[...] = norm_back(down_out[...], gain_post, grad)
    down_low = down_part.astype(bf16)
    down_grad[...] = down_low
    wait_all(down_copies)
    wait_all(gate_copies)
    wait_all(up_copies)
    step = min(512, sz.ff)
    pre_grad = jnp.zeros((sz.rows, sz.model), f32)
    for first in range(0, sz.ff, step):
        cols = slice(first, first + step)
        ffw_grad = dot_nt(down_low, w_down[cols, :])
        gate = gate_ref[:, cols]
        up = up_ref[:, cols]
        square = gate * gate
        bend = jnp.tanh(gelu_slope * (gate + gelu_cubic * square * gate))
        half_open = 0.5 * (1.0 + bend)
        slope = half_open + 0.5 * gate * (1.0 - bend * bend) * gelu_slope * (
            1.0 + 3.0 * gelu_cubic * square
        )
        gate_low = (ffw_grad * up * slope).astype(bf16)
        up_low = (ffw_grad * gate * half_open).astype(bf16)
        gate_grad[:, cols] = gate_low
        up_grad[:, cols] = up_low
        pre_grad = pre_grad + dot_nt(gate_low, w_gate[:, cols]) + dot_nt(up_low, w_up[:, cols])
    middle_part, gain_pre_grad[...] = norm_back(middle[...], gain_pre, pre_grad)
    total = grad + middle_part
    middle_grad[...] = total
    branch_part, gain_attn_grad[...] = norm_back(branch[...], gain_attn, total)
    branch_low = branch_part.astype(bf16)
    branch_grad[...] = branch_low
    wait_all(out_copies)
    attn_grad[...] = dot_nt(branch_low, w_out[...]).astype(bf16)


def attn_back_kernel(sz, block_count, paired, *refs):
    attn_grad, query_low, log_row, key_col, query_row = refs[:5]
    refs = refs[5:]
    blocks, refs = refs[:block_count], refs[block_count:]
    query_grad, parts, refs = refs[0], refs[1:-4], refs[-4:]
    kv, key_sum, value_sum, sems = refs
    if block_count > 1:
        wait_all(start_blocks(sz, blocks, kv, sems, 0))
    spans = sz.keys // sz.span
    heads_in = sz.chunk // sz.tokens
    chunks = range(0, sz.head_rows, sz.chunk)

    def probs_of(slot, group, first, at):
        query = query_low[group, first : first + sz.chunk, :]
        query_pos = query_row[:, first : first + sz.chunk]
        log_here = log_row[group, :, first : first + sz.chunk]
        scores = dot_nt(kv[slot, at, : sz.head_dim], query)
        probs = jnp.exp(jnp.where(key_col[at, :] <= query_pos, scores - log_here, masked))
        grad_rows = jnp.concatenate(
            [
                attn_grad[
                    group * sz.tokens : (group + 1) * sz.tokens,
                    (first // sz.tokens + part) * sz.head_dim : (first // sz.tokens + part + 1)
                    * sz.head_dim,
                ]
                for part in range(heads_in)
            ],
            axis=0,
        )
        return probs, dot_nt(kv[slot, at, sz.head_dim :], grad_rows), query, grad_rows

    def finish(slot, first, at, got, delta):
        probs, prob_grad, query, grad_rows = got
        score_grad = (probs * (prob_grad - delta)).astype(bf16)
        key_part = dot_nn(score_grad, query)
        value_part = dot_nn(probs.astype(bf16), grad_rows)
        if first == 0:
            key_sum[...] = key_part
            value_sum[...] = value_part
        else:
            key_sum[...] += key_part
            value_sum[...] += value_part
        return dot_tn(score_grad, kv[slot, at, : sz.head_dim])

    for group in range(sz.groups):
        if block_count > 1:
            for first in chunks:
                at = slice(0, sz.span)
                got = probs_of(group, group, first, at)
                delta = jnp.sum(got[0] * got[1], axis=0, keepdims=True)
                query_grad[group, first : first + sz.chunk, :] = finish(
                    group, first, at, got, delta
                )
            for index in range(block_count):
                at = slice(index * sz.tokens, (index + 1) * sz.tokens)
                if paired:
                    target = parts[index // 2].at[index % 2, group]
                else:
                    target = parts[index].at[group]
                target[:, : sz.head_dim] = key_sum[at, :].astype(bf16)
                target[:, sz.head_dim :] = value_sum[at, :].astype(bf16)
            continue
        load_group(sz, blocks[0], group, kv, sems, 0)
        deltas = []
        for first in chunks:

            def add_delta(index, delta, first=first):
                got = probs_of(0, group, first, pl.ds(index * sz.span, sz.span))
                return delta + jnp.sum(got[0] * got[1], axis=0, keepdims=True)

            deltas.append(lax.fori_loop(0, spans, add_delta, jnp.zeros((1, sz.chunk), f32)))
            query_grad[group, first : first + sz.chunk, :] = jnp.zeros(
                (sz.chunk, sz.head_dim), f32
            )

        def add_span(index, carry):
            at = pl.ds(index * sz.span, sz.span)
            for first, delta in zip(chunks, deltas):
                query_grad[group, first : first + sz.chunk, :] += finish(
                    0, first, at, probs_of(0, group, first, at), delta
                )
            per_span = sz.span // sz.tokens
            for step in range(per_span):
                rows = slice(step * sz.tokens, (step + 1) * sz.tokens)
                target = parts[0].at[index * per_span + step, group]
                target[:, : sz.head_dim] = key_sum[rows, :].astype(bf16)
                target[:, sz.head_dim :] = value_sum[rows, :].astype(bf16)
            return carry

        lax.fori_loop(0, spans, add_span, 0)


def ffw_back(sz, grad, gains, saved, weights):
    rows, model = sz.rows, sz.model
    gain = struct((1, model), f32)
    outs = [
        struct((rows, model), f32),
        struct((rows, model), bf16),
        struct((rows, sz.ff), bf16),
        struct((rows, sz.ff), bf16),
        struct((rows, model), bf16),
        gain,
        gain,
        gain,
        struct((rows, sz.query_cols), bf16),
    ]
    scratch = [
        pltpu.VMEM((sz.query_cols, model), bf16),
        pltpu.VMEM((model, sz.ff), bf16),
        pltpu.VMEM((model, sz.ff), bf16),
        pltpu.VMEM((sz.ff, model), bf16),
        pltpu.SemaphoreType.DMA((8,)),
    ]
    inputs = [
        grad, *gains, saved["down_out"], saved["gate"], saved["up"], saved["middle"],
        saved["branch"],
    ]
    far = [*weights["out"], *weights["gate"], *weights["up"], *weights["down"]]
    return call_kernel(functools.partial(ffw_back_kernel, sz), outs, inputs, far, scratch)


def attn_back(sz, attn_grad, saved, places, paired):
    blocks = saved["blocks"]
    outs = [struct((sz.groups, sz.head_rows, sz.head_dim), f32)]
    if paired and len(blocks) > 1:
        outs += [struct((2,) + block.shape, bf16) for block in blocks[::2]]
    else:
        outs += [struct(block.shape, bf16) for block in blocks]
    scratch = [
        pltpu.VMEM((sz.groups if len(blocks) > 1 else 1, sz.keys, 2 * sz.head_dim), bf16),
        pltpu.VMEM((sz.span, sz.head_dim), f32),
        pltpu.VMEM((sz.span, sz.head_dim), f32),
        pltpu.SemaphoreType.DMA((sz.blocks,)),
    ]
    inputs = [
        attn_grad, saved["query_low"], saved["log_row"], places["key_col"], places["query_row"]
    ]
    got = call_kernel(
        functools.partial(attn_back_kernel, sz, len(blocks), paired), outs, inputs, blocks, scratch
    )
    return got[0], got[1:]


gain_names = ("input", "attn", "pre", "post", "query", "key")
gain_pad = 16


def weight_kernel(sz, cuts, gain_count, left, right, *refs):
    gains, refs = refs[:gain_count], refs[gain_count:]
    outs, turned = refs[:-1], refs[-1]
    turned[...] = left[...].T
    half = left.shape[1] // 2
    fsdp_index = lax.axis_index("fsdp")
    y_index = lax.axis_index("ctx") & 1
    for side, owner in ((0, 1 - fsdp_index), (1, fsdp_index)):
        for part, y_half in ((0, y_index), (1, 1 - y_index)):
            base = owner * half + y_half * (half // 2)
            for index, (first_row, count, first_col, cols) in enumerate(cuts):
                out = outs[2 * index + side]
                rows = turned[pl.ds(pl.multiple_of(base + first_row, 16), count), :]
                first_out = part * (out.shape[0] // 2)
                out[first_out : first_out + count, :] = dot_nn(
                    rows, right[:, first_col : first_col + cols]
                ).astype(bf16)
                if gain_count:
                    out[first_out + count : first_out + count + gain_pad, :] = gain_rows(
                        sz, gains, owner, y_half, cols
                    )


def gain_rows(sz, gains, owner, y_half, cols):
    halves = []
    for gain in gains:
        half = gain.shape[1] // 2
        halves.append(jnp.where(owner == 0, gain[:, :half], gain[:, half:]))
    flat = jnp.where(y_half == 0, jnp.concatenate(halves, axis=1), 0.0)
    rows = [flat[:, first : first + cols] for first in range(0, flat.shape[1], cols)]
    rows.append(jnp.zeros((gain_pad - len(rows), cols), f32))
    return jnp.concatenate(rows, axis=0).astype(bf16)


def tail_kernel(sz, count, mine, other, key, value, *gains):
    y_index = lax.axis_index("ctx") & 1
    for source, y_half in ((mine, y_index), (other, 1 - y_index)):
        rows = pl.ds(pl.multiple_of(y_half * count, 16), count)
        key[rows, :] = source[:count, : sz.head_dim].astype(f32)
        value[rows, :] = source[:count, sz.head_dim :].astype(f32)
    row_count = sum(gain.shape[1] for gain in gains) // mine.shape[1]
    here = mine[count : count + gain_pad, :].astype(f32)
    there = other[count : count + gain_pad, :].astype(f32)
    lower = jnp.where(y_index == 0, here, there)
    flat = jnp.concatenate([lower[row : row + 1, :] for row in range(row_count)], axis=1)
    start = 0
    for gain in gains:
        gain[...] = flat[:, start : start + gain.shape[1]]
        start += gain.shape[1]


def finish_tail(sz, mine, other):
    half = sz.model // 2
    outs = [struct((half, sz.head_dim), f32)] * 2
    outs += [struct((1, sz.gain_at[name][1]), f32) for name in gain_names]
    return call_kernel(
        functools.partial(tail_kernel, sz, half // 2), outs, [mine, other], [], []
    )


def weight_terms(sz, left, right, cuts, gains=()):
    outs = []
    for _, count, _, cols in cuts:
        outs += [struct((2 * (count + (gain_pad if gains else 0)), cols), bf16)] * 2
    got = call_kernel(
        functools.partial(weight_kernel, sz, cuts, len(gains)),
        outs,
        [left, right, *gains],
        [],
        [pltpu.VMEM((left.shape[1], left.shape[0]), bf16)],
    )
    return [(got[2 * index], got[2 * index + 1]) for index in range(len(cuts))]


def query_back_kernel(
    sz, query_grad, query_lin, gain_own, gain_other, cos_ref, sin_ref, q_own, q_other,
    lin_grad, normed_grad, gain_grad, wq, sems,
):
    copies = start_halves(q_own, q_other, wq, sems, 0)
    gain_query = whole_gain(gain_own, gain_other, *sz.gain_at["query"])
    cos = jnp.concatenate([cos_ref[...]] * sz.groups, axis=0)
    sin = jnp.concatenate([sin_ref[...]] * sz.groups, axis=0)
    gain_sum = jnp.zeros((1, sz.head_dim), f32)
    for head in range(sz.heads):
        cols = slice(head * sz.head_dim, (head + 1) * sz.head_dim)
        rows = slice(head * sz.tokens, (head + 1) * sz.tokens)
        grad = jnp.concatenate([query_grad[g, rows, :] for g in range(sz.groups)], axis=0)
        turned = rotate(grad * score_scale, cos, -sin)
        part, gain_part = norm_back(query_lin[:, cols], gain_query, turned)
        lin_grad[:, cols] = part.astype(bf16)
        gain_sum = gain_sum + gain_part
    gain_grad[...] = gain_sum
    wait_all(copies)
    normed_grad[...] = dot_nt(lin_grad[...], wq[...])


def query_back(sz, query_grad, query_lin, gains, tables, w_query):
    return call_kernel(
        functools.partial(query_back_kernel, sz),
        [
            struct((sz.rows, sz.query_cols), bf16),
            struct((sz.rows, sz.model), f32),
            struct((1, sz.head_dim), f32),
        ],
        [query_grad, query_lin, *gains, *tables],
        [*w_query],
        [pltpu.VMEM((sz.model, sz.query_cols), bf16), pltpu.SemaphoreType.DMA((2,))],
    )


def input_back_kernel(sz, term_count, *refs):
    terms, refs = refs[:term_count], refs[term_count:]
    (
        key_lin, hidden, query_part, middle_grad, gain_own, gain_other, cos_ref, sin_ref,
        k_own, k_other, v_own, v_other, input_grad, kv_grad, gain_input_grad, gain_key_grad,
        wk, wv, sems,
    ) = refs
    k_copies = start_halves(k_own, k_other, wk, sems, 0)
    v_copies = start_halves(v_own, v_other, wv, sems, 2)
    gain_input = whole_gain(gain_own, gain_other, *sz.gain_at["input"])
    gain_key = whole_gain(gain_own, gain_other, *sz.gain_at["key"])
    cos = jnp.concatenate([cos_ref[...]] * sz.groups, axis=0)
    sin = jnp.concatenate([sin_ref[...]] * sz.groups, axis=0)
    total = terms[0][...].astype(f32)
    for term in terms[1:]:
        total = total + term[...].astype(f32)
    turned = rotate(total[:, : sz.head_dim], cos, -sin)
    key_part, gain_key_grad[...] = norm_back(key_lin[...], gain_key, turned)
    key_low = key_part.astype(bf16)
    value_low = total[:, sz.head_dim :].astype(bf16)
    kv_grad[:, : sz.head_dim] = key_low
    kv_grad[:, sz.head_dim :] = value_low
    wait_all(k_copies)
    wait_all(v_copies)
    normed_grad = query_part[...] + dot_nt(key_low, wk[...]) + dot_nt(value_low, wv[...])
    part, gain_input_grad[...] = norm_back(hidden[...].astype(f32), gain_input, normed_grad)
    input_grad[...] = (middle_grad[...] + part).astype(bf16)


def input_back(sz, terms, key_lin, hidden, query_part, middle_grad, gains, tables, w_key, w_value):
    half = (sz.model, sz.head_dim)
    flat = [term.reshape(sz.rows, 2 * sz.head_dim) for term in terms]
    return call_kernel(
        functools.partial(input_back_kernel, sz, len(flat)),
        [
            struct((sz.rows, sz.model), bf16),
            struct((sz.rows, 2 * sz.head_dim), bf16),
            struct((1, sz.model), f32),
            struct((1, sz.head_dim), f32),
        ],
        [*flat, key_lin, hidden, query_part, middle_grad, *gains, *tables],
        [*w_key, *w_value],
        [pltpu.VMEM(half, bf16), pltpu.VMEM(half, bf16), pltpu.SemaphoreType.DMA((4,))],
    )


def xor_permute(shard, axis, mask):
    count = lax.axis_size(axis)
    return lax.ppermute(shard, axis, [(i, i ^ mask) for i in range(count)])


def small_ctx():
    return lax.axis_size("ctx") == 8


def ctx_order():
    count = lax.axis_size("ctx")
    slots = jnp.arange(count, dtype=jnp.int32)
    if small_ctx():
        return lax.axis_index("ctx") ^ slots
    return slots


def after(value, *earlier):
    return lax.optimization_barrier((value, earlier))[0]


def gather_ctx(shard, meanwhile):
    if not small_ctx():
        return [lax.all_gather(shard, "ctx", axis=0)]
    blocks = [None] * 8
    blocks[0] = shard
    for mask in (6, 4, 2):
        blocks[mask] = xor_permute(shard, "ctx", mask)
    blocks[1] = xor_permute(shard, "ctx", 1)
    for mask in (2, 4, 6):
        blocks[mask] = after(blocks[mask], meanwhile)
        blocks[mask + 1] = xor_permute(blocks[mask], "ctx", 1)
    return blocks


def add_low(*terms):
    total = terms[0].astype(f32)
    for term in terms[1:]:
        total = total + term.astype(f32)
    return lax.optimization_barrier(total.astype(bf16))


def xor_pairs(count, mask):
    return [(i, i ^ mask) for i in range(count)]


def scatter_stages(parts):
    y_swap = xor_pairs(8, 1)
    came = yield [(parts[mask + 1], "ctx", y_swap) for mask in (6, 4, 2, 0)]
    sums = [add_low(parts[mask], got) for mask, got in zip((6, 4, 2), came)]
    got = yield [(low, "ctx", xor_pairs(8, mask)) for low, mask in zip(sums, (6, 4, 2))]
    return list(got) + [parts[0], came[3]]


def scatter_pairs(pairs):
    came = yield [(pairs[mask // 2], "ctx", xor_pairs(8, mask)) for mask in (6, 4, 2)]
    total = pairs[0].astype(f32)
    for term in came:
        total = total + term.astype(f32)
    other = lax.optimization_barrier(total[1].astype(bf16))
    own = lax.optimization_barrier(total[0])
    (got,) = yield [(other, "ctx", xor_pairs(8, 1))]
    return [own, got]


def sum_stages(make):
    send, keep = make()
    ctx_index = lax.axis_index("ctx")
    y_index = ctx_index & 1
    z_index = ctx_index >> 1
    half = send.shape[0] // 2
    y_swap = xor_pairs(8, 1)
    inward = [(z * 2 + y, t * 2 + y) for z, t in ((0, 1), (3, 2)) for y in (0, 1)]
    middle = [(z * 2 + y, t * 2 + y) for z, t in ((1, 2), (2, 1)) for y in (0, 1)]
    outward = [(z * 2 + y, t * 2 + y) for z, t in ((1, 0), (2, 3)) for y in (0, 1)]
    (core,) = yield [(send, "fsdp", [(0, 1), (1, 0)])]
    (came,) = yield [(add_low(keep[half:], core[half:]), "ctx", y_swap)]
    part = add_low(keep[:half], core[:half], came)
    (came,) = yield [(part, "ctx", inward)]
    part = add_low(part, came)
    (came,) = yield [(part, "ctx", middle)]
    part = add_low(part, came)
    (came,) = yield [(part, "ctx", outward)]
    total = jnp.where((z_index == 1) | (z_index == 2), part, came)
    (other,) = yield [(total, "ctx", y_swap)]
    return (total, other)


def join_halves(mine, other):
    y_index = lax.axis_index("ctx") & 1
    first = jnp.where(y_index == 0, mine, other)
    second = jnp.where(y_index == 0, other, mine)
    return jnp.concatenate([first, second], axis=0).astype(f32)


def sum_plain(send, keep):
    half = send.shape[0] // 2
    y_index = lax.axis_index("ctx") & 1
    came = xor_permute(send, "fsdp", 1)
    both = add_low(keep, came)
    first = jnp.where(y_index == 0, both[:half], both[half:])
    second = jnp.where(y_index == 0, both[half:], both[:half])
    whole = lax.psum(jnp.concatenate([first, second], axis=0).astype(f32), "ctx")
    first, second = whole[:half], whole[half:]
    return (jnp.where(y_index == 0, first, second), jnp.where(y_index == 0, second, first))


def run_turns(sets, turns, held):
    results = {}
    states = {
        name: dict(entries=list(one), active=[], turn=0, landed=None)
        for name, one in sets.items()
    }
    latest = [None, ()]

    def alive(state):
        return state["active"] or state["turn"] < len(state["entries"])

    def step(state):
        going = []
        for (name, stage, _), landed in zip(state["active"], state["landed"] or []):
            try:
                going.append((name, stage, stage.send(landed)))
            except StopIteration as end:
                results[name] = end.value
        if state["turn"] < len(state["entries"]):
            for name, make_stage in state["entries"][state["turn"]]:
                stage = make_stage()
                going.append((name, stage, next(stage)))
        state["turn"] += 1
        state["active"] = going
        state["landed"] = None
        if not going:
            return
        operands = [[move[0] for move in moves] for _, _, moves in going]
        for other in states.values():
            if other is not state and other["landed"] is not None:
                other["landed"] = after(other["landed"], operands)
        state["landed"] = [
            [lax.ppermute(value, axis, pairs) for value, axis, pairs in moves]
            for _, _, moves in going
        ]
        latest[:] = [state, operands]

    for turn in turns:
        if callable(turn):
            state, operands = latest
            got = turn(results, lambda value: after(value, operands))
            got, state["landed"] = lax.optimization_barrier((got, state["landed"]))
            held.update(got)
        else:
            step(states[turn])
    while any(alive(state) for state in states.values()):
        for state in states.values():
            if alive(state):
                step(state)
    return results


def run_alone(stage):
    moves = next(stage)
    while True:
        try:
            moves = stage.send([lax.ppermute(value, axis, pairs) for value, axis, pairs in moves])
        except StopIteration as end:
            return end.value


def on_device(
    inputs,
    out_cotangent,
    block_order,
    w_query,
    w_key,
    w_value,
    w_output,
    w_gate,
    w_up,
    w_down,
    g_input,
    g_query,
    g_key,
    g_post_attn,
    g_pre_ffw,
    g_post_ffw,
):
    section_index = lax.axis_index("section")
    fsdp_index = lax.axis_index("fsdp")
    ctx_index = lax.axis_index("ctx")
    ctx_size = lax.axis_size("ctx")
    micro_count, seq_local, tokens, model_width = inputs.shape
    head_dim = 2 * g_query.shape[1]
    sz = Sizes(
        micro_count * seq_local,
        tokens,
        model_width,
        w_query.shape[2] // head_dim,
        head_dim,
        w_gate.shape[2],
        ctx_size,
    )
    block_len = tokens // 2
    gains_own = jnp.concatenate([g_input, g_post_attn, g_pre_ffw, g_post_ffw, g_query, g_key], 1)
    gains = (gains_own, xor_permute(gains_own, "fsdp", 1))
    weights = {}
    for name, own in (
        ("key", w_key),
        ("value", w_value),
        ("query", w_query),
        ("out", w_output),
        ("gate", w_gate),
        ("up", w_up),
        ("down", w_down),
    ):
        weights[name] = (own[0], xor_permute(own[0], "fsdp", 1))
    slot_pairs = block_order.reshape(ctx_size, 2)
    offsets = jnp.arange(block_len, dtype=jnp.int32)

    def spread(slot_ids):
        return (slot_ids.reshape(-1)[:, None] * block_len + offsets[None, :]).reshape(-1)

    local_pos = spread(slot_pairs[ctx_index])
    key_pos = spread(slot_pairs[ctx_order()])
    tables = rotation_tables(local_pos, head_dim // 2)
    query_pos = jnp.tile(local_pos, sz.heads)
    places = {
        "key_row": key_pos.reshape(1, -1),
        "key_col": key_pos.reshape(-1, 1),
        "query_row": query_pos.reshape(1, -1),
        "query_col": query_pos.reshape(-1, 1),
    }
    block_shape = (sz.groups, tokens, 2 * head_dim)

    def forward(hidden, save):
        normed, key_lin, kv_low = project_kv(
            sz, hidden, gains, tables, weights["key"], weights["value"]
        )
        query_lin, query_low = project_query(sz, normed, gains, tables, weights["query"])
        if not save:
            kv_low = after(kv_low, weights)
        blocks = gather_ctx(kv_low.reshape(block_shape), query_low)
        got = forward_layer(sz, query_low, hidden, gains, places, blocks, weights, save)
        if not save:
            return got[0], None
        names = (
            "log_total", "attn_low", "branch", "middle", "pre_ffw", "gate", "up", "act", "down_out"
        )
        saved = dict(zip(names, got[1:]))
        saved["log_row"] = saved["log_total"].reshape(sz.groups, 1, sz.head_rows)
        saved.update(
            hidden=hidden, normed=normed, key_lin=key_lin, query_lin=query_lin,
            query_low=query_low, blocks=blocks,
        )
        return got[0], saved

    def input_part(terms, middle_grad, query_part, saved):
        return input_back(
            sz, terms, saved["key_lin"], saved["hidden"], query_part, middle_grad, gains, tables,
            weights["key"], weights["value"],
        )

    def queries_back(query_grad, saved):
        return query_back(
            sz, query_grad, saved["query_lin"], gains, tables, weights["query"]
        )

    def scatter_plain(parts):
        return [lax.psum_scatter(parts[0].astype(f32), "ctx", scatter_dimension=0, tiled=False)]

    own_input = inputs.reshape(sz.rows, model_width)
    first_result, _ = forward(own_input, False)
    received = lax.ppermute(first_result, "section", [(0, 1)])
    hidden = jnp.where(section_index == 0, own_input, received)
    result, saved = forward(hidden, True)

    own_grad = out_cotangent.reshape(sz.rows, model_width)
    got = ffw_back(sz, own_grad, gains, saved, weights)
    query_grad, parts = attn_back(sz, got[8], saved, places, False)
    _, query_part, _ = queries_back(query_grad, saved)
    terms = run_alone(scatter_stages(parts)) if small_ctx() else scatter_plain(parts)
    first_grad = input_part(terms, got[0], query_part, saved)[0]
    grad_received = lax.ppermute(first_grad, "section", [(1, 0)])
    grad_in = jnp.where(section_index == 1, own_grad, grad_received)

    got = ffw_back(sz, grad_in, gains, saved, weights)
    middle_grad, down_low, gate_low, up_low, branch_low, gain_post, gain_pre, gain_attn = got[:8]
    model_quarter = model_width // 4
    kv_width = 2 * head_dim
    down_cuts = [(0, sz.ff // 4, 0, model_width)]
    wide_cuts = [(0, model_quarter, 0, sz.ff)]
    out_cuts = [(0, sz.query_cols // 4, 0, model_width)]
    query_cuts = [(0, model_quarter, 0, sz.query_cols)]
    kv_cuts = [(0, model_quarter, 0, kv_width)]
    at = {"down": weight_terms(sz, saved["act"], down_low, down_cuts)}

    def do_gate(results, later):
        return {"gate": weight_terms(sz, saved["pre_ffw"], later(gate_low), wide_cuts)}

    def do_up(results, later):
        return {"up": weight_terms(sz, saved["pre_ffw"], later(up_low), wide_cuts)}

    def do_attention(results, later):
        query_grad, parts = attn_back(sz, later(got[8]), saved, places, True)
        return {"query_grad": query_grad, "parts": parts}

    def do_queries(results, later):
        low, query_part, gain_query = queries_back(later(at["query_grad"]), saved)
        terms = weight_terms(sz, saved["normed"], low, query_cuts)
        return {"query": terms, "query_part": query_part, "gain_query": gain_query}

    def do_out(results, later):
        return {"out": weight_terms(sz, saved["attn_low"], later(branch_low), out_cuts)}

    def do_tail(results, later):
        terms = results["kv"] if small_ctx() else scatter_plain(at["parts"])
        input_grad, kv_grad, gain_input, gain_key = input_part(
            later(terms), middle_grad, at["query_part"], saved
        )
        gain_grads = (gain_input, gain_attn, gain_pre, gain_post, at["gain_query"], gain_key)
        terms = weight_terms(sz, saved["normed"], kv_grad, kv_cuts, gain_grads)
        return {"tail": terms, "input_grad": input_grad}

    if small_ctx():

        def chunk(name, index):
            return (name + str(index), lambda: sum_stages(lambda: at[name][index]))

        sets = {
            "a": [[chunk("down", 0)], [], [chunk("up", 0)], [], [], [chunk("tail", 0)]],
            "b": [[chunk("gate", 0)], [chunk("out", 0)], [chunk("query", 0)]],
            "kv": [[("kv", lambda: scatter_pairs(at["parts"]))]],
        }
        turns = (
            ["a", "a", do_gate, "b", do_up, do_out, "b", do_attention, "a", do_queries, "b"]
            + ["a", "kv", "b", "a", "kv", "b", "kv", do_tail]
        )
        sums = run_turns(sets, turns, at)
    else:
        for work in (do_gate, do_up, do_attention, do_queries, do_out, do_tail):
            at.update(work({}, lambda value: value))
        sums = {}
        for name in ("down", "gate", "up", "out", "query", "tail"):
            for index, pair in enumerate(at[name]):
                sums[name + str(index)] = sum_plain(*pair)
    input_grad = at["input_grad"]
    sum_down = join_halves(*sums["down0"])
    sum_gate = join_halves(*sums["gate0"])
    sum_up = join_halves(*sums["up0"])
    sum_out = join_halves(*sums["out0"])
    sum_query = join_halves(*sums["query0"])
    sum_key, sum_value, *gain_parts = finish_tail(sz, *sums["tail0"])
    gain_sums = {name: part[0] for name, part in zip(gain_names, gain_parts)}
    shape = (micro_count, seq_local, tokens, model_width)
    members = (
        sum_query,
        sum_key,
        sum_value,
        sum_out,
        sum_gate,
        sum_up,
        sum_down,
        gain_sums["input"],
        gain_sums["query"],
        gain_sums["key"],
        gain_sums["attn"],
        gain_sums["pre"],
        gain_sums["post"],
    )
    return (result.reshape(shape)[None], input_grad.reshape(shape)[None]) + tuple(
        member[None] for member in members
    )


def solution(mesh):
    weight = P("section", "fsdp", None)
    gain = P("section", "fsdp")
    in_specs = (P(None, "fsdp", "ctx", None),) * 2 + (P(),) + (weight,) * 7 + (gain,) * 6
    out_specs = (
        (P("section", None, "fsdp", "ctx", None),) * 2 + (weight,) * 7 + (gain,) * 6
    )
    return jax.shard_map(
        on_device, mesh=mesh, in_specs=in_specs, out_specs=out_specs, check_vma=False
    )
```

```python
import functools

import jax
import jax.numpy as jnp
from jax import lax
from jax.experimental import pallas as pl
from jax.experimental.pallas import tpu as pltpu
from jax.sharding import PartitionSpec as P

epsilon = 1e-06
rope_base = 1000000.0
masked = -1e30
score_scale = 0.0625
gelu_slope = 0.7978845608028654
gelu_cubic = 0.044715
f32 = jnp.float32
bf16 = jnp.bfloat16
vmem_bytes = 56 * 1024 * 1024


def dot_nn(left, right):
    return jnp.dot(left, right, preferred_element_type=f32)


def dot_nt(left, right):
    return lax.dot_general(left, right, (((1,), (1,)), ((), ())), preferred_element_type=f32)


def dot_tn(left, right):
    return lax.dot_general(left, right, (((0,), (0,)), ((), ())), preferred_element_type=f32)


def norm_factor(values_in):
    return lax.rsqrt(jnp.mean(values_in * values_in, axis=-1, keepdims=True) + epsilon)


def norm_apply(values_in, gain_vec):
    return values_in * norm_factor(values_in) * gain_vec


def norm_back(values_in, gain_vec, grad_out):
    factor = norm_factor(values_in)
    scaled = grad_out * gain_vec
    grad_in = factor * (
        scaled - values_in * factor * factor * jnp.mean(scaled * values_in, axis=-1, keepdims=True)
    )
    grad_gain = jnp.sum(grad_out * values_in * factor, axis=0, keepdims=True)
    return (grad_in, grad_gain)


def rotate(values_in, cos_table, sin_table):
    half_width = values_in.shape[-1] // 2
    former = values_in[..., :half_width]
    latter = values_in[..., half_width:]
    return jnp.concatenate(
        [former * cos_table - latter * sin_table, latter * cos_table + former * sin_table], axis=-1
    )


def rotation_tables(positions, half_width):
    frequency = rope_base ** (-jnp.arange(half_width, dtype=f32) / half_width)
    angles = positions.astype(f32)[:, None] * frequency[None, :]
    return (jnp.cos(angles), jnp.sin(angles))


def call_kernel(body, out_shapes, inputs, far_inputs, scratch, mega_macs=0):
    moved = 0
    for array in [*inputs, *far_inputs, *out_shapes]:
        moved += array.size * jnp.dtype(array.dtype).itemsize
    whole = pl.BlockSpec(memory_space=pltpu.VMEM)
    far = pl.BlockSpec(memory_space=pl.ANY)
    return pl.pallas_call(
        body,
        out_shape=out_shapes,
        in_specs=[whole] * len(inputs) + [far] * len(far_inputs),
        out_specs=jax.tree.map(lambda _: whole, out_shapes),
        scratch_shapes=scratch,
        compiler_params=pltpu.CompilerParams(vmem_limit_bytes=vmem_bytes),
        cost_estimate=pl.CostEstimate(
            flops=2 * mega_macs * 10**6, bytes_accessed=moved * 3, transcendentals=0
        ),
    )(*inputs, *far_inputs)


def struct(shape, dtype):
    return jax.ShapeDtypeStruct(shape, dtype)


def start_halves(own, other, target, sems, first_sem):
    half = own.shape[0]
    fsdp_index = lax.axis_index("fsdp")
    copies = [
        pltpu.make_async_copy(
            own, target.at[pl.ds(fsdp_index * half, half)], sems.at[first_sem]
        ),
        pltpu.make_async_copy(
            other, target.at[pl.ds((1 - fsdp_index) * half, half)], sems.at[first_sem + 1]
        ),
    ]
    for copy in copies:
        copy.start()
    return copies


def wait_all(copies):
    for copy in copies:
        copy.wait()


def whole_gain(own_ref, other_ref, start, width):
    own = own_ref[:, start : start + width].astype(f32)
    other = other_ref[:, start : start + width].astype(f32)
    is_first = lax.axis_index("fsdp") == 0
    return jnp.concatenate(
        [jnp.where(is_first, own, other), jnp.where(is_first, other, own)], axis=1
    )


class Sizes:
    def __init__(self, groups, tokens, model, heads, head_dim, ff, blocks):
        self.groups, self.tokens, self.model = groups, tokens, model
        self.heads, self.head_dim, self.ff, self.blocks = heads, head_dim, ff, blocks
        self.rows = groups * tokens
        self.query_cols = heads * head_dim
        self.head_rows = heads * tokens
        self.keys = blocks * tokens
        self.span = tokens * min(8, blocks)
        self.chunk = min(256, self.head_rows)
        half = model // 2
        self.gain_at = {
            "input": (0, half),
            "attn": (half, half),
            "pre": (2 * half, half),
            "post": (3 * half, half),
            "query": (4 * half, head_dim // 2),
            "key": (4 * half + head_dim // 2, head_dim // 2),
        }


def kv_kernel(
    sz, hidden, gain_own, gain_other, cos_ref, sin_ref, k_own, k_other, v_own, v_other,
    normed, key_lin, kv_low, wk, wv, sems,
):
    k_copies = start_halves(k_own, k_other, wk, sems, 0)
    v_copies = start_halves(v_own, v_other, wv, sems, 2)
    gain_input = whole_gain(gain_own, gain_other, *sz.gain_at["input"])
    gain_key = whole_gain(gain_own, gain_other, *sz.gain_at["key"])
    low = norm_apply(hidden[...].astype(f32), gain_input).astype(bf16)
    normed[...] = low
    wait_all(k_copies)
    lin = dot_nn(low, wk[...])
    key_lin[...] = lin
    cos = jnp.concatenate([cos_ref[...]] * sz.groups, axis=0)
    sin = jnp.concatenate([sin_ref[...]] * sz.groups, axis=0)
    kv_low[:, : sz.head_dim] = rotate(norm_apply(lin, gain_key), cos, sin).astype(bf16)
    wait_all(v_copies)
    kv_low[:, sz.head_dim :] = dot_nn(low, wv[...]).astype(bf16)


def project_kv(sz, hidden, gains, tables, w_key, w_value):
    half = (sz.model, sz.head_dim)
    return call_kernel(
        functools.partial(kv_kernel, sz),
        [
            struct((sz.rows, sz.model), bf16),
            struct((sz.rows, sz.head_dim), f32),
            struct((sz.rows, 2 * sz.head_dim), bf16),
        ],
        [hidden, *gains, *tables],
        [*w_key, *w_value],
        [pltpu.VMEM(half, bf16), pltpu.VMEM(half, bf16), pltpu.SemaphoreType.DMA((4,))],
    )


def query_kernel(
    sz, normed, gain_own, gain_other, cos_ref, sin_ref, q_own, q_other,
    query_lin, query_low, wq, sems,
):
    copies = start_halves(q_own, q_other, wq, sems, 0)
    gain_query = whole_gain(gain_own, gain_other, *sz.gain_at["query"])
    cos = jnp.concatenate([cos_ref[...]] * sz.groups, axis=0)
    sin = jnp.concatenate([sin_ref[...]] * sz.groups, axis=0)
    low = normed[...]
    wait_all(copies)
    for head in range(sz.heads):
        cols = slice(head * sz.head_dim, (head + 1) * sz.head_dim)
        lin = dot_nn(low, wq[:, cols])
        query_lin[:, cols] = lin
        turned = rotate(norm_apply(lin, gain_query), cos, sin)
        turned = (turned.astype(bf16).astype(f32) * score_scale).astype(bf16)
        for group in range(sz.groups):
            query_low[group, head * sz.tokens : (head + 1) * sz.tokens, :] = turned[
                group * sz.tokens : (group + 1) * sz.tokens
            ]


def project_query(sz, normed, gains, tables, w_query):
    return call_kernel(
        functools.partial(query_kernel, sz),
        [
            struct((sz.rows, sz.query_cols), f32),
            struct((sz.groups, sz.head_rows, sz.head_dim), bf16),
        ],
        [normed, *gains, *tables],
        [*w_query],
        [pltpu.VMEM((sz.model, sz.query_cols), bf16), pltpu.SemaphoreType.DMA((2,))],
    )


def start_blocks(sz, blocks, target, sems, first_sem):
    copies = []
    for index, block in enumerate(blocks):
        copies.append(
            pltpu.make_async_copy(
                block,
                target.at[:, pl.ds(index * sz.tokens, sz.tokens)],
                sems.at[first_sem + index],
            )
        )
    for copy in copies:
        copy.start()
    return copies


def load_group(sz, stacked, group, target, sems, first_sem):
    def one(index):
        return pltpu.make_async_copy(
            stacked.at[index, group],
            target.at[0, pl.ds(index * sz.tokens, sz.tokens)],
            sems.at[first_sem + index],
        )

    def start(index, carry):
        one(index).start()
        return carry

    def wait(index, carry):
        one(index).wait()
        return carry

    lax.fori_loop(0, sz.blocks, start, 0)
    lax.fori_loop(0, sz.blocks, wait, 0)


def forward_kernel(sz, block_count, save, *refs):
    query_low, hidden, gain_own, gain_other, key_row, query_col = refs[:6]
    refs = refs[6:]
    blocks, refs = refs[:block_count], refs[block_count:]
    out_pair, gate_pair, up_pair, down_pair = (refs[2 * i : 2 * i + 2] for i in range(4))
    refs = refs[8:]
    result, refs = refs[0], refs[1:]
    if save:
        log_total, attn_low, branch_ref, middle_ref, pre_ref, gate_ref, up_ref, act_ref, down_ref = (
            refs[:9]
        )
        refs = refs[9:]
    else:
        attn_low, act_ref = refs[:2]
        refs = refs[2:]
    kv, w_out, w_gate, w_up, w_down, sems = refs
    if block_count > 1:
        kv_copies = start_blocks(sz, blocks, kv, sems, 8)
    out_copies = start_halves(*out_pair, w_out, sems, 0)
    gate_copies = start_halves(*gate_pair, w_gate, sems, 2)
    up_copies = start_halves(*up_pair, w_up, sems, 4)
    down_copies = start_halves(*down_pair, w_down, sems, 6)
    gain_attn = whole_gain(gain_own, gain_other, *sz.gain_at["attn"])
    gain_pre = whole_gain(gain_own, gain_other, *sz.gain_at["pre"])
    gain_post = whole_gain(gain_own, gain_other, *sz.gain_at["post"])
    if block_count > 1:
        wait_all(kv_copies)
    spans = sz.keys // sz.span
    for group in range(sz.groups):
        slot = group if block_count > 1 else 0
        if block_count == 1:
            load_group(sz, blocks[0], group, kv, sems, 8)
        for first in range(0, sz.head_rows, sz.chunk):
            query = query_low[group, first : first + sz.chunk, :]
            query_pos = query_col[first : first + sz.chunk, :]

            def one_span(index, state):
                row_max, row_total, row_sum = state
                at = pl.ds(index * sz.span, sz.span)
                scores = dot_nt(query, kv[slot, at, : sz.head_dim])
                scores = jnp.where(key_row[:, at] <= query_pos, scores, masked)
                new_max = jnp.maximum(row_max, jnp.max(scores, axis=1, keepdims=True))
                probs = jnp.exp(scores - new_max)
                part = dot_nn(probs.astype(bf16), kv[slot, at, sz.head_dim :])
                shrink = jnp.exp(row_max - new_max)
                return (
                    new_max,
                    row_total * shrink + jnp.sum(probs, axis=1, keepdims=True),
                    row_sum * shrink + part,
                )

            state = (
                jnp.full((sz.chunk, 1), masked, f32),
                jnp.zeros((sz.chunk, 1), f32),
                jnp.zeros((sz.chunk, sz.head_dim), f32),
            )
            if spans == 1:
                state = one_span(0, state)
            else:
                state = lax.fori_loop(0, spans, one_span, state)
            row_max, row_total, row_sum = state
            attended = (row_sum / row_total).astype(bf16)
            if save:
                log_total[group, first : first + sz.chunk, :] = row_max + jnp.log(row_total)
            for part in range(sz.chunk // sz.tokens):
                head = first // sz.tokens + part
                attn_low[
                    group * sz.tokens : (group + 1) * sz.tokens,
                    head * sz.head_dim : (head + 1) * sz.head_dim,
                ] = attended[part * sz.tokens : (part + 1) * sz.tokens]
    wait_all(out_copies)
    branch = dot_nn(attn_low[...], w_out[...])
    middle = hidden[...].astype(f32) + norm_apply(branch, gain_attn)
    pre_ffw = norm_apply(middle, gain_pre).astype(bf16)
    if save:
        branch_ref[...] = branch
        middle_ref[...] = middle
        pre_ref[...] = pre_ffw
    wait_all(gate_copies)
    wait_all(up_copies)
    step = min(512, sz.ff)
    for first in range(0, sz.ff, step):
        cols = slice(first, first + step)
        gate = dot_nn(pre_ffw, w_gate[:, cols])
        up = dot_nn(pre_ffw, w_up[:, cols])
        if save:
            gate_ref[:, cols] = gate
            up_ref[:, cols] = up
        bend = jnp.tanh(gelu_slope * (gate + gelu_cubic * gate * gate * gate))
        act_ref[:, cols] = (0.5 * gate * (1.0 + bend) * up).astype(bf16)
    wait_all(down_copies)
    down_out = dot_nn(act_ref[...], w_down[...])
    if save:
        down_ref[...] = down_out
    result[...] = (middle + norm_apply(down_out, gain_post)).astype(bf16)


def forward_layer(sz, query_low, hidden, gains, places, blocks, weights, save):
    rows, model = sz.rows, sz.model
    outs = [struct((rows, model), bf16)]
    attn = (rows, sz.query_cols)
    act = (rows, sz.ff)
    scratch = []
    if save:
        outs += [
            struct((sz.groups, sz.head_rows, 1), f32),
            struct(attn, bf16),
            struct((rows, model), f32),
            struct((rows, model), f32),
            struct((rows, model), bf16),
            struct(act, f32),
            struct(act, f32),
            struct(act, bf16),
            struct((rows, model), f32),
        ]
    else:
        scratch += [pltpu.VMEM(attn, bf16), pltpu.VMEM(act, bf16)]
    scratch += [
        pltpu.VMEM((sz.groups if len(blocks) > 1 else 1, sz.keys, 2 * sz.head_dim), bf16),
        pltpu.VMEM((sz.query_cols, model), bf16),
        pltpu.VMEM((model, sz.ff), bf16),
        pltpu.VMEM((model, sz.ff), bf16),
        pltpu.VMEM((sz.ff, model), bf16),
        pltpu.SemaphoreType.DMA((8 + sz.blocks,)),
    ]
    far = [*blocks, *weights["out"], *weights["gate"], *weights["up"], *weights["down"]]
    return call_kernel(
        functools.partial(forward_kernel, sz, len(blocks), save),
        outs,
        [query_low, hidden, *gains, places["key_row"], places["query_col"]],
        far,
        scratch,
    )


def ffw_back_kernel(sz, *refs):
    grad_ref, gain_own, gain_other, down_out, gate_ref, up_ref, middle, branch = refs[:8]
    refs = refs[8:]
    out_pair, gate_pair, up_pair, down_pair = (refs[2 * i : 2 * i + 2] for i in range(4))
    refs = refs[8:]
    (
        middle_grad, down_grad, gate_grad, up_grad, branch_grad, gain_post_grad, gain_pre_grad,
        gain_attn_grad, attn_grad,
    ) = refs[:9]
    w_out, w_gate, w_up, w_down, sems = refs[9:]
    down_copies = start_halves(*down_pair, w_down, sems, 0)
    gate_copies = start_halves(*gate_pair, w_gate, sems, 2)
    up_copies = start_halves(*up_pair, w_up, sems, 4)
    out_copies = start_halves(*out_pair, w_out, sems, 6)
    gain_attn = whole_gain(gain_own, gain_other, *sz.gain_at["attn"])
    gain_pre = whole_gain(gain_own, gain_other, *sz.gain_at["pre"])
    gain_post = whole_gain(gain_own, gain_other, *sz.gain_at["post"])
    grad = grad_ref[...].astype(f32)
    down_part, gain_post_grad[...] = norm_back(down_out[...], gain_post, grad)
    down_low = down_part.astype(bf16)
    down_grad[...] = down_low
    wait_all(down_copies)
    wait_all(gate_copies)
    wait_all(up_copies)
    step = min(512, sz.ff)
    pre_grad = jnp.zeros((sz.rows, sz.model), f32)
    for first in range(0, sz.ff, step):
        cols = slice(first, first + step)
        ffw_grad = dot_nt(down_low, w_down[cols, :])
        gate = gate_ref[:, cols]
        up = up_ref[:, cols]
        square = gate * gate
        bend = jnp.tanh(gelu_slope * (gate + gelu_cubic * square * gate))
        half_open = 0.5 * (1.0 + bend)
        slope = half_open + 0.5 * gate * (1.0 - bend * bend) * gelu_slope * (
            1.0 + 3.0 * gelu_cubic * square
        )
        gate_low = (ffw_grad * up * slope).astype(bf16)
        up_low = (ffw_grad * gate * half_open).astype(bf16)
        gate_grad[:, cols] = gate_low
        up_grad[:, cols] = up_low
        pre_grad = pre_grad + dot_nt(gate_low, w_gate[:, cols]) + dot_nt(up_low, w_up[:, cols])
    middle_part, gain_pre_grad[...] = norm_back(middle[...], gain_pre, pre_grad)
    total = grad + middle_part
    middle_grad[...] = total
    branch_part, gain_attn_grad[...] = norm_back(branch[...], gain_attn, total)
    branch_low = branch_part.astype(bf16)
    branch_grad[...] = branch_low
    wait_all(out_copies)
    attn_grad[...] = dot_nt(branch_low, w_out[...]).astype(bf16)


def attn_back_kernel(sz, block_count, paired, *refs):
    attn_grad, query_low, log_row, key_col, query_row = refs[:5]
    refs = refs[5:]
    blocks, refs = refs[:block_count], refs[block_count:]
    query_grad, parts, refs = refs[0], refs[1:-4], refs[-4:]
    kv, key_sum, value_sum, sems = refs
    if block_count > 1:
        wait_all(start_blocks(sz, blocks, kv, sems, 0))
    spans = sz.keys // sz.span
    heads_in = sz.chunk // sz.tokens
    chunks = range(0, sz.head_rows, sz.chunk)

    def probs_of(slot, group, first, at):
        query = query_low[group, first : first + sz.chunk, :]
        query_pos = query_row[:, first : first + sz.chunk]
        log_here = log_row[group, :, first : first + sz.chunk]
        scores = dot_nt(kv[slot, at, : sz.head_dim], query)
        probs = jnp.exp(jnp.where(key_col[at, :] <= query_pos, scores - log_here, masked))
        grad_rows = jnp.concatenate(
            [
                attn_grad[
                    group * sz.tokens : (group + 1) * sz.tokens,
                    (first // sz.tokens + part) * sz.head_dim : (first // sz.tokens + part + 1)
                    * sz.head_dim,
                ]
                for part in range(heads_in)
            ],
            axis=0,
        )
        return probs, dot_nt(kv[slot, at, sz.head_dim :], grad_rows), query, grad_rows

    def finish(slot, first, at, got, delta):
        probs, prob_grad, query, grad_rows = got
        score_grad = (probs * (prob_grad - delta)).astype(bf16)
        key_part = dot_nn(score_grad, query)
        value_part = dot_nn(probs.astype(bf16), grad_rows)
        if first == 0:
            key_sum[...] = key_part
            value_sum[...] = value_part
        else:
            key_sum[...] += key_part
            value_sum[...] += value_part
        return dot_tn(score_grad, kv[slot, at, : sz.head_dim])

    for group in range(sz.groups):
        if block_count > 1:
            for first in chunks:
                at = slice(0, sz.span)
                got = probs_of(group, group, first, at)
                delta = jnp.sum(got[0] * got[1], axis=0, keepdims=True)
                query_grad[group, first : first + sz.chunk, :] = finish(
                    group, first, at, got, delta
                )
            for index in range(block_count):
                at = slice(index * sz.tokens, (index + 1) * sz.tokens)
                if paired:
                    target = parts[index // 2].at[index % 2, group]
                else:
                    target = parts[index].at[group]
                target[:, : sz.head_dim] = key_sum[at, :].astype(bf16)
                target[:, sz.head_dim :] = value_sum[at, :].astype(bf16)
            continue
        load_group(sz, blocks[0], group, kv, sems, 0)
        deltas = []
        for first in chunks:

            def add_delta(index, delta, first=first):
                got = probs_of(0, group, first, pl.ds(index * sz.span, sz.span))
                return delta + jnp.sum(got[0] * got[1], axis=0, keepdims=True)

            deltas.append(lax.fori_loop(0, spans, add_delta, jnp.zeros((1, sz.chunk), f32)))
            query_grad[group, first : first + sz.chunk, :] = jnp.zeros(
                (sz.chunk, sz.head_dim), f32
            )

        def add_span(index, carry):
            at = pl.ds(index * sz.span, sz.span)
            for first, delta in zip(chunks, deltas):
                query_grad[group, first : first + sz.chunk, :] += finish(
                    0, first, at, probs_of(0, group, first, at), delta
                )
            per_span = sz.span // sz.tokens
            for step in range(per_span):
                rows = slice(step * sz.tokens, (step + 1) * sz.tokens)
                target = parts[0].at[index * per_span + step, group]
                target[:, : sz.head_dim] = key_sum[rows, :].astype(bf16)
                target[:, sz.head_dim :] = value_sum[rows, :].astype(bf16)
            return carry

        lax.fori_loop(0, spans, add_span, 0)


def ffw_back(sz, grad, gains, saved, weights):
    rows, model = sz.rows, sz.model
    gain = struct((1, model), f32)
    outs = [
        struct((rows, model), f32),
        struct((rows, model), bf16),
        struct((rows, sz.ff), bf16),
        struct((rows, sz.ff), bf16),
        struct((rows, model), bf16),
        gain,
        gain,
        gain,
        struct((rows, sz.query_cols), bf16),
    ]
    scratch = [
        pltpu.VMEM((sz.query_cols, model), bf16),
        pltpu.VMEM((model, sz.ff), bf16),
        pltpu.VMEM((model, sz.ff), bf16),
        pltpu.VMEM((sz.ff, model), bf16),
        pltpu.SemaphoreType.DMA((8,)),
    ]
    inputs = [
        grad, *gains, saved["down_out"], saved["gate"], saved["up"], saved["middle"],
        saved["branch"],
    ]
    far = [*weights["out"], *weights["gate"], *weights["up"], *weights["down"]]
    return call_kernel(functools.partial(ffw_back_kernel, sz), outs, inputs, far, scratch)


def attn_back(sz, attn_grad, saved, places, paired):
    blocks = saved["blocks"]
    outs = [struct((sz.groups, sz.head_rows, sz.head_dim), f32)]
    if paired and len(blocks) > 1:
        outs += [struct((2,) + block.shape, bf16) for block in blocks[::2]]
    else:
        outs += [struct(block.shape, bf16) for block in blocks]
    scratch = [
        pltpu.VMEM((sz.groups if len(blocks) > 1 else 1, sz.keys, 2 * sz.head_dim), bf16),
        pltpu.VMEM((sz.span, sz.head_dim), f32),
        pltpu.VMEM((sz.span, sz.head_dim), f32),
        pltpu.SemaphoreType.DMA((sz.blocks,)),
    ]
    inputs = [
        attn_grad, saved["query_low"], saved["log_row"], places["key_col"], places["query_row"]
    ]
    got = call_kernel(
        functools.partial(attn_back_kernel, sz, len(blocks), paired), outs, inputs, blocks, scratch
    )
    return got[0], got[1:]


gain_names = ("input", "attn", "pre", "post", "query", "key")
gain_pad = 16


def weight_kernel(sz, cuts, gain_count, left, right, *refs):
    gains, refs = refs[:gain_count], refs[gain_count:]
    outs, turned = refs[:-1], refs[-1]
    turned[...] = left[...].T
    half = left.shape[1] // 2
    fsdp_index = lax.axis_index("fsdp")
    y_index = lax.axis_index("ctx") & 1
    for side, owner in ((0, 1 - fsdp_index), (1, fsdp_index)):
        for part, y_half in ((0, y_index), (1, 1 - y_index)):
            base = owner * half + y_half * (half // 2)
            for index, (first_row, count, first_col, cols) in enumerate(cuts):
                out = outs[2 * index + side]
                rows = turned[pl.ds(pl.multiple_of(base + first_row, 16), count), :]
                first_out = part * (out.shape[0] // 2)
                out[first_out : first_out + count, :] = dot_nn(
                    rows, right[:, first_col : first_col + cols]
                ).astype(bf16)
                if gain_count:
                    out[first_out + count : first_out + count + gain_pad, :] = gain_rows(
                        sz, gains, owner, y_half, cols
                    )


def gain_rows(sz, gains, owner, y_half, cols):
    halves = []
    for gain in gains:
        half = gain.shape[1] // 2
        halves.append(jnp.where(owner == 0, gain[:, :half], gain[:, half:]))
    flat = jnp.where(y_half == 0, jnp.concatenate(halves, axis=1), 0.0)
    rows = [flat[:, first : first + cols] for first in range(0, flat.shape[1], cols)]
    rows.append(jnp.zeros((gain_pad - len(rows), cols), f32))
    return jnp.concatenate(rows, axis=0).astype(bf16)


def tail_kernel(sz, count, mine, other, key, value, *gains):
    y_index = lax.axis_index("ctx") & 1
    for source, y_half in ((mine, y_index), (other, 1 - y_index)):
        rows = pl.ds(pl.multiple_of(y_half * count, 16), count)
        key[rows, :] = source[:count, : sz.head_dim].astype(f32)
        value[rows, :] = source[:count, sz.head_dim :].astype(f32)
    row_count = sum(gain.shape[1] for gain in gains) // mine.shape[1]
    here = mine[count : count + gain_pad, :].astype(f32)
    there = other[count : count + gain_pad, :].astype(f32)
    lower = jnp.where(y_index == 0, here, there)
    flat = jnp.concatenate([lower[row : row + 1, :] for row in range(row_count)], axis=1)
    start = 0
    for gain in gains:
        gain[...] = flat[:, start : start + gain.shape[1]]
        start += gain.shape[1]


def finish_tail(sz, mine, other):
    half = sz.model // 2
    outs = [struct((half, sz.head_dim), f32)] * 2
    outs += [struct((1, sz.gain_at[name][1]), f32) for name in gain_names]
    return call_kernel(
        functools.partial(tail_kernel, sz, half // 2), outs, [mine, other], [], []
    )


def weight_terms(sz, left, right, cuts, gains=()):
    outs = []
    for _, count, _, cols in cuts:
        outs += [struct((2 * (count + (gain_pad if gains else 0)), cols), bf16)] * 2
    got = call_kernel(
        functools.partial(weight_kernel, sz, cuts, len(gains)),
        outs,
        [left, right, *gains],
        [],
        [pltpu.VMEM((left.shape[1], left.shape[0]), bf16)],
    )
    return [(got[2 * index], got[2 * index + 1]) for index in range(len(cuts))]


def query_back_kernel(
    sz, query_grad, query_lin, gain_own, gain_other, cos_ref, sin_ref, q_own, q_other,
    lin_grad, normed_grad, gain_grad, wq, sems,
):
    copies = start_halves(q_own, q_other, wq, sems, 0)
    gain_query = whole_gain(gain_own, gain_other, *sz.gain_at["query"])
    cos = jnp.concatenate([cos_ref[...]] * sz.groups, axis=0)
    sin = jnp.concatenate([sin_ref[...]] * sz.groups, axis=0)
    gain_sum = jnp.zeros((1, sz.head_dim), f32)
    for head in range(sz.heads):
        cols = slice(head * sz.head_dim, (head + 1) * sz.head_dim)
        rows = slice(head * sz.tokens, (head + 1) * sz.tokens)
        grad = jnp.concatenate([query_grad[g, rows, :] for g in range(sz.groups)], axis=0)
        turned = rotate(grad * score_scale, cos, -sin)
        part, gain_part = norm_back(query_lin[:, cols], gain_query, turned)
        lin_grad[:, cols] = part.astype(bf16)
        gain_sum = gain_sum + gain_part
    gain_grad[...] = gain_sum
    wait_all(copies)
    normed_grad[...] = dot_nt(lin_grad[...], wq[...])


def query_back(sz, query_grad, query_lin, gains, tables, w_query):
    return call_kernel(
        functools.partial(query_back_kernel, sz),
        [
            struct((sz.rows, sz.query_cols), bf16),
            struct((sz.rows, sz.model), f32),
            struct((1, sz.head_dim), f32),
        ],
        [query_grad, query_lin, *gains, *tables],
        [*w_query],
        [pltpu.VMEM((sz.model, sz.query_cols), bf16), pltpu.SemaphoreType.DMA((2,))],
    )


def input_back_kernel(sz, term_count, *refs):
    terms, refs = refs[:term_count], refs[term_count:]
    (
        key_lin, hidden, query_part, middle_grad, gain_own, gain_other, cos_ref, sin_ref,
        k_own, k_other, v_own, v_other, input_grad, kv_grad, gain_input_grad, gain_key_grad,
        wk, wv, sems,
    ) = refs
    k_copies = start_halves(k_own, k_other, wk, sems, 0)
    v_copies = start_halves(v_own, v_other, wv, sems, 2)
    gain_input = whole_gain(gain_own, gain_other, *sz.gain_at["input"])
    gain_key = whole_gain(gain_own, gain_other, *sz.gain_at["key"])
    cos = jnp.concatenate([cos_ref[...]] * sz.groups, axis=0)
    sin = jnp.concatenate([sin_ref[...]] * sz.groups, axis=0)
    total = terms[0][...].astype(f32)
    for term in terms[1:]:
        total = total + term[...].astype(f32)
    turned = rotate(total[:, : sz.head_dim], cos, -sin)
    key_part, gain_key_grad[...] = norm_back(key_lin[...], gain_key, turned)
    key_low = key_part.astype(bf16)
    value_low = total[:, sz.head_dim :].astype(bf16)
    kv_grad[:, : sz.head_dim] = key_low
    kv_grad[:, sz.head_dim :] = value_low
    wait_all(k_copies)
    wait_all(v_copies)
    normed_grad = query_part[...] + dot_nt(key_low, wk[...]) + dot_nt(value_low, wv[...])
    part, gain_input_grad[...] = norm_back(hidden[...].astype(f32), gain_input, normed_grad)
    input_grad[...] = (middle_grad[...] + part).astype(bf16)


def input_back(sz, terms, key_lin, hidden, query_part, middle_grad, gains, tables, w_key, w_value):
    half = (sz.model, sz.head_dim)
    flat = [term.reshape(sz.rows, 2 * sz.head_dim) for term in terms]
    return call_kernel(
        functools.partial(input_back_kernel, sz, len(flat)),
        [
            struct((sz.rows, sz.model), bf16),
            struct((sz.rows, 2 * sz.head_dim), bf16),
            struct((1, sz.model), f32),
            struct((1, sz.head_dim), f32),
        ],
        [*flat, key_lin, hidden, query_part, middle_grad, *gains, *tables],
        [*w_key, *w_value],
        [pltpu.VMEM(half, bf16), pltpu.VMEM(half, bf16), pltpu.SemaphoreType.DMA((4,))],
    )


def xor_permute(shard, axis, mask):
    count = lax.axis_size(axis)
    return lax.ppermute(shard, axis, [(i, i ^ mask) for i in range(count)])


def small_ctx():
    return lax.axis_size("ctx") == 8


def ctx_order():
    count = lax.axis_size("ctx")
    slots = jnp.arange(count, dtype=jnp.int32)
    if small_ctx():
        return lax.axis_index("ctx") ^ slots
    return slots


def after(value, *earlier):
    return lax.optimization_barrier((value, earlier))[0]


def gather_ctx(shard, meanwhile):
    if not small_ctx():
        return [lax.all_gather(shard, "ctx", axis=0)]
    blocks = [None] * 8
    blocks[0] = shard
    for mask in (6, 4, 2):
        blocks[mask] = xor_permute(shard, "ctx", mask)
    blocks[1] = xor_permute(shard, "ctx", 1)
    for mask in (2, 4, 6):
        blocks[mask] = after(blocks[mask], meanwhile)
        blocks[mask + 1] = xor_permute(blocks[mask], "ctx", 1)
    return blocks


def add_low(*terms):
    total = terms[0].astype(f32)
    for term in terms[1:]:
        total = total + term.astype(f32)
    return lax.optimization_barrier(total.astype(bf16))


def xor_pairs(count, mask):
    return [(i, i ^ mask) for i in range(count)]


def scatter_stages(parts):
    y_swap = xor_pairs(8, 1)
    came = yield [(parts[mask + 1], "ctx", y_swap) for mask in (6, 4, 2, 0)]
    sums = [add_low(parts[mask], got) for mask, got in zip((6, 4, 2), came)]
    got = yield [(low, "ctx", xor_pairs(8, mask)) for low, mask in zip(sums, (6, 4, 2))]
    return list(got) + [parts[0], came[3]]


def scatter_pairs(pairs):
    came = yield [(pairs[mask // 2], "ctx", xor_pairs(8, mask)) for mask in (6, 4, 2)]
    total = pairs[0].astype(f32)
    for term in came:
        total = total + term.astype(f32)
    other = lax.optimization_barrier(total[1].astype(bf16))
    own = lax.optimization_barrier(total[0])
    (got,) = yield [(other, "ctx", xor_pairs(8, 1))]
    return [own, got]


def sum_stages(make):
    send, keep = make()
    ctx_index = lax.axis_index("ctx")
    y_index = ctx_index & 1
    z_index = ctx_index >> 1
    half = send.shape[0] // 2
    y_swap = xor_pairs(8, 1)
    inward = [(z * 2 + y, t * 2 + y) for z, t in ((0, 1), (3, 2)) for y in (0, 1)]
    middle = [(z * 2 + y, t * 2 + y) for z, t in ((1, 2), (2, 1)) for y in (0, 1)]
    outward = [(z * 2 + y, t * 2 + y) for z, t in ((1, 0), (2, 3)) for y in (0, 1)]
    (core,) = yield [(send, "fsdp", [(0, 1), (1, 0)])]
    (came,) = yield [(add_low(keep[half:], core[half:]), "ctx", y_swap)]
    part = add_low(keep[:half], core[:half], came)
    (came,) = yield [(part, "ctx", inward)]
    part = add_low(part, came)
    (came,) = yield [(part, "ctx", middle)]
    part = add_low(part, came)
    (came,) = yield [(part, "ctx", outward)]
    total = jnp.where((z_index == 1) | (z_index == 2), part, came)
    (other,) = yield [(total, "ctx", y_swap)]
    return (total, other)


def join_halves(mine, other):
    y_index = lax.axis_index("ctx") & 1
    first = jnp.where(y_index == 0, mine, other)
    second = jnp.where(y_index == 0, other, mine)
    return jnp.concatenate([first, second], axis=0).astype(f32)


def sum_plain(send, keep):
    half = send.shape[0] // 2
    y_index = lax.axis_index("ctx") & 1
    came = xor_permute(send, "fsdp", 1)
    both = add_low(keep, came)
    first = jnp.where(y_index == 0, both[:half], both[half:])
    second = jnp.where(y_index == 0, both[half:], both[:half])
    whole = lax.psum(jnp.concatenate([first, second], axis=0).astype(f32), "ctx")
    first, second = whole[:half], whole[half:]
    return (jnp.where(y_index == 0, first, second), jnp.where(y_index == 0, second, first))


def run_turns(sets, turns, beside, held):
    results = {}
    states = {
        name: dict(entries=list(one), active=[], turn=0, landed=None)
        for name, one in sets.items()
    }
    latest = [None, ()]

    def alive(state):
        return state["active"] or state["turn"] < len(state["entries"])

    def step(state):
        going = []
        for (name, stage, _), landed in zip(state["active"], state["landed"] or []):
            try:
                going.append((name, stage, stage.send(landed)))
            except StopIteration as end:
                results[name] = end.value
        if state["turn"] < len(state["entries"]):
            for name, make_stage in state["entries"][state["turn"]]:
                stage = make_stage()
                going.append((name, stage, next(stage)))
        state["turn"] += 1
        state["active"] = going
        state["landed"] = None
        if not going:
            return
        operands = [[move[0] for move in moves] for _, _, moves in going]
        for other in states.values():
            if other is not state and other["landed"] is not None:
                other["landed"] = after(other["landed"], operands)
        state["landed"] = [
            [lax.ppermute(value, axis, pairs) for value, axis, pairs in moves]
            for _, _, moves in going
        ]
        latest[:] = [state, operands]

    for turn in turns:
        if callable(turn):
            state, operands = latest
            got = turn(results, lambda value: after(value, operands))
            if turn in beside:
                got, state["landed"] = lax.optimization_barrier((got, state["landed"]))
            held.update(got)
        else:
            step(states[turn])
    while any(alive(state) for state in states.values()):
        for state in states.values():
            if alive(state):
                step(state)
    return results


def run_alone(stage):
    moves = next(stage)
    while True:
        try:
            moves = stage.send([lax.ppermute(value, axis, pairs) for value, axis, pairs in moves])
        except StopIteration as end:
            return end.value


def on_device(
    inputs,
    out_cotangent,
    block_order,
    w_query,
    w_key,
    w_value,
    w_output,
    w_gate,
    w_up,
    w_down,
    g_input,
    g_query,
    g_key,
    g_post_attn,
    g_pre_ffw,
    g_post_ffw,
):
    section_index = lax.axis_index("section")
    fsdp_index = lax.axis_index("fsdp")
    ctx_index = lax.axis_index("ctx")
    ctx_size = lax.axis_size("ctx")
    micro_count, seq_local, tokens, model_width = inputs.shape
    head_dim = 2 * g_query.shape[1]
    sz = Sizes(
        micro_count * seq_local,
        tokens,
        model_width,
        w_query.shape[2] // head_dim,
        head_dim,
        w_gate.shape[2],
        ctx_size,
    )
    block_len = tokens // 2
    gains_own = jnp.concatenate([g_input, g_post_attn, g_pre_ffw, g_post_ffw, g_query, g_key], 1)
    gains = (gains_own, xor_permute(gains_own, "fsdp", 1))
    weights = {}
    for name, own in (
        ("key", w_key),
        ("value", w_value),
        ("query", w_query),
        ("out", w_output),
        ("gate", w_gate),
        ("up", w_up),
        ("down", w_down),
    ):
        weights[name] = (own[0], xor_permute(own[0], "fsdp", 1))
    slot_pairs = block_order.reshape(ctx_size, 2)
    offsets = jnp.arange(block_len, dtype=jnp.int32)

    def spread(slot_ids):
        return (slot_ids.reshape(-1)[:, None] * block_len + offsets[None, :]).reshape(-1)

    local_pos = spread(slot_pairs[ctx_index])
    key_pos = spread(slot_pairs[ctx_order()])
    tables = rotation_tables(local_pos, head_dim // 2)
    query_pos = jnp.tile(local_pos, sz.heads)
    places = {
        "key_row": key_pos.reshape(1, -1),
        "key_col": key_pos.reshape(-1, 1),
        "query_row": query_pos.reshape(1, -1),
        "query_col": query_pos.reshape(-1, 1),
    }
    block_shape = (sz.groups, tokens, 2 * head_dim)

    def forward(hidden, save):
        normed, key_lin, kv_low = project_kv(
            sz, hidden, gains, tables, weights["key"], weights["value"]
        )
        query_lin, query_low = project_query(sz, normed, gains, tables, weights["query"])
        if not save:
            kv_low = after(kv_low, weights)
        blocks = gather_ctx(kv_low.reshape(block_shape), query_low)
        got = forward_layer(sz, query_low, hidden, gains, places, blocks, weights, save)
        if not save:
            return got[0], None
        names = (
            "log_total", "attn_low", "branch", "middle", "pre_ffw", "gate", "up", "act", "down_out"
        )
        saved = dict(zip(names, got[1:]))
        saved["log_row"] = saved["log_total"].reshape(sz.groups, 1, sz.head_rows)
        saved.update(
            hidden=hidden, normed=normed, key_lin=key_lin, query_lin=query_lin,
            query_low=query_low, blocks=blocks,
        )
        return got[0], saved

    def input_part(terms, middle_grad, query_part, saved):
        return input_back(
            sz, terms, saved["key_lin"], saved["hidden"], query_part, middle_grad, gains, tables,
            weights["key"], weights["value"],
        )

    def queries_back(query_grad, saved):
        return query_back(
            sz, query_grad, saved["query_lin"], gains, tables, weights["query"]
        )

    def scatter_plain(parts):
        return [lax.psum_scatter(parts[0].astype(f32), "ctx", scatter_dimension=0, tiled=False)]

    own_input = inputs.reshape(sz.rows, model_width)
    first_result, _ = forward(own_input, False)
    received = lax.ppermute(first_result, "section", [(0, 1)])
    hidden = jnp.where(section_index == 0, own_input, received)
    result, saved = forward(hidden, True)

    own_grad = out_cotangent.reshape(sz.rows, model_width)
    got = ffw_back(sz, own_grad, gains, saved, weights)
    query_grad, parts = attn_back(sz, got[8], saved, places, False)
    _, query_part, _ = queries_back(query_grad, saved)
    terms = run_alone(scatter_stages(parts)) if small_ctx() else scatter_plain(parts)
    first_grad = input_part(terms, got[0], query_part, saved)[0]
    grad_received = lax.ppermute(first_grad, "section", [(1, 0)])
    grad_in = jnp.where(section_index == 1, own_grad, grad_received)

    got = ffw_back(sz, grad_in, gains, saved, weights)
    middle_grad, down_low, gate_low, up_low, branch_low, gain_post, gain_pre, gain_attn = got[:8]
    model_quarter = model_width // 4
    kv_width = 2 * head_dim
    down_cuts = [(0, sz.ff // 4, 0, model_width)]
    wide_cuts = [(0, model_quarter, 0, sz.ff)]
    out_cuts = [(0, sz.query_cols // 4, 0, model_width)]
    query_cuts = [(0, model_quarter, 0, sz.query_cols)]
    kv_cuts = [(0, model_quarter, 0, kv_width)]
    at = {"down": weight_terms(sz, saved["act"], down_low, down_cuts)}

    def do_gate(results, later):
        return {"gate": weight_terms(sz, saved["pre_ffw"], later(gate_low), wide_cuts)}

    def do_up(results, later):
        return {"up": weight_terms(sz, saved["pre_ffw"], later(up_low), wide_cuts)}

    def do_attention(results, later):
        query_grad, parts = attn_back(sz, later(got[8]), saved, places, True)
        return {"query_grad": query_grad, "parts": parts}

    def do_queries(results, later):
        low, query_part, gain_query = queries_back(later(at["query_grad"]), saved)
        terms = weight_terms(sz, saved["normed"], low, query_cuts)
        return {"query": terms, "query_part": query_part, "gain_query": gain_query}

    def do_out(results, later):
        return {"out": weight_terms(sz, saved["attn_low"], later(branch_low), out_cuts)}

    def do_tail(results, later):
        terms = results["kv"] if small_ctx() else scatter_plain(at["parts"])
        input_grad, kv_grad, gain_input, gain_key = input_part(
            later(terms), middle_grad, at["query_part"], saved
        )
        gain_grads = (gain_input, gain_attn, gain_pre, gain_post, at["gain_query"], gain_key)
        terms = weight_terms(sz, saved["normed"], kv_grad, kv_cuts, gain_grads)
        return {"tail": terms, "input_grad": input_grad}

    if small_ctx():

        def chunk(name, index):
            return (name + str(index), lambda: sum_stages(lambda: at[name][index]))

        sets = {
            "a": [[chunk("down", 0)], [], [chunk("up", 0)], [], [], [chunk("tail", 0)]],
            "b": [[chunk("gate", 0)], [chunk("out", 0)], [chunk("query", 0)]],
            "kv": [[("kv", lambda: scatter_pairs(at["parts"]))]],
        }
        beside = (do_attention, do_queries)
        turns = (
            ["a", "a", do_gate, "b", do_up, do_out, "b", do_attention, "a", do_queries, "b"]
            + ["a", "kv", "b", "a", "kv", "b", "kv", do_tail]
        )
        sums = run_turns(sets, turns, beside, at)
    else:
        for work in (do_gate, do_up, do_attention, do_queries, do_out, do_tail):
            at.update(work({}, lambda value: value))
        sums = {}
        for name in ("down", "gate", "up", "out", "query", "tail"):
            for index, pair in enumerate(at[name]):
                sums[name + str(index)] = sum_plain(*pair)
    input_grad = at["input_grad"]
    sum_down = join_halves(*sums["down0"])
    sum_gate = join_halves(*sums["gate0"])
    sum_up = join_halves(*sums["up0"])
    sum_out = join_halves(*sums["out0"])
    sum_query = join_halves(*sums["query0"])
    sum_key, sum_value, *gain_parts = finish_tail(sz, *sums["tail0"])
    gain_sums = {name: part[0] for name, part in zip(gain_names, gain_parts)}
    shape = (micro_count, seq_local, tokens, model_width)
    members = (
        sum_query,
        sum_key,
        sum_value,
        sum_out,
        sum_gate,
        sum_up,
        sum_down,
        gain_sums["input"],
        gain_sums["query"],
        gain_sums["key"],
        gain_sums["attn"],
        gain_sums["pre"],
        gain_sums["post"],
    )
    return (result.reshape(shape)[None], input_grad.reshape(shape)[None]) + tuple(
        member[None] for member in members
    )


def solution(mesh):
    weight = P("section", "fsdp", None)
    gain = P("section", "fsdp")
    in_specs = (P(None, "fsdp", "ctx", None),) * 2 + (P(),) + (weight,) * 7 + (gain,) * 6
    out_specs = (
        (P("section", None, "fsdp", "ctx", None),) * 2 + (weight,) * 7 + (gain,) * 6
    )
    return jax.shard_map(
        on_device, mesh=mesh, in_specs=in_specs, out_specs=out_specs, check_vma=False
    )
```
